32 devices in a mesh: dp: 2 (over x), seq: 4 (over y, core), heads: 4 (over z).
Axes of the slice: x: 2, y: 2, z: 4, core: 2. Of those that a mesh axis runs over, the one named last changes fastest.
Arguments:
- tokens: bfloat16 [8, 1024, 1024], P('dp', ('seq', 'heads')), may hold values from -6 to 6
- querymap: bfloat16 [1024, 1024], P(None, 'heads'), may hold values from -0.1875 to 0.1875
- querybias: bfloat16 [1024], P('heads'), may hold values from -2 to 2
- keymap: bfloat16 [1024, 1024], P(None, 'heads'), may hold values from -0.1875 to 0.1875
- valuemap: bfloat16 [1024, 1024], P(None, 'heads'), may hold values from -0.1875 to 0.1875
- valuebias: bfloat16 [1024], P('heads'), may hold values from -2 to 2
- mergemap: bfloat16 [1024, 1024], P('heads'), may hold values from -0.5 to 0.5
- mergebias: bfloat16 [1024], replicated, may hold values from -2 to 2
- normgain: bfloat16 [1024], replicated, may hold values from 0.69921875 to 1.296875
- normshift: bfloat16 [1024], replicated, may hold values from -2 to 2
- innermap: bfloat16 [1024, 4096], P(None, 'heads'), may hold values from -0.1875 to 0.1875
- innerbias: bfloat16 [4096], P('heads'), may hold values from -2 to 2
- outermap: bfloat16 [4096, 1024], P('heads'), may hold values from -0.09375 to 0.09375
- outerbias: bfloat16 [1024], replicated, may hold values from -2 to 2
- finalgain: bfloat16 [1024], replicated, may hold values from 0.69921875 to 1.296875
- finalshift: bfloat16 [1024], replicated, may hold values from -2 to 2
- lengths: int32 [8], P('dp'), may hold values from 16 to 1024, as said below
- cotangent: bfloat16 [8, 1024, 1024], P('dp', ('seq', 'heads')), may hold values from -6 to 6
Outputs:
- layer_output: bfloat16 [8, 1024, 1024], P('dp', ('seq', 'heads'))
- tokens_grad: bfloat16 [8, 1024, 1024], P('dp', ('seq', 'heads'))
- querymap_grad: float32 [1024, 1024], P(None, 'heads')
- querybias_grad: float32 [1024], P('heads')
- keymap_grad: float32 [1024, 1024], P(None, 'heads')
- valuemap_grad: float32 [1024, 1024], P(None, 'heads')
- valuebias_grad: float32 [1024], P('heads')
- mergemap_grad: float32 [1024, 1024], P('heads')
- mergebias_grad: float32 [1024], replicated
- normgain_grad: float32 [1024], replicated
- normshift_grad: float32 [1024], replicated
- innermap_grad: float32 [1024, 4096], P(None, 'heads')
- innerbias_grad: float32 [4096], P('heads')
- outermap_grad: float32 [4096, 1024], P('heads')
- outerbias_grad: float32 [1024], replicated
- finalgain_grad: float32 [1024], replicated
- finalshift_grad: float32 [1024], replicated
The draws below stay inside these ranges and needn't reach their ends.
Inputs may be any that keep to these rules, and one draw needn't show every extreme that they name: `lengths`: in each aligned block of 4 proteins (those of one dp index) one protein, drawn from the seed, has length 1024; the others are mostly short.
All inputs are finite; a program needn't handle non-finite values.
Results may differ from the reference program's by a relative error of at most 0.02.
Values may be sent and summed in bfloat16 or wider, within the bound.
No kernel may reach another device: no remote copies, remote signals or barrier semaphores. Data moves between devices by JAX's collectives and lax.ppermute only.
A program may use at most 192 MiB of HBM per device.

```python
import jax
import jax.numpy as jnp
from jax import lax

D = 1024
HEADS = 16
HEAD_DIM = 64
FF = 4096
SEQS_DEV = 4
LENGTH = 1024
BATCH = 8


def draw_lengths(key, part):
    key = jax.random.fold_in(key, 11)
    first_key, second_key = jax.random.split(key)
    raw_draw = jax.random.randint(first_key, (BATCH,), 0, 1024)
    shorter = 16 + (LENGTH - 16) * (raw_draw * raw_draw // 1024) // 1024
    chosen = jax.random.randint(second_key, (BATCH // SEQS_DEV,), 0, SEQS_DEV)
    indices = jnp.arange(BATCH, dtype=jnp.int32)
    longest = indices % SEQS_DEV == chosen[indices // SEQS_DEV]
    return jnp.where(longest, LENGTH, shorter).astype(jnp.int32)


def level_of(own_key, shape, cuts, low, top_value):
    gain, own = 1.0, jax.random.fold_in(own_key, 6)
    for axis_at, shards_of in cuts:
        steps = jnp.exp(jax.random.uniform(jax.random.fold_in(own, axis_at), (shards_of,), jnp.float32, low / len(cuts), top_value / len(cuts)))
        gain = gain * jnp.repeat(steps, shape[axis_at] // shards_of).reshape([-1 if axis == axis_at else 1 for axis in range(len(shape))])
    return gain


def normal_values(stream_key, dims, width, limit, cuts=(), kind=jnp.bfloat16):
    gain = level_of(stream_key, dims, cuts, -0.22, 0.18) if cuts else 1.0
    values = jax.random.normal(stream_key, dims, jnp.float32) * width * gain
    return jnp.minimum(jnp.maximum(values, -limit), limit).astype(kind)


def setup_inputs(seed: int = 0) -> dict:
    key_list = jax.random.split(jax.random.key(seed), 19)
    return {
        "tokens": normal_values(key_list[0], (BATCH, LENGTH, D), 1.0, 6.0, ((0, 2), (1, 16))),
        "querymap": normal_values(key_list[1], (D, D), D ** -0.5, 0.1875, ((1, 4),)),
        "querybias": normal_values(key_list[2], (D,), 0.3, 2.0, ((0, 4),)),
        "keymap": normal_values(key_list[3], (D, D), D ** -0.5, 0.1875, ((1, 4),)),
        "valuemap": normal_values(key_list[4], (D, D), D ** -0.5, 0.1875, ((1, 4),)),
        "valuebias": normal_values(key_list[5], (D,), 0.3, 2.0, ((0, 4),)),
        "mergemap": normal_values(key_list[6], (D, D), (D // 8) ** -0.5, 0.5, ((0, 4),)),
        "mergebias": normal_values(key_list[7], (D,), 0.3, 2.0),
        "normgain": jnp.clip(1.0 + 0.06 * jax.random.normal(key_list[8], (D,), jnp.float32), 0.69921875, 1.296875).astype(jnp.bfloat16),
        "normshift": normal_values(key_list[9], (D,), 0.3, 2.0),
        "innermap": normal_values(key_list[10], (D, FF), D ** -0.5, 0.1875, ((1, 4),)),
        "innerbias": normal_values(key_list[11], (FF,), 0.3, 2.0, ((0, 4),)),
        "outermap": normal_values(key_list[12], (FF, D), FF ** -0.5, 0.09375, ((0, 4),)),
        "outerbias": normal_values(key_list[13], (D,), 0.3, 2.0),
        "finalgain": jnp.clip(1.0 + 0.06 * jax.random.normal(key_list[14], (D,), jnp.float32), 0.69921875, 1.296875).astype(jnp.bfloat16),
        "finalshift": normal_values(key_list[15], (D,), 0.3, 2.0),
        "lengths": draw_lengths(jax.random.fold_in(key_list[18], 71), 0),
        "cotangent": normal_values(key_list[17], (BATCH, LENGTH, D), 1.0, 6.0, ((0, 2), (1, 16))),
    }


@jax.custom_vjp
def low(v):
    return lax.optimization_barrier(v.astype(jnp.bfloat16)).astype(jnp.float32)

@jax.custom_vjp
def low_back(v):
    return v

def low_keep(v):
    return (low(v), None)

def low_pass(kept, grad):
    return (grad,)

def back_keep(v):
    return (v, None)

def back_low(kept, grad):
    return (low(grad),)
low.defvjp(low_keep, low_pass)
low_back.defvjp(back_keep, back_low)
epsilon = 1e-06
score_scale = 0.125
masked_score = -1000000000.0

def layer_norm(values, scales, offsets):
    centered = values - lax.optimization_barrier(jnp.mean(values, axis=-1, keepdims=True))
    variance = lax.optimization_barrier(jnp.mean(centered * centered, axis=-1, keepdims=True))
    return centered * lax.rsqrt(variance + epsilon) * scales + offsets

def protein_layer(params, protein, keyvalid):
    querymap, querybias, keymap, valuemap, valuebias, mergemap, mergebias, normgain, normshift, innermap, innerbias, outermap, outerbias, finalgain, finalshift = params
    highest = lax.Precision.HIGHEST
    positions = protein.shape[0]
    queries = low(low_back(jnp.dot(protein, querymap, precision=highest) + querybias))
    keyrows = low(low_back(jnp.dot(protein, keymap, precision=highest)))
    valrows = low(low_back(jnp.dot(protein, valuemap, precision=highest) + valuebias))
    query_heads = queries.reshape(positions, HEADS, HEAD_DIM)
    key_heads = keyrows.reshape(positions, HEADS, HEAD_DIM)
    value_heads = valrows.reshape(positions, HEADS, HEAD_DIM)
    scores = low_back(jnp.einsum('qhd,khd->hqk', query_heads, key_heads, precision=highest) * score_scale)
    scores = jnp.where(keyvalid[None, None, :], scores, masked_score)
    weights_low = low(jax.nn.softmax(scores, axis=-1))
    context = jnp.einsum('hqk,khd->qhd', weights_low, value_heads, precision=highest).reshape(positions, D)
    context = low(low_back(context))
    merged = low_back(jnp.dot(context, mergemap, precision=highest) + mergebias)
    normed = layer_norm(protein + merged, normgain, normshift)
    inner_pre = low_back(jnp.dot(low(normed), innermap, precision=highest) + innerbias)
    active = low(jax.nn.gelu(inner_pre, approximate=False))
    branch = low_back(jnp.dot(active, outermap, precision=highest) + outerbias)
    return layer_norm(normed + branch, finalgain, finalshift)

def reference(tokens, querymap, querybias, keymap, valuemap, valuebias, mergemap, mergebias, normgain, normshift, innermap, innerbias, outermap, outerbias, finalgain, finalshift, lengths, cotangent):
    positions = jnp.arange(LENGTH, dtype=jnp.int32)
    keyvalid = positions[None, :] < lengths[:, None]
    params = tuple((member.astype(jnp.float32) for member in (querymap, querybias, keymap, valuemap, valuebias, mergemap, mergebias, normgain, normshift, innermap, innerbias, outermap, outerbias, finalgain, finalshift)))

    def forward(inputs, weights):

        def one_step(running, protein_pair):
            return (running, jax.checkpoint(protein_layer)(weights, protein_pair[0], protein_pair[1]))
        unused, outputs = lax.scan(one_step, jnp.zeros((), jnp.float32), (inputs, keyvalid))
        return outputs
    outputs, pullback = jax.vjp(forward, tokens.astype(jnp.float32), params)
    masked_grad = cotangent.astype(jnp.float32) * keyvalid[:, :, None].astype(jnp.float32)
    tokens_grad, grads = pullback(masked_grad)
    return (outputs.astype(jnp.bfloat16), tokens_grad.astype(jnp.bfloat16), grads[0], grads[1], grads[2], grads[3], grads[4], grads[5], grads[6], grads[7], grads[8], grads[9], grads[10], grads[11], grads[12], grads[13], grads[14])
```

```python
import functools

import jax
import jax.numpy as jnp
from jax import lax
from jax.experimental import pallas as pl
from jax.experimental.pallas import tpu as pltpu
from jax.sharding import PartitionSpec as P

HEAD_DIM = 64


epsilon = 1e-06
score_scale = 0.125
masked_score = -1000000000.0
low = jnp.bfloat16
wide = jnp.float32
vmem_bytes = 48 * 1024 * 1024


def dot(a, b):
    return jnp.dot(a, b, preferred_element_type=wide)


def dot_nt(a, b):
    return lax.dot_general(a, b, (((1,), (1,)), ((), ())), preferred_element_type=wide)


def dot_tn(a, b):
    return lax.dot_general(a, b, (((0,), (0,)), ((), ())), preferred_element_type=wide)


def swap(value, axis, stride):
    size = lax.axis_size(axis)
    return lax.ppermute(value, axis, [(i, i ^ stride) for i in range(size)])


def after(value, *others):
    return lax.optimization_barrier((value, *others))[0]


def bit_of(bit):
    axis, stride = bit
    return (lax.axis_index(axis) // stride) % 2


def widen(own, other, bit, axis=0):
    upper = bit_of(bit) == 1
    return jnp.concatenate(
        [jnp.where(upper, other, own), jnp.where(upper, own, other)], axis=axis
    )


def halve(value, bit, axis=0):
    half = value.shape[axis] // 2
    at = bit_of(bit) * half
    keep = lax.dynamic_slice_in_dim(value, at, half, axis)
    send = lax.dynamic_slice_in_dim(value, half - at, half, axis)
    return keep, send


def add_low(a, b):
    return (a.astype(wide) + b.astype(wide)).astype(low)


def params(mebibytes):
    return pltpu.CompilerParams(vmem_limit_bytes=mebibytes * 1024 * 1024)


in_vmem = pl.BlockSpec(memory_space=pltpu.VMEM)
in_smem = pl.BlockSpec(memory_space=pltpu.SMEM)


def kernel_call(body, name, arrays, out, flops, scalars=(), scratch=(), mebibytes=16, exps=0):
    size = lambda a: a.size * a.dtype.itemsize
    return pl.pallas_call(
        body,
        in_specs=[in_smem] * len(scalars) + [in_vmem] * len(arrays),
        out_specs=[in_vmem] * len(out),
        out_shape=[jax.ShapeDtypeStruct(*o) for o in out],
        scratch_shapes=list(scratch),
        compiler_params=params(mebibytes),
        cost_estimate=pl.CostEstimate(
            flops=flops, bytes_accessed=sum(size(a) for a in arrays), transcendentals=exps
        ),
        name=name,
    )(*scalars, *arrays)


def place(pos, proteins, groups, share, i, j):
    seq, heads = pos[proteins], pos[proteins + 1]
    return pl.multiple_of(((seq ^ i) * groups + (heads ^ j)) * share, share)


def masked(scores, length, first):
    key_at = first + lax.broadcasted_iota(jnp.int32, scores.shape, 0)
    return jnp.where(key_at < length, scores, masked_score)


def chunks(n, block):
    return [(0, n - block, False)] * (n > block) + [(n - block, n, True)]


def attend_kernel(pieces, groups, pos, *refs):
    q_refs = refs[:groups]
    kv_refs = refs[groups : groups + pieces * groups]
    ctx_refs = refs[groups + pieces * groups : -3]
    ctx_t_ref, lse_ref, kv_all = refs[-3:]
    proteins, share, width = q_refs[0].shape
    total = kv_all.shape[0]
    block = min(256, total)
    heads = range(width // HEAD_DIM)

    def protein(p, carry):
        length = pos[p]
        blocks = (length + block - 1) // block
        for i in range(pieces):
            for j in range(groups):
                at = place(pos, proteins, groups, share, i, j)

                @pl.when(at < blocks * block)
                def _():
                    kv_all[pl.ds(at, share), :] = kv_refs[i * groups + j][p]

        def body(count):
            n = count * block
            queries = jnp.concatenate([ref[p] for ref in q_refs]) * jnp.asarray(score_scale, low)
            cols = lambda h: slice(h * HEAD_DIM, (h + 1) * HEAD_DIM)
            value_cols = lambda h: slice(width + h * HEAD_DIM, width + (h + 1) * HEAD_DIM)
            cuts = chunks(n, block)
            scores = [
                [dot_nt(kv_all[a:b, cols(h)], queries[:, cols(h)]) for a, b, _ in cuts]
                for h in heads
            ]
            weights, denominators = [], []
            for h in heads:
                found = [
                    masked(value, length, a) if last else value
                    for value, (a, _, last) in zip(scores[h], cuts)
                ]
                high = functools.reduce(
                    jnp.maximum, [jnp.max(value, axis=0, keepdims=True) for value in found]
                )
                found = [jnp.exp(value - high) for value in found]
                denominator = sum(jnp.sum(value, axis=0, keepdims=True) for value in found)
                lse_ref[p, h : h + 1, :] = high + jnp.log(denominator)
                weights.append([value.astype(low) for value in found])
                denominators.append(denominator)
            context_t = jnp.concatenate(
                [
                    sum(
                        dot_tn(kv_all[a:b, value_cols(h)], value)
                        for (a, b, _), value in zip(cuts, weights[h])
                    )
                    / denominators[h]
                    for h in heads
                ]
            )
            ctx_t_ref[p] = context_t
            context = context_t.T.astype(low)
            for j, ref in enumerate(ctx_refs):
                ref[p] = context[j * share : (j + 1) * share]

        for count in range(1, total // block + 1):
            pl.when(blocks == count)(functools.partial(body, count))
        return carry

    lax.fori_loop(0, proteins, protein, 0)


def attend_back_kernel(pieces, groups, pos, *refs):
    q_refs, dctx_refs = refs[:groups], refs[groups : 2 * groups]
    ctx_t_ref, lse_ref = refs[2 * groups : 2 * groups + 2]
    refs = refs[2 * groups + 2 :]
    kv_refs, refs = refs[: pieces * groups], refs[pieces * groups :]
    dq_ref, dkv_refs, (kv_all, dkv_all) = refs[0], refs[1:-2], refs[-2:]
    _, share, width = q_refs[0].shape
    rows = groups * share
    proteins = pl.num_programs(0)
    length = pos[pl.program_id(0)]
    total = kv_all.shape[0]
    block = min(256, total)
    blocks = jnp.where(pos[proteins] * rows < length, (length + block - 1) // block, 0)

    @pl.when(blocks == 0)
    def _():
        for ref in (dq_ref, *dkv_refs):
            ref[...] = jnp.zeros(ref.shape, low)

    def body(count):
        n = count * block
        for i in range(pieces):
            for j in range(groups):
                at = place(pos, proteins, groups, share, i, j)
                kv_all[pl.ds(at, share), :] = kv_refs[i * groups + j][0]
        queries = jnp.concatenate([ref[0] for ref in q_refs]) * jnp.asarray(score_scale, low)
        dctx = jnp.concatenate([ref[0] for ref in dctx_refs])
        product = dctx.astype(wide).T * ctx_t_ref[0]
        dq, dk, dv = [], [], []
        for h in range(width // HEAD_DIM):
            cols = slice(h * HEAD_DIM, (h + 1) * HEAD_DIM)
            keys = kv_all[:n, cols]
            values = kv_all[:n, width + h * HEAD_DIM : width + (h + 1) * HEAD_DIM]
            scores = masked(dot_nt(keys, queries[:, cols]), length, 0)
            probs = jnp.exp(scores - lse_ref[0, h : h + 1, :])
            delta = jnp.sum(product[cols, :], axis=0, keepdims=True)
            dprobs = dot_nt(values, dctx[:, cols])
            dscores = (probs * (dprobs - delta)).astype(low)
            dv.append(dot(probs.astype(low), dctx[:, cols]))
            dk.append(dot(dscores, queries[:, cols]))
            dq.append(dot_tn(keys, dscores))
        dkv_all[:n, :width] = jnp.concatenate(dk, axis=1).astype(low)
        dkv_all[:n, width:] = jnp.concatenate(dv, axis=1).astype(low)
        if n < total:
            dkv_all[n:, :] = jnp.zeros((total - n, 2 * width), low)
        dq_all = jnp.concatenate(dq, axis=0).T * score_scale
        dq_ref[...] = dq_all.astype(low).reshape(groups, 1, share, width)
        for i, ref in enumerate(dkv_refs):
            for j in range(groups):
                at = place(pos, proteins, groups, share, i, j)
                ref[j, 0] = dkv_all[pl.ds(at, share), :]

    for count in range(1, total // block + 1):
        pl.when(blocks == count)(functools.partial(body, count))


def rows_spec(*shape):
    return pl.BlockSpec((1, *shape), lambda p, pos: (p, 0, 0))


def attend(pos, queries, kv_pieces):
    groups = len(queries)
    proteins, share, width = queries[0].shape
    rows = groups * share
    total = share * len(kv_pieces)
    found = kernel_call(
        functools.partial(attend_kernel, len(kv_pieces) // groups, groups),
        "attend",
        [*queries, *kv_pieces],
        [(queries[0].shape, low)] * groups
        + [((proteins, width, rows), wide), ((proteins, 8, rows), wide)],
        proteins * rows * total * width * 8,
        scalars=[pos],
        scratch=[pltpu.VMEM((total, 2 * width), low)],
        mebibytes=32,
        exps=proteins * rows * total * (width // HEAD_DIM),
    )
    return found[:groups], found[groups], found[groups + 1]


def attend_back(pos, queries, dctx, ctx_t, lse, kv_pieces):
    groups = len(queries)
    proteins, share, width = queries[0].shape
    rows = groups * share
    total = share * len(kv_pieces)
    spec, pair_spec = rows_spec(share, width), rows_spec(share, 2 * width)
    out_spec = lambda w: pl.BlockSpec((groups, 1, share, w), lambda p, pos: (0, p, 0, 0))
    out = lambda w: jax.ShapeDtypeStruct((groups, proteins, share, w), low)
    pieces = len(kv_pieces) // groups
    found = pl.pallas_call(
        functools.partial(attend_back_kernel, pieces, groups),
        grid_spec=pltpu.PrefetchScalarGridSpec(
            num_scalar_prefetch=1,
            grid=(proteins,),
            in_specs=[spec] * (2 * groups)
            + [rows_spec(width, rows), rows_spec(8, rows)]
            + [pair_spec] * len(kv_pieces),
            out_specs=[out_spec(width)] + [out_spec(2 * width)] * pieces,
            scratch_shapes=[pltpu.VMEM((total, 2 * width), low)] * 2,
        ),
        out_shape=[out(width)] + [out(2 * width)] * pieces,
        compiler_params=params(32),
        cost_estimate=pl.CostEstimate(
            flops=proteins * rows * total * width * 20,
            bytes_accessed=proteins * (rows + total) * width * 10,
            transcendentals=proteins * rows * total * (width // HEAD_DIM),
        ),
        name="attend_back",
    )(pos, *queries, *dctx, ctx_t, lse, *kv_pieces)
    return found[0], found[1:]


def unit_of(values):
    centered = values - jnp.mean(values, axis=-1, keepdims=True)
    variance = jnp.mean(centered * centered, axis=-1, keepdims=True)
    inverse = lax.rsqrt(variance + epsilon)
    return centered * inverse, inverse


def norm_back(grad_rows, unitized, inverse, scales):
    scaled = grad_rows * scales
    grad_mean = jnp.mean(scaled, axis=-1, keepdims=True)
    cross_mean = jnp.mean(scaled * unitized, axis=-1, keepdims=True)
    return inverse * (scaled - grad_mean - unitized * cross_mean)


def steps(rows):
    size = 64 if rows % 64 == 0 else rows
    return [slice(at, at + size) for at in range(0, rows, size)]


def merge_kernel(groups, parts, slot, *refs):
    ctx_refs, refs = refs[:groups], refs[groups:]
    own_map, refs = refs[0], refs[1:]
    part_refs, refs = refs[: len(parts)], refs[len(parts) :]
    tok_ref, bias_ref, gain_ref, shift_ref = refs[:4]
    normed_ref, low_ref, unit_ref, inv_ref, maps_ref, by_slot = refs[4:]
    others = groups - 1
    for masks, ref in zip(parts, part_refs):
        for k, mask in enumerate(masks):
            for j in range(others):
                by_slot[j, slot[0] ^ mask] = ref[k * others + j]
    for j in range(others):
        maps_ref[j] = by_slot[j].reshape(own_map.shape)
    merged = bias_ref[...].astype(wide) + dot(ctx_refs[0][...], own_map[...])
    for j in range(others):
        merged += dot(ctx_refs[j + 1][...], maps_ref[j])
    unit_ref[...] = tok_ref[...].astype(wide) + merged
    for rows in steps(tok_ref.shape[0]):
        unit, inverse = unit_of(unit_ref[rows, :])
        normed = unit * gain_ref[...].astype(wide) + shift_ref[...].astype(wide)
        normed_ref[rows, :] = normed
        low_ref[rows, :] = normed.astype(low)
        unit_ref[rows, :] = unit
        inv_ref[rows, :] = jnp.broadcast_to(inverse, (inverse.shape[0], 128))


def merge_norm(slot, ctx, own_map, parts, masks, tok, bias, gain, shift):
    rows, model = tok.shape
    groups = len(ctx)
    return kernel_call(
        functools.partial(merge_kernel, groups, masks),
        "merge_norm",
        [*ctx, own_map, *parts, tok, bias, gain, shift],
        [
            ((rows, model), wide),
            ((rows, model), low),
            ((rows, model), wide),
            ((rows, 128), wide),
            ((groups - 1, *own_map.shape), low),
        ],
        2 * rows * model * model,
        scalars=[slot],
        scratch=[pltpu.VMEM((groups - 1, 2 * parts[0].shape[0] // (groups - 1), *parts[0].shape[1:]), low)],
    )


def final_kernel(*refs):
    (normed_ref, near_ref, core_ref, far_ref, bias_ref, gain_ref, shift_ref, cot_ref, live_ref) = refs[:9]
    out_ref, dsum_ref, dbranch_ref, sums_ref = refs[9:]
    gain = gain_ref[...].astype(wide)
    gain_sum = shift_sum = bias_sum = 0.0
    for rows in steps(normed_ref.shape[0]):
        branch = near_ref[rows, :].astype(wide) + core_ref[rows, :].astype(wide)
        branch = branch + far_ref[rows, :].astype(wide) + bias_ref[...].astype(wide)
        unit, inverse = unit_of(normed_ref[rows, :] + branch)
        out_ref[rows, :] = (unit * gain + shift_ref[...].astype(wide)).astype(low)
        grad = cot_ref[rows, :].astype(wide) * live_ref[rows, 0:1]
        dsum = norm_back(grad, unit, inverse, gain)
        dsum_ref[rows, :] = dsum
        dbranch = dsum.astype(low)
        dbranch_ref[rows, :] = dbranch
        gain_sum += jnp.sum(grad * unit, axis=0, keepdims=True)
        shift_sum += jnp.sum(grad, axis=0, keepdims=True)
        bias_sum += jnp.sum(dbranch.astype(wide), axis=0, keepdims=True)
    sums_ref[...] = jnp.zeros(sums_ref.shape, wide)
    sums_ref[0:1, :] = bias_sum
    sums_ref[1:2, :] = gain_sum
    sums_ref[2:3, :] = shift_sum


def final_norm(normed, near, core, far, bias, gain, shift, cot, live):
    rows, model = normed.shape
    return kernel_call(
        final_kernel,
        "final_norm",
        [normed, near, core, far, bias, gain, shift, cot, live],
        [((rows, model), low), ((rows, model), wide), ((rows, model), low), ((8, model), wide)],
        40 * rows * model,
    )


def first_back_kernel(groups, *refs):
    (dsum_ref, near_ref, core_ref, far_ref, unit_ref, inv_ref, gain_ref, own_map, maps_ref) = refs[:9]
    dfirst_ref, dmerged_ref, sums_ref = refs[9:12]
    dctx_refs = refs[12:]
    gain = gain_ref[...].astype(wide)
    gain_sum = shift_sum = bias_sum = 0.0
    for rows in steps(dsum_ref.shape[0]):
        grad = near_ref[rows, :].astype(wide) + core_ref[rows, :].astype(wide)
        grad = dsum_ref[rows, :] + grad + far_ref[rows, :].astype(wide)
        unit = unit_ref[rows, :]
        dfirst = norm_back(grad, unit, inv_ref[rows, 0:1], gain)
        dfirst_ref[rows, :] = dfirst
        dmerged = dfirst.astype(low)
        dmerged_ref[rows, :] = dmerged
        gain_sum += jnp.sum(grad * unit, axis=0, keepdims=True)
        shift_sum += jnp.sum(grad, axis=0, keepdims=True)
        bias_sum += jnp.sum(dmerged.astype(wide), axis=0, keepdims=True)
    for j in range(groups):
        merge_map = maps_ref[j - 1] if j else own_map[...]
        dctx_refs[j][...] = dot_nt(dmerged_ref[...], merge_map).astype(low)
    sums_ref[...] = jnp.zeros(sums_ref.shape, wide)
    sums_ref[3:4, :] = bias_sum
    sums_ref[4:5, :] = gain_sum
    sums_ref[5:6, :] = shift_sum


def first_back(dsum, near, core, far, unit, inverse, gain, own_map, maps):
    rows, model = dsum.shape
    groups, width = maps.shape[0] + 1, own_map.shape[0]
    found = kernel_call(
        functools.partial(first_back_kernel, groups),
        "first_back",
        [dsum, near, core, far, unit, inverse, gain, own_map, maps],
        [((rows, model), wide), ((rows, model), low), ((8, model), wide)]
        + [((rows, width), low)] * groups,
        2 * rows * model * model,
    )
    return found[0], found[1], found[2], found[3:]


def forward_kernel(a_ref, b_ref, inner_ref, outer_ref, bias_ref, act_ref, slope_ref, own_ref, other_ref):
    rows = a_ref.shape[0]
    for ref, out, at in ((a_ref, own_ref, 0), (b_ref, other_ref, rows)):
        pre = dot_nt(ref[...], inner_ref[...]) + bias_ref[...]
        upper = 0.5 + 0.5 * lax.erf(pre * 0.7071067811865476)
        active = (pre * upper).astype(low)
        slope = upper + pre * (0.3989422804014327 * jnp.exp(-0.5 * pre * pre))
        act_ref[at : at + rows, :] = active
        slope_ref[at : at + rows, :] = slope.astype(low)
        out[...] = dot(active, outer_ref[...]).astype(low)


def feed_forward(a, b, inner, outer, bias):
    rows, model = a.shape
    hidden = inner.shape[0]
    return kernel_call(
        forward_kernel,
        "feed_forward",
        [a, b, inner, outer, bias],
        [((2 * rows, hidden), low)] * 2 + [((rows, model), low)] * 2,
        8 * rows * model * hidden,
        exps=4 * rows * hidden,
    )


def backward_kernel(a_ref, b_ref, inner_ref, outer_ref, slope_ref, dinner_ref, own_ref, other_ref):
    rows = a_ref.shape[0]
    for ref, out, at in ((a_ref, own_ref, 0), (b_ref, other_ref, rows)):
        dactive = dot_nt(ref[...], outer_ref[...])
        dinner = (dactive * slope_ref[at : at + rows, :].astype(wide)).astype(low)
        dinner_ref[at : at + rows, :] = dinner
        out[...] = dot(dinner, inner_ref[...]).astype(low)


def feed_backward(a, b, inner, outer, slope):
    rows, model = a.shape
    hidden = inner.shape[0]
    return kernel_call(
        backward_kernel,
        "feed_backward",
        [a, b, inner, outer, slope],
        [((2 * rows, hidden), low)] + [((rows, model), low)] * 2,
        8 * rows * model * hidden,
    )


def grad_kernel(numbers, block, bias, *refs):
    hid, row_refs, out_ref = refs[:2], refs[2:-1], refs[-1]
    model = out_ref.shape[-1]
    for k, number in enumerate(numbers):
        cols = slice(number * block, (number + 1) * block)
        total = sums = 0.0
        for i, ref in enumerate(hid):
            half = ref.shape[0] // 2
            total += dot_tn(ref[:half, cols], row_refs[2 * i][...])
            total += dot_tn(ref[half:, cols], row_refs[2 * i + 1][...])
            if bias:
                sums += jnp.sum(ref[:, cols].astype(wide), axis=0, keepdims=True)
        out_ref[k, :block, :] = total.astype(low)
        if bias:
            out_ref[k, block:, :] = jnp.pad(sums, ((0, 15), (0, model - block))).astype(low)


def weight_grad(hid, row_list, block, numbers, bias):
    rows, model = row_list[0].shape
    return kernel_call(
        functools.partial(grad_kernel, numbers, block, bias),
        "weight_grad",
        [*hid, *row_list],
        [((len(numbers), block + 16 * bias, model), low)],
        8 * rows * model * len(numbers) * block,
    )[0]


def units_kernel(units, shares, slot, inner_ref, outer_ref, bias_ref, own_inner, own_outer, own_bias):
    for m in range(shares):
        at = pl.multiple_of((slot[0] ^ (m << 1)) * units, units)
        own_inner[m] = inner_ref[:, pl.ds(at, units)].T
        own_outer[m] = outer_ref[pl.ds(at, units), :]
        own_bias[m] = jnp.broadcast_to(bias_ref[:, pl.ds(at, units)], (16, units))


def own_units(slot, shares, innermap, outermap, innerbias):
    model = innermap.shape[0]
    units = innermap.shape[1] // (2 * shares)
    if units % 128:
        found = []
        for m in range(shares):
            at = (slot[0] ^ (m << 1)) * units
            inner = lax.dynamic_slice_in_dim(innermap, at, units, 1).T
            outer = lax.dynamic_slice_in_dim(outermap, at, units, 0)
            bias = lax.dynamic_slice_in_dim(innerbias, at, units, 1)
            found.append((inner, outer, jnp.broadcast_to(bias, (16, units))))
        return [jnp.stack(pieces) for pieces in zip(*found)]
    return kernel_call(
        functools.partial(units_kernel, units, shares),
        "own_units",
        [innermap, outermap, innerbias],
        [((shares, units, model), low)] * 2 + [((shares, 16, units), innerbias.dtype)],
        shares * units * model,
        scalars=[slot],
    )


def join_kernel(units, count, *refs):
    own_inner, own_outer, own_bias = refs[:3]
    inner_parts, outer_parts = refs[3 : 3 + count], refs[3 + count : -3]
    inner_ref, outer_ref, bias_ref = refs[-3:]
    at = 0
    for ref in inner_parts:
        for k in range(ref.shape[0]):
            m = at // (2 * units)
            far = at + units
            inner_ref[at:far, :] = own_inner[m]
            inner_ref[far : far + units, :] = ref[k, :units, :]
            bias_ref[:, at:far] = own_bias[m, 0:1, :].astype(wide)
            bias_ref[:, far : far + units] = ref[k, units : units + 1, :units].astype(wide)
            at += 2 * units
    at = 0
    for ref in outer_parts:
        for k in range(ref.shape[0]):
            m = at // (2 * units)
            outer_ref[at : at + units, :] = own_outer[m]
            outer_ref[at + units : at + 2 * units, :] = ref[k]
            at += 2 * units


def join_units(own, inner_parts, outer_parts):
    own_inner, own_outer, own_bias = own
    shares, units, model = own_inner.shape
    hidden = 2 * shares * units
    return kernel_call(
        functools.partial(join_kernel, units, len(inner_parts)),
        "join_units",
        [*own, *inner_parts, *outer_parts],
        [((hidden, model), low)] * 2 + [((1, hidden), wide)],
        hidden * model,
    )


def slot_order(number, bits):
    return ((number & 1) << (bits - 1)) | (number >> 1)


def qkv_kernel(counts, slots, slot, *refs):
    out_ref, q_all, kv_all = refs[-3:]
    dq_ref, refs = refs[0], refs[1:-3]
    width, model = dq_ref.shape[-1], out_ref.shape[-1]
    q_all[...] = dq_ref[...].reshape(q_all.shape)
    q_sum = jnp.sum(q_all[...].astype(wide), axis=0, keepdims=True)
    q_grad = kv_grad = kv_sum = 0.0
    for i, count in enumerate(counts):
        dkv_ref, tok_refs, refs = refs[0], refs[1 : 1 + count], refs[1 + count :]
        kv_all[...] = dkv_ref[...].reshape(kv_all.shape)
        kv_sum += jnp.sum(kv_all[...].astype(wide), axis=0, keepdims=True)
        at = 0
        for tok_ref in tok_refs:
            there = slice(at, at + tok_ref.shape[0])
            at += tok_ref.shape[0]
            kv_grad += dot_tn(kv_all[there, :], tok_ref[...])
            if i == 0:
                q_grad += dot_tn(q_all[there, :], tok_ref[...])
    grad = jnp.concatenate([q_grad, kv_grad]).astype(low)
    sums = jnp.concatenate([q_sum, kv_sum], axis=1)
    bits = slots.bit_length() - 1
    block = 3 * width // slots
    for b in range(slots):
        at = slot_order(slot[0] ^ b, bits)
        out_ref[at, :block, :] = grad[b * block : (b + 1) * block]
        line = jnp.pad(sums[:, b * block : (b + 1) * block], ((0, 15), (0, model - block)))
        out_ref[at, block : block + 16, :] = line.astype(low)


def qkv_grads(slot, slots, dq, pairs):
    model = pairs[0][1][0].shape[-1]
    groups, width = dq.shape[0], dq.shape[-1]
    total = dq.size // width
    return kernel_call(
        functools.partial(qkv_kernel, [len(tok) for _, tok in pairs], slots),
        "qkv_grads",
        [dq] + [a for dkv, tok in pairs for a in (dkv, *tok)],
        [((slots, 3 * width // slots + 16, model), low)],
        10 * total * model * width,
        scalars=[slot],
        scratch=[pltpu.VMEM((total, width), low), pltpu.VMEM((total, 2 * width), low)],
        mebibytes=24,
    )[0]


def feed_out_kernel(units, grads_ref, inner_ref, outer_ref):
    slots = grads_ref.shape[0]
    for k in range(slots):
        cols = slice(k * units, (k + 1) * units)
        inner_ref[:, cols] = grads_ref[k, :units, :].astype(wide).T
        outer_ref[cols, :] = grads_ref[k, units : 2 * units, :].astype(wide)


def feed_out(grads, units):
    slots, _, model = grads.shape
    hidden = slots * units
    return kernel_call(
        functools.partial(feed_out_kernel, units),
        "feed_out",
        [grads],
        [((model, hidden), wide), ((hidden, model), wide)],
        slots * units * model,
        mebibytes=40,
    )


def qkv_out_kernel(block, order, slot, *refs):
    parts, refs = refs[: len(order)], refs[len(order) :]
    q_ref, k_ref, v_ref, merge_ref, bias_ref, rows_all, merge_all = refs
    width = q_ref.shape[1]
    for masks, part in zip(order, parts):
        for k, mask in enumerate(masks):
            at = slot[0] ^ mask
            rows_all[at] = part[k, :block, :]
            bias_ref[pl.ds(at, 1), :] = part[k, block : block + 1, :].astype(wide)
            merge_all[at] = part[k, block + 16 :, :]
    grad = rows_all[...].reshape(3 * width, -1)
    for i, ref in enumerate((q_ref, k_ref, v_ref)):
        ref[...] = grad[i * width : (i + 1) * width].astype(wide).T
    merge_ref[...] = merge_all[...].reshape(merge_ref.shape).astype(wide)


def qkv_out(slot, parts, order, block, width):
    model = parts[0].shape[-1]
    slots = 3 * width // block
    size = width // slots
    return kernel_call(
        functools.partial(qkv_out_kernel, block, order),
        "qkv_out",
        parts,
        [((model, width), wide)] * 3 + [((width, model), wide), ((slots, model), wide)],
        3 * width * model,
        scalars=[slot],
        scratch=[pltpu.VMEM((slots, block, model), low), pltpu.VMEM((slots, size, model), low)],
    )


def shards(
    tokens,
    querymap,
    querybias,
    keymap,
    valuemap,
    valuebias,
    mergemap,
    mergebias,
    normgain,
    normshift,
    innermap,
    innerbias,
    outermap,
    outerbias,
    finalgain,
    finalshift,
    lengths,
    cotangent,
):
    proteins, share, model = tokens.shape
    groups = lax.axis_size("heads")
    rows = proteins * share
    width = querymap.shape[1]
    seq, heads = lax.axis_index("seq"), lax.axis_index("heads")
    seq_size, dp_size = lax.axis_size("seq"), lax.axis_size("dp")
    pos = jnp.concatenate([lengths, jnp.stack([seq, heads]).astype(jnp.int32)])
    core_bit, row_bit, far_bit = ("seq", 1), ("heads", 1), ("heads", 2)
    seq_bits = [("seq", 1 << k) for k in range(1, seq_size.bit_length() - 1)]
    share_bits = seq_bits + [("dp", 1 << k) for k in range(dp_size.bit_length() - 1)]
    slot_bits = [core_bit] + share_bits
    slots = 1 << len(slot_bits)
    shares = slots // 2
    slot = lax.axis_index("dp") * seq_size + seq
    units = innermap.shape[1] // slots
    merge_units = width // slots
    row = lambda vector: vector.reshape(1, -1)

    slot_scalar = slot.reshape(1).astype(jnp.int32)

    own_rows = tokens.reshape(rows, model)
    second = swap(own_rows, *far_bit)
    first = swap(own_rows, *row_bit)
    kv_map = jnp.concatenate([keymap, valuemap], axis=1)
    kv_bias = jnp.concatenate([jnp.zeros_like(valuebias), valuebias]).astype(wide)

    def keys_values(piece):
        return (dot(piece, kv_map) + kv_bias).astype(low).reshape(proteins, share, 2 * width)

    def query_rows(piece):
        found = (dot(piece, querymap) + querybias.astype(wide)).astype(low)
        return found.reshape(proteins, share, width)

    kv_own, q_own = keys_values(own_rows), query_rows(own_rows)
    merge_own = lax.dynamic_slice_in_dim(mergemap, slot * merge_units, merge_units, 0)
    merge_first = swap(merge_own, *row_bit)
    own = own_units(slot_scalar, shares, innermap, outermap, row(innerbias))
    inner_pack = jnp.concatenate([own[0][0], jnp.pad(own[2][0], ((0, 0), (0, model - units)))])
    third = swap(after(second, inner_pack, q_own), *row_bit)
    kv_first, kv_second = keys_values(first), keys_values(second)
    q_first, q_second = query_rows(first), query_rows(second)
    merge_far = swap(after(jnp.stack([merge_own, merge_first]), kv_second), *far_bit)
    inner_pack = swap(after(inner_pack, kv_second), *far_bit)
    kv_third, q_third = keys_values(third), query_rows(third)
    outer_pack = swap(after(own[1][0], kv_third), *far_bit)
    token_pieces = [own_rows, first, second, third]
    queries = [q_own, q_first, q_second, q_third]
    kv_by_seq = {0: [kv_own, kv_first, kv_second, kv_third]}
    for axis, stride in seq_bits + [core_bit]:
        for i in list(kv_by_seq):
            kv_by_seq[i | stride] = [swap(piece, axis, stride) for piece in kv_by_seq[i]]
    kv_pieces = [piece for i in range(seq_size) for piece in kv_by_seq[i]]

    merge_parts = jnp.concatenate([merge_first[None], merge_far])
    merge_masks = [0]
    for k in reversed(range(1, len(slot_bits))):
        merge_parts = after(merge_parts, kv_third)
        merge_parts = jnp.concatenate([merge_parts, swap(merge_parts, *slot_bits[k])])
        merge_masks = merge_masks + [mask | (1 << k) for mask in merge_masks]
    inner_parts = [inner_pack[None]]
    for k, bit in enumerate(share_bits):
        if k:
            inner_parts = [after(jnp.concatenate(inner_parts), context[0])]
        inner_parts.append(swap(after(inner_parts[0], kv_third), *bit))
        if not k:
            context, context_t, logsum = attend(
                pos, after(queries, inner_parts[0]), kv_pieces
            )
    outer_parts, outer_order = after(outer_pack, context[0])[None], [0]
    for k in reversed(range(len(share_bits))):
        outer_parts = jnp.concatenate([outer_parts, swap(outer_parts, *share_bits[k])])
        outer_order = outer_order + [m | (1 << k) for m in outer_order]
    outer_parts = [outer_parts[outer_order.index(m)][None] for m in range(shares)]

    merge_core = swap(after(merge_parts, context[0]), *core_bit)
    context = [c.reshape(rows, width) for c in context]
    context = [context[0]] + [swap(context[j], "heads", j) for j in range(1, groups)]
    normed, normed_low, first_unit, first_inverse, other_maps = merge_norm(
        slot_scalar,
        context,
        mergemap,
        [merge_parts, merge_core],
        [merge_masks, [mask | 1 for mask in merge_masks]],
        own_rows,
        row(mergebias),
        row(normgain),
        row(normshift),
    )
    inner_t, outer_w, inner_b = join_units(own, inner_parts, after(outer_parts, normed_low))

    def gather_rows(own):
        across = swap(own, *row_bit)
        near = swap(own, *core_bit)
        return own, near, across, swap(across, *core_bit)

    normed_rows = gather_rows(normed_low)
    near_act, near_slope, near_own, near_other = feed_forward(
        normed_rows[0], normed_rows[1], inner_t, outer_w, inner_b
    )
    far_act, far_slope, far_own, far_other = feed_forward(
        after(normed_rows[2], near_act), normed_rows[3], inner_t, outer_w, inner_b
    )
    far_sum = swap(add_low(far_own, swap(far_other, *core_bit)), *row_bit)
    seq_tokens = {0: [jnp.concatenate(token_pieces[:2]), jnp.concatenate(token_pieces[2:])]}
    seq_tokens[0] = after(seq_tokens[0], near_act)
    for axis, stride in seq_bits:
        for i in list(seq_tokens):
            one = swap(seq_tokens[i][0], axis, stride)
            two = swap(after(seq_tokens[i][1], one), axis, stride)
            seq_tokens[i | stride] = [one, two]
    own_at = (seq * groups + heads) * share + jnp.arange(share, dtype=jnp.int32)
    live = (own_at[None, :] < lengths[:, None]).astype(wide).reshape(rows, 1)
    layer_output, dsum_final, dbranch, final_sums = final_norm(
        normed,
        near_own,
        swap(near_other, *core_bit),
        after(far_sum, seq_tokens[seq_bits[0][1]][0]),
        row(outerbias),
        row(finalgain),
        row(finalshift),
        cotangent.reshape(rows, model),
        jnp.broadcast_to(live, (rows, 128)),
    )
    dbranch_rows = gather_rows(dbranch)
    near_dinner, near_own, near_other = feed_backward(
        dbranch_rows[0], dbranch_rows[1], inner_t, outer_w, near_slope
    )
    far_dinner, far_own, far_other = feed_backward(
        after(dbranch_rows[2], near_dinner), dbranch_rows[3], inner_t, outer_w, far_slope
    )
    far_part = add_low(far_own, swap(far_other, *core_bit))
    far_sum = swap(far_part, *row_bit)

    hid_block = 2 * units
    last = len(share_bits) - 1
    numbers = lambda k, side: [m for m in range(shares) if (m >> k) & 1 == side]
    near_far = [near_act, far_act], [near_dinner, far_dinner]
    outer_send = weight_grad(
        near_far[0], after(dbranch_rows, far_part), hid_block, numbers(last, 1), 0
    )
    outer_got = swap(outer_send, *share_bits[last])
    inner_send = weight_grad(
        near_far[1], after(normed_rows, outer_send), hid_block, numbers(0, 1), 1
    )
    inner_got = swap(inner_send, *share_bits[0])
    outer_keep = weight_grad(
        near_far[0], after(dbranch_rows, inner_send), hid_block, numbers(last, 0), 0
    )
    inner_keep = weight_grad(
        near_far[1], after(normed_rows, outer_keep), hid_block, numbers(0, 0), 1
    )

    dfirst, dmerged, first_sums, dcontext = first_back(
        dsum_final,
        near_own,
        swap(near_other, *core_bit),
        after(far_sum, inner_keep),
        first_unit,
        first_inverse,
        row(normgain),
        mergemap,
        other_maps,
    )
    dcontext = [dcontext[0]] + [swap(dcontext[j], "heads", j) for j in range(1, groups)]
    dcontext = [d.reshape(proteins, share, width) for d in dcontext]

    def shared_sum(keep, got, k):
        value = add_low(keep, got)
        for bit in reversed([b for i, b in enumerate(share_bits) if i != k]):
            half = value.shape[0] // 2
            send, value = value[half:], value[:half]
            value = add_low(value, after(swap(send, *bit), dqueries) if half == 1 else swap(send, *bit))
        return value[0]

    merge_sum = jnp.stack([dot_tn(piece, dmerged) for piece in context]).astype(low)
    extra = jnp.concatenate([final_sums + first_sums, jnp.zeros((8, model), wide)])

    def merge_step(merge_sum, extra, bit, wait):
        keep, send = halve(merge_sum, bit, 1)
        size = send.shape[1]
        block = jnp.concatenate([send.reshape(-1, model), extra.astype(low)])
        block = after(swap(block, *bit), wait)
        extra = extra + block[groups * size :].astype(wide)
        return add_low(keep, block[: groups * size].reshape(keep.shape)), extra

    dqueries, dkv_by_seq = attend_back(pos, queries, dcontext, context_t, logsum, kv_pieces)
    dkv_parts = [
        add_low(dkv_by_seq[i], swap(dkv_by_seq[i + 1], *core_bit)) for i in range(0, seq_size, 2)
    ]
    far_first = dkv_parts[1]
    half = groups // 2
    dkv_halves = []
    for at in (half, 0):
        parts = [part[at : at + half] for part in dkv_parts]
        for k in reversed(range(len(seq_bits))):
            count = 1 << k
            got = [swap(parts[count + i], *seq_bits[k]) for i in range(count)]
            parts = [add_low(parts[i], got[i]) for i in range(count)]
        dkv_halves.append(parts[0].reshape(half, rows, 2 * width))

    outer_sum = shared_sum(outer_keep, after(outer_got, dmerged), last)
    inner_sum = shared_sum(inner_keep, after(inner_got, dmerged), 0)
    pack = jnp.concatenate([inner_sum[units:], outer_sum[units:]])
    block = swap(after(pack, far_first), *far_bit)

    pairs = [(dkv_parts[0], token_pieces)] + [
        (dkv_parts[i], seq_tokens[2 * i]) for i in range(1, seq_size // 2)
    ]
    slot_grads = qkv_grads(slot_scalar, slots, after(dqueries, pack), pairs)
    block = after(block, slot_grads)
    pack = jnp.concatenate(
        [
            add_low(inner_sum[:units], block[:units]),
            add_low(outer_sum[:units], block[units + 16 :]),
            jnp.pad(
                add_low(inner_sum[2 * units :, :units], block[units : units + 16, units : 2 * units]),
                ((0, 0), (0, model - units)),
            ),
        ]
    )
    grads = lax.all_gather(pack, ("dp", "seq"))
    dkv = [dkv_halves[1][0], dkv_halves[1][1], dkv_halves[0][0], dkv_halves[0][1]]
    dqs = dqueries.reshape(groups, rows, width)
    parts = [dot_nt(dqs[j], querymap) + dot_nt(dkv[j], kv_map) for j in range(groups)]
    rest = swap(parts[3].astype(low), *row_bit)
    near = swap(parts[1].astype(low), *row_bit)
    far = swap((parts[2] + rest.astype(wide)).astype(low), *far_bit)
    tokens_grad = (dfirst + parts[0] + near.astype(wide) + far.astype(wide)).astype(low)
    innermap_grad, outermap_grad = feed_out(grads, units)
    innerbias_grad = grads[:, 2 * units, :units].reshape(-1).astype(wide)

    for k, bit in reversed(list(enumerate(share_bits + [core_bit]))):
        half = 1 << k
        slot_grads = add_low(slot_grads[:half], swap(slot_grads[half:], *bit))
    waits = [dqueries, far_first] + [slot_grads] * len(slot_bits)
    for bit, wait in zip(reversed(slot_bits), waits):
        merge_sum, extra = merge_step(merge_sum, extra, bit, wait)
    block = jnp.concatenate([merge_sum[1], merge_sum[3], extra.astype(low)])
    block = swap(block, *row_bit)
    extra = extra + block[2 * merge_units :].astype(wide)
    merge_near = add_low(merge_sum[0], block[:merge_units])
    merge_far = add_low(merge_sum[2], block[merge_units : 2 * merge_units])
    block = swap(jnp.concatenate([merge_far, extra.astype(low)]), *far_bit)
    extra = extra + block[merge_units:].astype(wide)
    merge_near = add_low(merge_near, block[:merge_units])
    out_pack = jnp.concatenate([slot_grads[0], merge_near])[None]
    parts, order = [out_pack], [[0]]
    for k in range(1, len(slot_bits)):
        parts = [jnp.concatenate(parts)] if len(parts) > 1 else parts
        order = [sum(order, [])]
        parts = parts + [swap(parts[0], *slot_bits[k])]
        order = order + [[mask | (1 << k) for mask in order[0]]]
    core_parts = [swap(part, *core_bit) for part in parts]
    core_order = [[mask | 1 for mask in masks] for masks in order]
    q_grad, k_grad, v_grad, mergemap_grad, bias_rows = qkv_out(
        slot_scalar, parts + core_parts, order + core_order, 3 * width // slots, width
    )
    bias_grads = bias_rows[:, : 3 * width // slots].reshape(-1)
    shape = tokens.shape
    return (
        layer_output.reshape(shape),
        tokens_grad.reshape(shape),
        q_grad,
        bias_grads[:width],
        k_grad,
        v_grad,
        bias_grads[2 * width :],
        mergemap_grad,
        extra[3],
        extra[4],
        extra[5],
        innermap_grad,
        innerbias_grad,
        outermap_grad,
        extra[0],
        extra[1],
        extra[2],
    )


def solution(mesh):
    return jax.shard_map(
        shards,
        mesh=mesh,
        in_specs=(
            P("dp", ("seq", "heads"), None),
            P(None, "heads"),
            P("heads"),
            P(None, "heads"),
            P(None, "heads"),
            P("heads"),
            P("heads", None),
            P(),
            P(),
            P(),
            P(None, "heads"),
            P("heads"),
            P("heads", None),
            P(),
            P(),
            P(),
            P("dp"),
            P("dp", ("seq", "heads"), None),
        ),
        out_specs=(
            P("dp", ("seq", "heads"), None),
            P("dp", ("seq", "heads"), None),
            P(None, "heads"),
            P("heads"),
            P(None, "heads"),
            P(None, "heads"),
            P("heads"),
            P("heads", None),
            P(),
            P(),
            P(),
            P(None, "heads"),
            P("heads"),
            P("heads", None),
            P(),
            P(),
            P(),
        ),
        check_vma=False,
    )
```

```python
import functools

import jax
import jax.numpy as jnp
from jax import lax
from jax.experimental import pallas as pl
from jax.experimental.pallas import tpu as pltpu
from jax.sharding import PartitionSpec as P

HEAD_DIM = 64


epsilon = 1e-06
score_scale = 0.125
masked_score = -1000000000.0
low = jnp.bfloat16
wide = jnp.float32
vmem_bytes = 48 * 1024 * 1024


def dot(a, b):
    return jnp.dot(a, b, preferred_element_type=wide)


def dot_nt(a, b):
    return lax.dot_general(a, b, (((1,), (1,)), ((), ())), preferred_element_type=wide)


def dot_tn(a, b):
    return lax.dot_general(a, b, (((0,), (0,)), ((), ())), preferred_element_type=wide)


def swap(value, axis, stride):
    size = lax.axis_size(axis)
    return lax.ppermute(value, axis, [(i, i ^ stride) for i in range(size)])


def swap_slots(value, mask):
    size = lax.axis_size("dp") * lax.axis_size("seq")
    return lax.ppermute(value, ("dp", "seq"), [(i, i ^ mask) for i in range(size)])


def bit_of(bit):
    axis, stride = bit
    return (lax.axis_index(axis) // stride) % 2


def add_low(a, b):
    return (a.astype(wide) + b.astype(wide)).astype(low)


def params(mebibytes):
    return pltpu.CompilerParams(vmem_limit_bytes=mebibytes * 1024 * 1024)


in_vmem = pl.BlockSpec(memory_space=pltpu.VMEM)
in_smem = pl.BlockSpec(memory_space=pltpu.SMEM)
anywhere = pl.BlockSpec(memory_space=pl.ANY)
in_hbm = pl.BlockSpec(memory_space=pltpu.HBM)
hbm = True
kernels_alone = ("attend", "attend_back", "merge_norm", "project", "join_units", "stack_pairs")


def kernel_call(
    body, name, arrays, out, scalars=(), scratch=(), mebibytes=16, waits=(), far_in=(), local=(), flops=1
):
    ns, na, nw, no, nl = len(scalars), len(arrays), len(waits), len(out), len(local)
    alone = name in kernels_alone
    far_in = [i for i in range(na) if alone and (far_in is hbm or i in far_in)]
    far_out = [i for i, o in enumerate(out) if alone and len(o) > 2 and o[2]]
    buffers = [pltpu.VMEM(arrays[i].shape, arrays[i].dtype) for i in far_in]
    buffers += [pltpu.VMEM(out[i][0], out[i][1]) for i in far_out]
    count = len(buffers)

    def whole(*refs):
        here = list(refs[: ns + na])
        at = ns + na + nw
        kept, outs, rest = refs[at : at + nl], list(refs[at + nl : at + nl + no]), refs[at + nl + no :]
        rest, (*held_refs, sems) = (rest[: len(rest) - count - 1], rest[len(rest) - count - 1 :])
        copies = []
        for k, i in enumerate(far_in):
            copies.append(pltpu.make_async_copy(here[ns + i], held_refs[k], sems.at[k]))
            copies[-1].start()
            here[ns + i] = held_refs[k]
        for copy in copies:
            copy.wait()
        copies = []
        for k, i in enumerate(far_out, len(far_in)):
            copies.append(pltpu.make_async_copy(held_refs[k], outs[i], sems.at[k]))
            outs[i] = held_refs[k]
        body(*here, *kept, *outs, *rest)
        for copy in copies:
            copy.start()
        for copy in copies:
            copy.wait()

    return pl.pallas_call(
        whole,
        in_specs=[in_smem] * ns
        + [in_hbm if i in far_in else in_vmem for i in range(na)]
        + [anywhere] * nw
        + [in_hbm] * nl,
        out_specs=[in_hbm if i in far_out else in_vmem for i in range(no)],
        out_shape=[jax.ShapeDtypeStruct(o[0], o[1]) for o in out],
        scratch_shapes=list(scratch) + buffers + [pltpu.SemaphoreType.DMA((max(count, 1),))],
        compiler_params=params(60 if alone else mebibytes),
        cost_estimate=pl.CostEstimate(flops=flops, bytes_accessed=1, transcendentals=0),
        name=name,
    )(*scalars, *arrays, *waits, *local)


def nothing(*refs):
    pass


def gate(values, waits):
    found = pl.pallas_call(
        nothing,
        in_specs=[anywhere] * (len(values) + len(waits)),
        out_specs=[anywhere] * len(values),
        out_shape=[jax.ShapeDtypeStruct(v.shape, v.dtype) for v in values],
        input_output_aliases={i: i for i in range(len(values))},
        compiler_params=params(1),
        name="gate",
    )(*values, *waits)
    return list(found)


def pad16(count):
    return -(-count // 16) * 16


def place(pos, proteins, groups, share, i, j):
    seq, heads = pos[proteins], pos[proteins + 1]
    return pl.multiple_of(((seq ^ i) * groups + (heads ^ j)) * share, share)


def masked(scores, length, first):
    key_at = first + lax.broadcasted_iota(jnp.int32, scores.shape, 0)
    return jnp.where(key_at < length, scores, masked_score)


def chunks(n, block):
    return [(0, n - block, False)] * (n > block) + [(n - block, n, True)]


def piece_list(refs, groups):
    found, count = [], 0
    for ref in refs:
        for n in range(ref.shape[0]):
            found.append((ref, count // groups, count % groups, n))
            count += 1
    return found


def start_keys(pos, p, proteins, groups, kv_refs, kv_all, sems, blocks, block, wait):
    share = kv_refs[0].shape[2]
    for k, (ref, i, j, n) in enumerate(piece_list(kv_refs, groups)):
        at = place(pos, proteins, groups, share, i, j)

        @pl.when(at < blocks * block)
        def _():
            copy = pltpu.make_async_copy(ref.at[n, p], kv_all.at[p, pl.ds(at, share), :], sems.at[p])
            if wait:
                copy.wait()
            else:
                copy.start()


def query_rows(refs, p):
    found = [ref[n, p] for ref in refs for n in range(ref.shape[0])]
    return jnp.concatenate(found) * jnp.asarray(score_scale, low)


def attend_kernel(counts, pos, *refs):
    stacks, arrays, groups = counts
    q_refs, kv_refs = refs[:stacks], refs[stacks : stacks + arrays]
    ctx_refs, (ctx_t_ref, lse_ref, kv_all, sems) = refs[stacks + arrays : -4], refs[-4:]
    _, proteins, share, width = q_refs[0].shape
    total = kv_all.shape[1]
    block = min(256, total)
    heads = range(width // HEAD_DIM)

    def keys_of(p, wait):
        blocks = (pos[p] + block - 1) // block
        start_keys(pos, p, proteins, groups, kv_refs, kv_all, sems, blocks, block, wait)
        return blocks

    for p in range(proteins):
        keys_of(p, False)

    def protein(p, carry):
        length = pos[p]
        blocks = keys_of(p, True)

        def body(count):
            n = count * block
            queries = query_rows(q_refs, p)
            cols = lambda h: slice(h * HEAD_DIM, (h + 1) * HEAD_DIM)
            value_cols = lambda h: slice(width + h * HEAD_DIM, width + (h + 1) * HEAD_DIM)
            cuts = chunks(n, block)
            scores = [
                [dot_nt(kv_all[p, a:b, cols(h)], queries[:, cols(h)]) for a, b, _ in cuts]
                for h in heads
            ]
            weights, denominators = [], []
            for h in heads:
                found = [
                    masked(value, length, a) if last else value
                    for value, (a, _, last) in zip(scores[h], cuts)
                ]
                high = functools.reduce(
                    jnp.maximum, [jnp.max(value, axis=0, keepdims=True) for value in found]
                )
                found = [jnp.exp(value - high) for value in found]
                denominator = sum(jnp.sum(value, axis=0, keepdims=True) for value in found)
                lse_ref[p, h : h + 1, :] = high + jnp.log(denominator)
                weights.append([value.astype(low) for value in found])
                denominators.append(denominator)
            context_t = jnp.concatenate(
                [
                    sum(
                        dot_tn(kv_all[p, a:b, value_cols(h)], value)
                        for (a, b, _), value in zip(cuts, weights[h])
                    )
                    / denominators[h]
                    for h in heads
                ]
            )
            ctx_t_ref[p] = context_t
            context = context_t.T.astype(low)
            for j, ref in enumerate(ctx_refs):
                ref[p] = context[j * share : (j + 1) * share]

        for count in range(1, total // block + 1):
            pl.when(blocks == count)(functools.partial(body, count))
        return carry

    lax.fori_loop(0, proteins, protein, 0)


def attend_back_kernel(counts, pos, *refs):
    stacks, arrays, groups = counts
    q_refs, dctx_refs, refs = refs[:stacks], refs[stacks : stacks + groups], refs[stacks + groups :]
    ctx_t_ref, lse_ref, kv_refs, refs = refs[0], refs[1], refs[2 : 2 + arrays], refs[2 + arrays :]
    dq_ref, dkv_refs, (kv_all, dkv_all, sems) = refs[0], refs[1:-3], refs[-3:]
    _, proteins, share, width = q_refs[0].shape
    rows = groups * share
    total = kv_all.shape[1]
    block = min(256, total)
    heads = range(width // HEAD_DIM)

    def keys_of(p, wait):
        blocks = jnp.where(pos[proteins] * rows < pos[p], (pos[p] + block - 1) // block, 0)
        start_keys(pos, p, proteins, groups, kv_refs, kv_all, sems, blocks, block, wait)
        return blocks

    for p in range(proteins):
        keys_of(p, False)

    def protein(p, carry):
        length = pos[p]
        blocks = keys_of(p, True)

        @pl.when(blocks == 0)
        def _():
            for ref in (dq_ref, *dkv_refs):
                ref[:, p] = jnp.zeros((groups, share, ref.shape[-1]), low)

        def body(count):
            n = count * block
            queries = query_rows(q_refs, p)
            dctx = jnp.concatenate([ref[p] for ref in dctx_refs])
            product = dctx.astype(wide).T * ctx_t_ref[p]
            cols = lambda h: slice(h * HEAD_DIM, (h + 1) * HEAD_DIM)
            value_cols = lambda h: slice(width + h * HEAD_DIM, width + (h + 1) * HEAD_DIM)
            deltas = [jnp.sum(product[cols(h), :], axis=0, keepdims=True) for h in heads]
            dq = []
            for a, b, last in chunks(n, block):
                scores = [dot_nt(kv_all[p, a:b, cols(h)], queries[:, cols(h)]) for h in heads]
                dprobs = [dot_nt(kv_all[p, a:b, value_cols(h)], dctx[:, cols(h)]) for h in heads]
                probs, dscores = [], []
                for h in heads:
                    score = masked(scores[h], length, a) if last else scores[h]
                    prob = jnp.exp(score - lse_ref[p, h : h + 1, :])
                    probs.append(prob.astype(low))
                    dscores.append((prob * (dprobs[h] - deltas[h])).astype(low))
                dv = [dot(probs[h], dctx[:, cols(h)]) for h in heads]
                dk = [dot(dscores[h], queries[:, cols(h)]) for h in heads]
                dq.append(
                    jnp.concatenate([dot_tn(kv_all[p, a:b, cols(h)], dscores[h]) for h in heads])
                )
                dkv_all[a:b, :width] = jnp.concatenate(dk, axis=1).astype(low)
                dkv_all[a:b, width:] = jnp.concatenate(dv, axis=1).astype(low)
            if n < total:
                dkv_all[n:, :] = jnp.zeros((total - n, 2 * width), low)
            dq_all = (sum(dq).T * score_scale).astype(low)
            for j in range(groups):
                dq_ref[j, p] = dq_all[j * share : (j + 1) * share]
            for i, ref in enumerate(dkv_refs):
                for j in range(groups):
                    at = place(pos, proteins, groups, share, i, j)
                    ref[j, p] = dkv_all[pl.ds(at, share), :]

        for count in range(1, total // block + 1):
            pl.when(blocks == count)(functools.partial(body, count))
        return carry

    lax.fori_loop(0, proteins, protein, 0)


def attend(pos, queries, kv_pieces, waits):
    groups = sum(q.shape[0] for q in queries)
    _, proteins, share, width = queries[0].shape
    rows = groups * share
    total = share * sum(piece.shape[0] for piece in kv_pieces)
    found = kernel_call(
        functools.partial(attend_kernel, (len(queries), len(kv_pieces), groups)),
        "attend",
        queries,
        [((proteins, share, width), low, hbm)] * groups
        + [((proteins, width, rows), wide, hbm), ((proteins, 8, rows), wide, hbm)],
        scalars=[pos],
        scratch=[
            pltpu.VMEM((proteins, total, 2 * width), low),
            pltpu.SemaphoreType.DMA((proteins,)),
        ],
        mebibytes=32,
        far_in=hbm,
        local=kv_pieces,
        waits=waits,
        flops=int(1e10),
    )
    return found[:groups], found[groups], found[groups + 1]


def attend_back(pos, queries, dctx, ctx_t, lse, kv_pieces, waits):
    groups = len(dctx)
    _, proteins, share, width = queries[0].shape
    total = share * sum(piece.shape[0] for piece in kv_pieces)
    pieces = total // (groups * share)
    arrays = [*queries, *dctx, ctx_t, lse]
    found = kernel_call(
        functools.partial(attend_back_kernel, (len(queries), len(kv_pieces), groups)),
        "attend_back",
        arrays,
        [((groups, proteins, share, width), low)]
        + [((groups, proteins, share, 2 * width), low)] * pieces,
        scalars=[pos],
        scratch=[
            pltpu.VMEM((proteins, total, 2 * width), low),
            pltpu.VMEM((total, 2 * width), low),
            pltpu.SemaphoreType.DMA((proteins,)),
        ],
        mebibytes=32,
        far_in=[i for i in range(len(arrays)) if not 0 <= i - len(queries) < groups],
        local=kv_pieces,
        waits=waits,
        flops=int(2e10),
    )
    return found[0], found[1:]


def project_kernel(count, *refs):
    tok_refs, (qmap_ref, kmap_ref, vmap_ref, qbias_ref, vbias_ref, q_ref, kv_ref) = refs[:count], refs[count:]
    width = q_ref.shape[-1]
    for j, tok_ref in enumerate(tok_refs):
        shape = q_ref.shape[1:]
        queries = dot(tok_ref[...], qmap_ref[...]) + qbias_ref[...].astype(wide)
        q_ref[j] = queries.astype(low).reshape(shape)
        kv_ref[j, :, :, :width] = dot(tok_ref[...], kmap_ref[...]).astype(low).reshape(shape)
        values = dot(tok_ref[...], vmap_ref[...]) + vbias_ref[...].astype(wide)
        kv_ref[j, :, :, width:] = values.astype(low).reshape(shape)


def project(tok, maps, proteins, waits=()):
    width = maps[0].shape[1]
    share = tok[0].shape[0] // proteins
    return kernel_call(
        functools.partial(project_kernel, len(tok)),
        "project",
        [*tok, *maps],
        [
            ((len(tok), proteins, share, width), low, hbm),
            ((len(tok), proteins, share, 2 * width), low, hbm),
        ],
        waits=waits,
        far_in=hbm,
    )


def unit_of(values):
    centered = values - jnp.mean(values, axis=-1, keepdims=True)
    variance = jnp.mean(centered * centered, axis=-1, keepdims=True)
    inverse = lax.rsqrt(variance + epsilon)
    return centered * inverse, inverse


def norm_back(grad_rows, unitized, inverse, scales):
    scaled = grad_rows * scales
    grad_mean = jnp.mean(scaled, axis=-1, keepdims=True)
    cross_mean = jnp.mean(scaled * unitized, axis=-1, keepdims=True)
    return inverse * (scaled - grad_mean - unitized * cross_mean)


def steps(rows):
    size = 64 if rows % 64 == 0 else rows
    return [slice(at, at + size) for at in range(0, rows, size)]


def merge_kernel(groups, heads, *refs):
    ctx_refs, refs = refs[:groups], refs[groups:]
    own_map, maps_all, tok_ref, small_ref = refs[:4]
    normed_ref, low_ref, unit_ref, inv_ref, maps_ref = refs[4:]
    others = groups - 1
    slots, _, size, _ = maps_all.shape
    for j in range(others):
        for k in range(slots):
            maps_ref[j, k * size : (k + 1) * size, :] = maps_all[k, heads[0] ^ (j + 1)]
    merged = small_ref[0:1, :] + dot(ctx_refs[0][...], own_map[...])
    for j in range(others):
        merged += dot(ctx_refs[j + 1][...], maps_ref[j])
    unit_ref[...] = tok_ref[...].astype(wide) + merged
    for rows in steps(tok_ref.shape[0]):
        unit, inverse = unit_of(unit_ref[rows, :])
        normed = unit * small_ref[1:2, :] + small_ref[2:3, :]
        normed_ref[rows, :] = normed
        low_ref[rows, :] = normed.astype(low)
        unit_ref[rows, :] = unit
        inv_ref[rows, :] = jnp.broadcast_to(inverse, (inverse.shape[0], 128))


def merge_norm(heads, ctx, own_map, maps_all, tok, small, waits):
    rows, model = tok.shape
    groups = len(ctx)
    return kernel_call(
        functools.partial(merge_kernel, groups),
        "merge_norm",
        [*ctx, own_map, maps_all, tok, small],
        [
            ((rows, model), wide, hbm),
            ((rows, model), low, hbm),
            ((rows, model), wide, hbm),
            ((rows, 128), wide, hbm),
            ((groups - 1, *own_map.shape), low, hbm),
        ],
        scalars=[heads],
        waits=waits,
        far_in=hbm,
    )


def final_kernel(*refs):
    normed_ref, near_ref, core_ref, far_ref, small_ref, cot_ref, live_ref = refs[:7]
    out_ref, dsum_ref, dbranch_ref, sums_ref = refs[7:]
    gain = small_ref[4:5, :]
    gain_sum = shift_sum = bias_sum = 0.0
    for rows in steps(normed_ref.shape[0]):
        branch = near_ref[rows, :].astype(wide) + core_ref[rows, :].astype(wide)
        branch = branch + far_ref[rows, :].astype(wide) + small_ref[3:4, :]
        unit, inverse = unit_of(normed_ref[rows, :] + branch)
        out_ref[rows, :] = (unit * gain + small_ref[5:6, :]).astype(low)
        grad = cot_ref[rows, :].astype(wide) * live_ref[rows, 0:1]
        dsum = norm_back(grad, unit, inverse, gain)
        dsum_ref[rows, :] = dsum
        dbranch = dsum.astype(low)
        dbranch_ref[rows, :] = dbranch
        gain_sum += jnp.sum(grad * unit, axis=0, keepdims=True)
        shift_sum += jnp.sum(grad, axis=0, keepdims=True)
        bias_sum += jnp.sum(dbranch.astype(wide), axis=0, keepdims=True)
    sums_ref[...] = jnp.zeros(sums_ref.shape, wide)
    sums_ref[0:1, :] = bias_sum
    sums_ref[1:2, :] = gain_sum
    sums_ref[2:3, :] = shift_sum


def final_norm(normed, near, core, across, small, cot, live, waits):
    rows, model = normed.shape
    return kernel_call(
        final_kernel,
        "final_norm",
        [normed, near, core, across, small, cot, live],
        [
            ((rows, model), low, hbm),
            ((rows, model), wide, hbm),
            ((rows, model), low),
            ((8, model), wide, hbm),
        ],
        far_in=[0, 4, 5, 6],
        waits=waits,
    )


def first_back_kernel(groups, *refs):
    dsum_ref, near_ref, core_ref, far_ref, unit_ref, inv_ref, small_ref, own_map, maps_ref = refs[:9]
    dfirst_ref, dmerged_ref, sums_ref = refs[9:12]
    dctx_refs = refs[12:]
    gain = small_ref[1:2, :]
    gain_sum = shift_sum = bias_sum = 0.0
    for rows in steps(dsum_ref.shape[0]):
        grad = near_ref[rows, :].astype(wide) + core_ref[rows, :].astype(wide)
        grad = dsum_ref[rows, :] + grad + far_ref[rows, :].astype(wide)
        unit = unit_ref[rows, :]
        dfirst = norm_back(grad, unit, inv_ref[rows, 0:1], gain)
        dfirst_ref[rows, :] = dfirst
        dmerged = dfirst.astype(low)
        dmerged_ref[rows, :] = dmerged
        gain_sum += jnp.sum(grad * unit, axis=0, keepdims=True)
        shift_sum += jnp.sum(grad, axis=0, keepdims=True)
        bias_sum += jnp.sum(dmerged.astype(wide), axis=0, keepdims=True)
    for j in range(groups):
        merge_map = maps_ref[j - 1] if j else own_map[...]
        dctx_refs[j][...] = dot_nt(dmerged_ref[...], merge_map).astype(low)
    sums_ref[...] = jnp.zeros(sums_ref.shape, wide)
    sums_ref[3:4, :] = bias_sum
    sums_ref[4:5, :] = gain_sum
    sums_ref[5:6, :] = shift_sum


def first_back(dsum, near, core, across, unit, inverse, small, own_map, maps, waits):
    rows, model = dsum.shape
    groups, width = maps.shape[0] + 1, own_map.shape[0]
    found = kernel_call(
        functools.partial(first_back_kernel, groups),
        "first_back",
        [dsum, near, core, across, unit, inverse, small, own_map, maps],
        [((rows, model), wide, hbm), ((rows, model), low), ((8, model), wide, hbm)]
        + [((rows, width), low)] * groups,
        waits=waits,
        far_in=[0, 4, 5, 6, 7, 8],
    )
    return found[0], found[1], found[2], found[3:]


def forward_kernel(a_ref, b_ref, inner_ref, outer_ref, bias_ref, act_ref, slope_ref, own_ref, other_ref):
    rows = a_ref.shape[0]
    for ref, out, at in ((a_ref, own_ref, 0), (b_ref, other_ref, rows)):
        pre = dot_nt(ref[...], inner_ref[...]) + bias_ref[...]
        upper = 0.5 + 0.5 * lax.erf(pre * 0.7071067811865476)
        active = (pre * upper).astype(low)
        slope = upper + pre * (0.3989422804014327 * jnp.exp(-0.5 * pre * pre))
        act_ref[at : at + rows, :] = active
        slope_ref[at : at + rows, :] = slope.astype(low)
        out[...] = dot(active, outer_ref[...]).astype(low)


def feed_forward(a, b, inner, outer, bias, waits=()):
    rows, model = a.shape
    hidden = inner.shape[0]
    return kernel_call(
        forward_kernel,
        "feed_forward",
        [a, b, inner, outer, bias],
        [((2 * rows, hidden), low, hbm)] * 2 + [((rows, model), low)] * 2,
        waits=waits,
        far_in=[0, 1],
    )


def backward_kernel(a_ref, b_ref, inner_ref, outer_ref, slope_ref, dinner_ref, own_ref, other_ref):
    rows = a_ref.shape[0]
    for ref, out, at in ((a_ref, own_ref, 0), (b_ref, other_ref, rows)):
        dactive = dot_nt(ref[...], outer_ref[...])
        dinner = (dactive * slope_ref[at : at + rows, :].astype(wide)).astype(low)
        dinner_ref[at : at + rows, :] = dinner
        out[...] = dot(dinner, inner_ref[...]).astype(low)


def feed_backward(a, b, inner, outer, slope, waits=()):
    rows, model = a.shape
    hidden = inner.shape[0]
    return kernel_call(
        backward_kernel,
        "feed_backward",
        [a, b, inner, outer, slope],
        [((2 * rows, hidden), low, hbm)] + [((rows, model), low)] * 2,
        waits=waits,
        far_in=[4],
    )


def grad_kernel(numbers, block, bias, split, *refs):
    hid, row_refs, refs = refs[:2], refs[2:6], refs[6:]
    got_ref, out_refs = (refs[0], refs[1:]) if split else (None, refs)
    model = out_refs[0].shape[-1]
    half = len(numbers) // len(out_refs)
    for k, number in enumerate(numbers):
        cols = slice(number * block, (number + 1) * block)
        total = sums = 0.0
        for i, ref in enumerate(hid):
            rows = ref.shape[0] // 2
            total += dot_tn(ref[:rows, cols], row_refs[2 * i][...])
            total += dot_tn(ref[rows:, cols], row_refs[2 * i + 1][...])
            if bias:
                sums += jnp.sum(ref[:, cols].astype(wide), axis=0, keepdims=True)
        out_ref, at = out_refs[k // half], k % half
        if split:
            total += got_ref[k, :block, :].astype(wide)
        out_ref[at, :block, :] = total.astype(low)
        if bias:
            sums = jnp.pad(sums, ((0, 15), (0, model - block)))
            if split:
                sums += got_ref[k, block:, :].astype(wide)
            out_ref[at, block:, :] = sums.astype(low)


def weight_grad(hid, row_list, block, numbers, bias, waits, got=None):
    model = row_list[0].shape[1]
    split = got is not None
    count = len(numbers) // (1 + split)
    found = kernel_call(
        functools.partial(grad_kernel, numbers, block, bias, split),
        "weight_grad",
        [*hid, *row_list] + [got] * split,
        [((count, block + 16 * bias, model), low)] * (1 + split),
        waits=waits,
    )
    return found if split else found[0]


def units_kernel(units, shares, slot, inner_ref, outer_ref, bias_ref, own_inner, own_outer, own_bias):
    for m in range(shares):
        at = pl.multiple_of((slot[0] ^ (m << 1)) * units, units)
        own_inner[m] = inner_ref[:, pl.ds(at, units)].T
        own_outer[m] = outer_ref[pl.ds(at, units), :]
        own_bias[m] = jnp.broadcast_to(bias_ref[:, pl.ds(at, units)], (16, units))


def own_units(slot, shares, innermap, outermap, innerbias, waits):
    model = innermap.shape[0]
    units = innermap.shape[1] // (2 * shares)
    if units % 128:
        found = []
        for m in range(shares):
            at = (slot[0] ^ (m << 1)) * units
            inner = lax.dynamic_slice_in_dim(innermap, at, units, 1).T
            outer = lax.dynamic_slice_in_dim(outermap, at, units, 0)
            bias = lax.dynamic_slice_in_dim(innerbias, at, units, 1)
            found.append((inner, outer, jnp.broadcast_to(bias, (16, units))))
        return [jnp.stack(pieces) for pieces in zip(*found)]
    return kernel_call(
        functools.partial(units_kernel, units, shares),
        "own_units",
        [innermap, outermap, innerbias],
        [((shares, units, model), low, hbm)] * 2 + [((shares, 16, units), innerbias.dtype, hbm)],
        scalars=[slot],
        waits=waits,
        far_in=[0, 1],
    )


def pack_kernel(own_inner, own_outer, own_bias, pack_ref):
    units = own_inner.shape[1]
    pack_ref[:units, :] = own_inner[0]
    pack_ref[units : 2 * units, :] = own_outer[0]
    pack_ref[2 * units :, :] = jnp.zeros((16, pack_ref.shape[1]), low)
    pack_ref[2 * units :, :units] = own_bias[0]


def pack_units(own, waits):
    _, units, model = own[0].shape
    return kernel_call(
        pack_kernel, "pack_units", own, [((2 * units + 16, model), low)], waits=waits, far_in=hbm
    )[0]


def split_kernel(units, pack_ref, inner_ref, outer_ref):
    inner_ref[0, :units, :] = pack_ref[:units, :]
    inner_ref[0, units:, :] = pack_ref[2 * units :, :]
    outer_ref[0] = pack_ref[units : 2 * units, :]


def split_units(units, pack, waits):
    model = pack.shape[1]
    return kernel_call(
        functools.partial(split_kernel, units),
        "split_units",
        [pack],
        [((1, units + 16, model), low), ((1, units, model), low)],
        waits=waits,
    )


def stack_kernel(*refs):
    count = len(refs) // 3
    for k in range(count):
        a_ref, b_ref, out_ref = refs[2 * k], refs[2 * k + 1], refs[2 * count + k]
        out_ref[: a_ref.shape[0]] = a_ref[...]
        out_ref[a_ref.shape[0] :] = b_ref[...]


def stack_pairs(pairs):
    return kernel_call(
        stack_kernel,
        "stack_pairs",
        [value for pair in pairs for value in pair],
        [((2 * a.shape[0], *a.shape[1:]), a.dtype) for a, _ in pairs],
    )


def join_kernel(units, masks, own_inner, own_outer, own_bias, *refs):
    parts, (inner_ref, outer_ref, bias_ref) = refs[:-3], refs[-3:]
    for m in range(own_inner.shape[0]):
        at, far = 2 * m * units, (2 * m + 1) * units
        inner_ref[at:far, :] = own_inner[m]
        outer_ref[at:far, :] = own_outer[m]
        bias_ref[:, at:far] = own_bias[m, 0:1, :].astype(wide)
    for which, (ref, order) in enumerate(zip(parts, masks)):
        for k, m in enumerate(order):
            far = (2 * m + 1) * units
            if which < 2:
                inner_ref[far : far + units, :] = ref[k, :units, :]
                bias_ref[:, far : far + units] = ref[k, units : units + 16, :units].astype(wide)[:1]
            else:
                outer_ref[far : far + units, :] = ref[k]


def join_units(own, parts, masks, waits):
    shares, units, model = own[0].shape
    hidden = 2 * shares * units
    return kernel_call(
        functools.partial(join_kernel, units, masks),
        "join_units",
        [*own, *parts],
        [((hidden, model), low)] * 2 + [((1, hidden), wide)],
        waits=waits,
        far_in=hbm,
    )


def slot_order(number, bits):
    return ((number & 1) << (bits - 1)) | (number >> 1)


def qkv_kernel(counts, slots, slot, *refs):
    out_ref, q_all, kv_all = refs[-3:]
    dq_ref, refs = refs[0], refs[1:-3]
    width, model = dq_ref.shape[-1], out_ref.shape[-1]
    q_all[...] = dq_ref[...].reshape(q_all.shape)
    q_sum = jnp.sum(q_all[...].astype(wide), axis=0, keepdims=True)
    q_grad = kv_grad = kv_sum = 0.0
    for i, count in enumerate(counts):
        dkv_ref, tok_refs, refs = refs[0], refs[1 : 1 + count], refs[1 + count :]
        kv_all[...] = dkv_ref[...].reshape(kv_all.shape)
        kv_sum += jnp.sum(kv_all[...].astype(wide), axis=0, keepdims=True)
        at = 0
        for tok_ref in tok_refs:
            there = slice(at, at + tok_ref.shape[0])
            at += tok_ref.shape[0]
            kv_grad += dot_tn(kv_all[there, :], tok_ref[...])
            if i == 0:
                q_grad += dot_tn(q_all[there, :], tok_ref[...])
    grad = jnp.concatenate([q_grad, kv_grad]).astype(low)
    sums = jnp.concatenate([q_sum, kv_sum], axis=1)
    bits = slots.bit_length() - 1
    block = 3 * width // slots
    for b in range(slots):
        at = slot_order(slot[0] ^ b, bits)
        out_ref[at, :block, :] = grad[b * block : (b + 1) * block]
        line = jnp.pad(sums[:, b * block : (b + 1) * block], ((0, 15), (0, model - block)))
        out_ref[at, pad16(block) :, :] = line.astype(low)


def qkv_grads(slot, slots, dq, pairs, waits):
    model = pairs[0][1][0].shape[-1]
    groups, width = dq.shape[0], dq.shape[-1]
    total = dq.size // width
    far_at, at = [], 1
    for dkv, tok in pairs:
        far_at += range(at + 1, at + 1 + len(tok))
        at += 1 + len(tok)
    return kernel_call(
        functools.partial(qkv_kernel, [len(tok) for _, tok in pairs], slots),
        "qkv_grads",
        [dq] + [a for dkv, tok in pairs for a in (dkv, *tok)],
        [((slots, pad16(3 * width // slots) + 16, model), low)],
        far_in=far_at,
        scalars=[slot],
        waits=waits,
        scratch=[pltpu.VMEM((total, width), low), pltpu.VMEM((total, 2 * width), low)],
        mebibytes=24,
    )[0]


def hold_kernel(value_ref, out_ref):
    out_ref[...] = value_ref[...]


def hold(value, waits):
    out = [(value.shape, value.dtype)]
    return kernel_call(hold_kernel, "hold", [value], out, waits=waits)[0]


def add_kernel(a_ref, b_ref, *out_refs):
    at = 0
    for ref in out_refs:
        there = slice(at, at + ref.shape[0])
        at += ref.shape[0]
        ref[...] = (a_ref[there].astype(wide) + b_ref[there].astype(wide)).astype(ref.dtype)


def add_split(a, b, counts, waits=(), kind=low):
    out = [((count, *a.shape[1:]), kind) for count in counts]
    return kernel_call(add_kernel, "add_split", [a, b], out, waits=waits)


def dtokens_kernel(dq_ref, own_ref, got_ref, q_ref, k_ref, v_ref, *out_refs):
    width = dq_ref.shape[-1]
    rows = dq_ref.shape[1] * dq_ref.shape[2]
    for j, ref in enumerate(out_refs):
        dkv = (own_ref[j].astype(wide) + got_ref[j].astype(wide)).astype(low)
        dkv = dkv.reshape(rows, 2 * width)
        total = dot_nt(dq_ref[j].reshape(rows, width), q_ref[...])
        total += dot_nt(dkv[:, :width], k_ref[...]) + dot_nt(dkv[:, width:], v_ref[...])
        ref[...] = total.astype(ref.dtype)


def dtokens(dq, own, got, maps, waits):
    rows, model = dq.shape[1] * dq.shape[2], maps[0].shape[0]
    return kernel_call(
        dtokens_kernel,
        "dtokens",
        [dq, own, got, *maps],
        [((rows, model), wide), ((rows, model), low)] * (dq.shape[0] // 2),
        waits=waits,
    )


def tokens_kernel(dfirst_ref, part_ref, near_ref, far_ref, out_ref):
    total = dfirst_ref[...] + part_ref[...] + near_ref[...].astype(wide)
    out_ref[...] = (total + far_ref[...].astype(wide)).astype(low)


def pack_sums_kernel(units, inner_ref, inner_got, outer_ref, outer_got, own_ref, send_ref):
    model = own_ref.shape[1]
    inner = inner_ref[0].astype(wide) + inner_got[0].astype(wide)
    outer = outer_ref[0].astype(wide) + outer_got[0].astype(wide)
    sums = inner[2 * units :, : 2 * units].astype(low)
    for k, ref in enumerate((own_ref, send_ref)):
        there = slice(k * units, (k + 1) * units)
        ref[:units, :] = inner[there].astype(low)
        ref[units : 2 * units, :] = outer[there].astype(low)
        ref[2 * units :, :] = jnp.zeros((16, model), low)
        ref[2 * units :, :units] = sums[:, there]


def pack_sums(units, inner, inner_got, outer, outer_got, waits):
    model = inner.shape[-1]
    return kernel_call(
        functools.partial(pack_sums_kernel, units),
        "pack_sums",
        [inner, inner_got, outer, outer_got],
        [((2 * units + 16, model), low)] * 2,
        waits=waits,
    )


def merge_grad_kernel(groups, core, *refs):
    ctx_refs, (dmerged_ref, a_ref, b_ref, keep_ref, send_ref, grad_all) = refs[:groups], refs[groups:]
    half = keep_ref.shape[1]
    for j, ref in enumerate(ctx_refs):
        grad_all[...] = dot_tn(ref[...], dmerged_ref[...]).astype(low)
        keep = pl.multiple_of(core[0] * half, half)
        send = pl.multiple_of((1 - core[0]) * half, half)
        keep_ref[j] = grad_all[pl.ds(keep, half), :]
        send_ref[j * half : (j + 1) * half, :] = grad_all[pl.ds(send, half), :]
    sums = a_ref[...] + b_ref[...]
    send_ref[groups * half :, :] = jnp.concatenate([sums, jnp.zeros_like(sums)]).astype(low)


def merge_grads(core, ctx, dmerged, a, b):
    rows, width = ctx[0].shape
    model = dmerged.shape[1]
    groups, half = len(ctx), width // 2
    return kernel_call(
        functools.partial(merge_grad_kernel, groups),
        "merge_grads",
        [*ctx, dmerged, a, b],
        [((groups, half, model), low), ((groups * half + 16, model), low)],
        far_in=[i for i in range(groups + 3) if i != groups],
        scalars=[core],
        scratch=[pltpu.VMEM((width, model), low)],
    )


def merge_heads_kernel(groups, a_ref, b_ref, keep_ref, got_ref, near_ref, send_ref, sums_ref):
    half = keep_ref.shape[1]
    total = lambda j: keep_ref[j].astype(wide) + got_ref[j * half : (j + 1) * half, :].astype(wide)
    for k in range(groups // 2):
        near_ref[k] = total(2 * k).astype(low)
        send_ref[k * half : (k + 1) * half, :] = total(2 * k + 1).astype(low)
    sums = a_ref[...] + b_ref[...] + got_ref[groups * half : groups * half + 16, :].astype(wide)[:8]
    sums_ref[...] = sums
    at = groups // 2 * half
    send_ref[at:, :] = jnp.concatenate([sums, jnp.zeros_like(sums)]).astype(low)


def merge_heads(a, b, keep, got):
    groups, half, model = keep.shape
    count = groups // 2
    return kernel_call(
        functools.partial(merge_heads_kernel, groups),
        "merge_heads",
        [a, b, keep, got],
        [((count, half, model), low), ((count * half + 16, model), low), ((8, model), wide)],
    )


def merge_far_kernel(keep_ref, got_ref, sums_ref, near_ref, send_ref, out_sums_ref):
    half = keep_ref.shape[1]
    near_ref[...] = (keep_ref[0].astype(wide) + got_ref[:half, :].astype(wide)).astype(low)
    far = keep_ref[1].astype(wide) + got_ref[half : 2 * half, :].astype(wide)
    send_ref[:half, :] = far.astype(low)
    sums = sums_ref[...] + got_ref[2 * half :, :].astype(wide)[:8]
    out_sums_ref[...] = sums
    send_ref[half:, :] = jnp.concatenate([sums, jnp.zeros_like(sums)]).astype(low)


def merge_far(keep, got, sums, waits):
    _, half, model = keep.shape
    return kernel_call(
        merge_far_kernel,
        "merge_far",
        [keep, got, sums],
        [((half, model), low), ((half + 16, model), low), ((8, model), wide)],
        waits=waits,
    )


def slots_kernel(block, size, slot, grad_ref, core_ref, near_ref, far_ref, sums_ref, *refs):
    own_ref, send_refs, (out_sums_ref, rows_all) = refs[0], refs[1:-2], refs[-2:]
    shares = len(send_refs) + 1
    half = near_ref.shape[0]
    merged = (near_ref[...].astype(wide) + far_ref[:half, :].astype(wide)).astype(low)
    for k in range(shares):
        rows_all[k] = merged[k * size : (k + 1) * size]
    sums = sums_ref[...] + far_ref[half:, :].astype(wide)[:8]
    out_sums_ref[...] = sums
    start = pad16(block) + 16
    for m, ref in enumerate((own_ref, *send_refs)):
        ref[:start, :] = (grad_ref[m].astype(wide) + core_ref[m].astype(wide)).astype(low)
        ref[start : start + size, :] = rows_all[(slot[0] >> 1) ^ m]
        if m:
            both = jnp.concatenate([sums, jnp.zeros_like(sums)]).astype(low)
            ref[start + pad16(size) :, :] = both


def slot_parts(slot, block, size, grads, core, near, far, sums, waits):
    shares, _, model = core.shape
    rows = pad16(block) + 16 + pad16(size)
    return kernel_call(
        functools.partial(slots_kernel, block, size),
        "slot_parts",
        [grads, core, near, far, sums],
        [((rows, model), low)]
        + [((rows + 16, model), low)] * (shares - 1)
        + [((8, model), wide)],
        scalars=[slot],
        scratch=[pltpu.VMEM((shares, size, model), low)],
        waits=waits,
    )


def slot_sum_kernel(own_ref, sums_ref, *refs):
    got_refs, (out_ref, out_sums_ref) = refs[:-2], refs[-2:]
    rows = own_ref.shape[0]
    total, sums = own_ref[...].astype(wide), sums_ref[...]
    for ref in got_refs:
        total += ref[:rows, :].astype(wide)
        sums += ref[rows:, :].astype(wide)[:8]
    out_ref[...] = total.astype(low)
    out_sums_ref[...] = sums


def slot_sum(own, sums, got, waits):
    return kernel_call(
        slot_sum_kernel,
        "slot_sum",
        [own, sums, *got],
        [(own.shape, low), (sums.shape, wide)],
        waits=waits,
    )


def feed_out_kernel(units, grads_ref, inner_ref, outer_ref, bias_ref, here, inner, outer, bias, sems):
    slots, rows, model = grads_ref.shape
    copies = [pltpu.make_async_copy(grads_ref.at[k], here.at[k], sems.at[0, k]) for k in range(slots)]
    for copy in copies:
        copy.start()
    done = []
    for k, copy in enumerate(copies):
        copy.wait()
        cols = slice(k * units, (k + 1) * units)
        inner[:, cols] = here[k, :units, :].astype(wide).T
        outer[cols, :] = here[k, units : 2 * units, :].astype(wide)
        bias[k : k + 1, :] = here[k, 2 * units : 2 * units + 16, :units].astype(wide)[:1]
        done.append(pltpu.make_async_copy(inner.at[:, cols], inner_ref.at[:, cols], sems.at[1, k]))
        done.append(pltpu.make_async_copy(outer.at[cols, :], outer_ref.at[cols, :], sems.at[2, k]))
        done[-2].start()
        done[-1].start()
    done.append(pltpu.make_async_copy(bias, bias_ref, sems.at[0, 0]))
    done[-1].start()
    for copy in done:
        copy.wait()


def feed_out(grads, units):
    slots, rows, model = grads.shape
    hidden = slots * units
    if units % 128:
        inner = grads[:, :units].reshape(hidden, model).astype(wide).T
        outer = grads[:, units : 2 * units].reshape(hidden, model).astype(wide)
        return inner, outer, grads[:, 2 * units, :units].astype(wide)
    shapes = [(model, hidden), (hidden, model), (slots, units)]
    return pl.pallas_call(
        functools.partial(feed_out_kernel, units),
        in_specs=[in_hbm],
        out_specs=[in_hbm] * 3,
        out_shape=[jax.ShapeDtypeStruct(shape, wide) for shape in shapes],
        scratch_shapes=[pltpu.VMEM(grads.shape, low)]
        + [pltpu.VMEM(shape, wide) for shape in shapes]
        + [pltpu.SemaphoreType.DMA((3, slots))],
        compiler_params=params(60),
        name="feed_out",
    )(grads)


def qkv_out_kernel(block, order, slot, *refs):
    parts, refs = refs[: len(order)], refs[len(order) :]
    q_ref, k_ref, v_ref, merge_ref, bias_ref, rows_all, merge_all = refs
    start, size = pad16(block), merge_all.shape[1]
    width = q_ref.shape[1]
    slots = merge_all.shape[0]
    for mask, part in zip(order, parts):
        at = slot[0] ^ mask
        rows_all[at] = part[:block, :]
        bias_ref[pl.ds(at, 1), :] = part[start : start + 16, :].astype(wide)[:1]
        at = (at & 1) * (slots // 2) + (at >> 1)
        merge_all[at] = part[start + 16 : start + 16 + size, :]
    grad = rows_all[...].reshape(3 * width, -1)
    for i, ref in enumerate((q_ref, k_ref, v_ref)):
        ref[...] = grad[i * width : (i + 1) * width].astype(wide).T
    merge_ref[...] = merge_all[...].reshape(merge_ref.shape).astype(wide)


def qkv_out(slot, parts, order, block, width):
    model = parts[0].shape[-1]
    slots = 3 * width // block
    size = width // slots
    return kernel_call(
        functools.partial(qkv_out_kernel, block, order),
        "qkv_out",
        parts,
        [((model, width), wide)] * 3 + [((width, model), wide), ((slots, model), wide)],
        scalars=[slot],
        scratch=[pltpu.VMEM((slots, block, model), low), pltpu.VMEM((slots, size, model), low)],
    )


def shards(
    tokens,
    querymap,
    querybias,
    keymap,
    valuemap,
    valuebias,
    mergemap,
    mergebias,
    normgain,
    normshift,
    innermap,
    innerbias,
    outermap,
    outerbias,
    finalgain,
    finalshift,
    lengths,
    cotangent,
):
    proteins, share, model = tokens.shape
    groups = lax.axis_size("heads")
    rows = proteins * share
    width = querymap.shape[1]
    seq, heads = lax.axis_index("seq"), lax.axis_index("heads")
    seq_size, dp_size = lax.axis_size("seq"), lax.axis_size("dp")
    pos = jnp.concatenate([lengths, jnp.stack([seq, heads]).astype(jnp.int32)])
    core_bit, row_bit, far_bit = ("seq", 1), ("heads", 1), ("heads", 2)
    seq_bits = [("seq", 1 << k) for k in range(1, seq_size.bit_length() - 1)]
    share_bits = seq_bits + [("dp", 1 << k) for k in range(dp_size.bit_length() - 1)]
    slot_bits = [core_bit] + share_bits
    slots = 1 << len(slot_bits)
    shares = slots // 2
    slot = lax.axis_index("dp") * seq_size + seq
    units = innermap.shape[1] // slots
    merge_units = width // slots
    row = lambda vector: vector.reshape(1, -1)

    slot_scalar = slot.reshape(1).astype(jnp.int32)

    own_rows = tokens.reshape(rows, model)
    small = jnp.stack([mergebias, normgain, normshift, outerbias, finalgain, finalshift])
    small = jnp.pad(small.astype(wide), ((0, 2), (0, 0)))
    second = swap(own_rows, *far_bit)
    first = swap(own_rows, *row_bit)
    maps = [querymap, keymap, valuemap]
    biases = [row(querybias), row(valuebias)]
    merge_own = lax.dynamic_slice_in_dim(mergemap, slot * merge_units, merge_units, 0)
    merge_all = lax.all_gather(merge_own, ("dp", "seq", "heads"))
    merge_all = merge_all.reshape(slots, groups, merge_units, model)
    own = own_units(slot_scalar, shares, innermap, outermap, row(innerbias), [small])

    def exchange_keys(piece):
        found = {0: piece}
        for axis, stride in seq_bits + [core_bit]:
            for i in list(found):
                found[i | stride] = swap(found[i], axis, stride)
        return found

    maps_biases = [*maps, *biases]
    seq_tokens = {i: [] for i in range(0, seq_size, 2)}

    def exchange_tokens(piece):
        found = {0: piece}
        for axis, stride in seq_bits:
            for i in list(found):
                found[i | stride] = swap(found[i], axis, stride)
        for i in found:
            seq_tokens[i].append(found[i])
        return [found[i] for i in found if i]

    far_tokens = [exchange_tokens(own_rows)]
    far_units = swap(pack_units(own, []), *far_bit)
    second_held = hold(second, [first, own[0], *far_tokens[0]])
    third = swap(second_held, *row_bit)
    q_three, kv_three = project([own_rows, first, second_held], maps_biases, proteins)
    kv_three = exchange_keys(kv_three)
    q_last, kv_last = project([third], maps_biases, proteins, [q_three])
    kv_last = exchange_keys(kv_last)
    queries = [q_three, q_last]
    kv_pieces = [stack[i] for i in range(seq_size) for stack in (kv_three, kv_last)]
    token_pieces = [own_rows, first, second, third]
    pairs = split_units(units, far_units, [q_last])
    order = list(range(len(share_bits)))
    masks = [[0], [0]]
    for k, bits in enumerate(zip(order, order[::-1])):
        if k:
            pairs = stack_pairs(pairs)
        pairs = [(p, swap(p, *share_bits[bit])) for p, bit in zip(pairs, bits)]
        masks = [(have, [m | (1 << bit) for m in have]) for have, bit in zip(masks, bits)]
        if k < len(order) - 1:
            masks = [a + b for a, b in masks]
    far_tokens += [exchange_tokens(piece) for piece in token_pieces[1:]]

    stacked = [p for pair in pairs for p in pair[:1]]
    context, context_t, logsum = attend(pos, queries, kv_pieces, stacked)
    context = [c.reshape(rows, width) for c in context]
    context = [context[0]] + [swap(context[j], "heads", j) for j in range(1, groups)]
    normed, normed_low, first_unit, first_inverse, other_maps = merge_norm(
        heads.reshape(1).astype(jnp.int32),
        context,
        mergemap,
        merge_all,
        own_rows,
        small,
        [],
    )
    inner_t, outer_w, inner_b = join_units(
        own, [p for pair in pairs for p in pair], [m for pair in masks for m in pair], [normed_low]
    )

    normed_near, normed_across = swap(normed_low, *core_bit), swap(normed_low, *row_bit)
    near_act, near_slope, near_own, near_other = feed_forward(
        normed_low, normed_near, inner_t, outer_w, inner_b
    )
    normed_across = hold(normed_across, [near_act, *far_tokens[1]])
    normed_both = swap(normed_across, *core_bit)
    normed_rows = [normed_low, normed_near, normed_across, normed_both]
    far_act, far_slope, far_own, far_other = feed_forward(
        normed_across, normed_both, inner_t, outer_w, inner_b, [near_act]
    )
    (far_part,) = add_split(far_own, swap(far_other, *core_bit), [rows])
    far_sum = swap(far_part, *row_bit)
    own_at = (seq * groups + heads) * share + jnp.arange(share, dtype=jnp.int32)
    live = (own_at[None, :] < lengths[:, None]).astype(wide).reshape(rows, 1)
    layer_output, dsum_final, dbranch, final_sums = final_norm(
        normed,
        near_own,
        swap(near_other, *core_bit),
        far_sum,
        small,
        cotangent.reshape(rows, model),
        jnp.broadcast_to(live, (rows, 128)),
        far_tokens[2],
    )
    dbranch_near, dbranch_across = swap(dbranch, *core_bit), swap(dbranch, *row_bit)
    near_dinner, near_own, near_other = feed_backward(
        dbranch, dbranch_near, inner_t, outer_w, near_slope
    )
    dbranch_across = hold(dbranch_across, [near_dinner, *far_tokens[3]])
    dbranch_both = swap(dbranch_across, *core_bit)
    dbranch_rows = [dbranch, dbranch_near, dbranch_across, dbranch_both]
    hid_block = 2 * units
    last = len(share_bits) - 1
    numbers = lambda k, side: [m for m in range(shares) if (m >> k) & 1 == side]
    acts = [near_act, far_act]
    outer_send = weight_grad(acts, dbranch_rows, hid_block, numbers(last, 1), 0, [near_dinner])
    outer_got = swap(outer_send, *share_bits[last])
    far_dinner, far_own, far_other = feed_backward(
        dbranch_across,
        dbranch_both,
        inner_t,
        outer_w,
        far_slope,
        [outer_send, near_dinner],
    )
    (far_part,) = add_split(far_own, swap(far_other, *core_bit), [rows])
    far_sum = swap(far_part, *row_bit)

    dinners = [near_dinner, far_dinner]
    inner_send = weight_grad(dinners, normed_rows, hid_block, numbers(0, 1), 1, [far_part])
    inner_got = swap(inner_send, *share_bits[0])
    dfirst, dmerged, first_sums, dcontext = first_back(
        dsum_final,
        near_own,
        swap(near_other, *core_bit),
        far_sum,
        first_unit,
        first_inverse,
        small,
        mergemap,
        other_maps,
        [inner_send],
    )
    dcontext = [dcontext[0]] + [swap(dcontext[j], "heads", j) for j in range(1, groups)]
    dcontext = [d.reshape(proteins, share, width) for d in dcontext]
    core = bit_of(core_bit).reshape(1).astype(jnp.int32)
    merge_keep, merge_send = merge_grads(core, context, dmerged, final_sums, first_sums)
    merge_keep, merge_send, sums = merge_heads(
        final_sums, first_sums, merge_keep, swap(merge_send, *core_bit)
    )
    merge_got = swap(merge_send, *row_bit)
    merge_near, merge_send, sums = merge_far(merge_keep, merge_got, sums, [])
    merge_got = swap(merge_send, *far_bit)

    def shared_sum(hid, row_list, got, k, bias, waits):
        bits = [b for i, b in enumerate(share_bits) if i != k]
        if not bits:
            (keep,) = weight_grad(hid, row_list, hid_block, numbers(k, 0), bias, waits)
            return keep, got
        keep, send = weight_grad(hid, row_list, hid_block, numbers(k, 0), bias, waits, got)
        got = swap(send, *bits[-1])
        for bit in reversed(bits[:-1]):
            half = keep.shape[0] // 2
            keep, send = add_split(keep, got, [half, half])
            got = swap(send, *bit)
        return keep, got

    outer_sums = shared_sum(acts, dbranch_rows, outer_got, last, 0, [merge_send])
    inner_sums = shared_sum(dinners, normed_rows, inner_got, 0, 1, [merge_send])

    dqueries, dkv_by_seq = attend_back(
        pos, queries, dcontext, context_t, logsum, kv_pieces, [outer_sums[0], inner_sums[0], merge_send]
    )
    half = groups // 2
    dkv_by_seq = list(dkv_by_seq)
    dkv_by_seq[1::2] = gate(dkv_by_seq[1::2], [inner_sums[1], outer_sums[1], merge_got])
    own_pack, send_pack = pack_sums(units, *inner_sums, *outer_sums, [dqueries])
    far_pack = swap(send_pack, *far_bit)
    dkv_parts = [
        add_split(dkv_by_seq[i], swap(dkv_by_seq[i + 1], *core_bit), [groups])[0]
        for i in range(0, seq_size, 2)
    ]
    pairs = list(zip(dkv_parts, [seq_tokens[i] for i in range(0, seq_size, 2)]))
    slot_grads = qkv_grads(slot_scalar, slots, dqueries, pairs, [send_pack])
    block = 3 * width // slots
    slot_send = slot_parts(
        slot_scalar,
        block,
        merge_units,
        slot_grads,
        swap(slot_grads[shares:], *core_bit),
        merge_near,
        merge_got,
        sums,
        [],
    )
    slot_got = [swap_slots(slot_send[m], m << 1) for m in range(1, shares)]
    parts = dkv_parts
    for k in reversed(range(len(seq_bits))):
        count = 1 << k
        got = [swap(parts[count + i], *seq_bits[k]) for i in range(count)]
        if k:
            parts = [add_split(parts[i], got[i], [groups])[0] for i in range(count)]

    got[:1] = gate(got[:1], slot_got)

    part_none, part_one, part_two, part_three = dtokens(
        dqueries, parts[0], got[0], maps, [slot_send[0]]
    )
    rest = swap(part_three, *row_bit)
    near = swap(part_one, *row_bit)
    out_pack, extra = slot_sum(slot_send[0], slot_send[-1], slot_got, [part_three])
    (far_send,) = add_split(part_two, rest, [rows], [out_pack])
    far = swap(far_send, *far_bit)

    (pack,) = add_split(own_pack, far_pack, [own_pack.shape[0]], [part_three])
    grads = lax.all_gather(pack, ("dp", "seq"))

    parts = [out_pack] + [swap_slots(out_pack, m << 1) for m in range(1, shares)]
    order = [m << 1 for m in range(shares)]
    q_grad, k_grad, v_grad, mergemap_grad, bias_rows = qkv_out(
        slot_scalar,
        parts + [swap(part, *core_bit) for part in parts],
        order + [m | 1 for m in order],
        block,
        width,
    )
    tokens_grad = kernel_call(
        tokens_kernel, "tokens_grad", [dfirst, part_none, near, far], [((rows, model), low)]
    )[0]
    innermap_grad, outermap_grad, innerbias_grad = feed_out(grads, units)
    innerbias_grad = innerbias_grad.reshape(-1)
    bias_grads = bias_rows[:, :block].reshape(-1)
    shape = tokens.shape
    return (
        layer_output.reshape(shape),
        tokens_grad.reshape(shape),
        q_grad,
        bias_grads[:width],
        k_grad,
        v_grad,
        bias_grads[2 * width :],
        mergemap_grad,
        extra[3],
        extra[4],
        extra[5],
        innermap_grad,
        innerbias_grad,
        outermap_grad,
        extra[0],
        extra[1],
        extra[2],
    )


def solution(mesh):
    return jax.shard_map(
        shards,
        mesh=mesh,
        in_specs=(
            P("dp", ("seq", "heads"), None),
            P(None, "heads"),
            P("heads"),
            P(None, "heads"),
            P(None, "heads"),
            P("heads"),
            P("heads", None),
            P(),
            P(),
            P(),
            P(None, "heads"),
            P("heads"),
            P("heads", None),
            P(),
            P(),
            P(),
            P("dp"),
            P("dp", ("seq", "heads"), None),
        ),
        out_specs=(
            P("dp", ("seq", "heads"), None),
            P("dp", ("seq", "heads"), None),
            P(None, "heads"),
            P("heads"),
            P(None, "heads"),
            P(None, "heads"),
            P("heads"),
            P("heads", None),
            P(),
            P(),
            P(),
            P(None, "heads"),
            P("heads"),
            P("heads", None),
            P(),
            P(),
            P(),
        ),
        check_vma=False,
    )
```

```python
import functools

import jax
import jax.numpy as jnp
from jax import lax
from jax.experimental import pallas as pl
from jax.experimental.pallas import tpu as pltpu
from jax.sharding import PartitionSpec as P

HEAD_DIM = 64


epsilon = 1e-06
score_scale = 0.125
masked_score = -1000000000.0
low = jnp.bfloat16
wide = jnp.float32
vmem_bytes = 48 * 1024 * 1024


def dot(a, b):
    return jnp.dot(a, b, preferred_element_type=wide)


def dot_nt(a, b):
    return lax.dot_general(a, b, (((1,), (1,)), ((), ())), preferred_element_type=wide)


def dot_tn(a, b):
    return lax.dot_general(a, b, (((0,), (0,)), ((), ())), preferred_element_type=wide)


def swap(value, axis, stride):
    size = lax.axis_size(axis)
    return lax.ppermute(value, axis, [(i, i ^ stride) for i in range(size)])


def swap_slots(value, mask):
    size = lax.axis_size("dp") * lax.axis_size("seq")
    return lax.ppermute(value, ("dp", "seq"), [(i, i ^ mask) for i in range(size)])


def bit_of(bit):
    axis, stride = bit
    return (lax.axis_index(axis) // stride) % 2


def add_low(a, b):
    return (a.astype(wide) + b.astype(wide)).astype(low)


def params(mebibytes):
    return pltpu.CompilerParams(vmem_limit_bytes=mebibytes * 1024 * 1024)


in_vmem = pl.BlockSpec(memory_space=pltpu.VMEM)
in_smem = pl.BlockSpec(memory_space=pltpu.SMEM)
anywhere = pl.BlockSpec(memory_space=pl.ANY)
in_hbm = pl.BlockSpec(memory_space=pltpu.HBM)
hbm = True
kernels_alone = ("attend", "attend_back", "merge_norm", "project", "join_units", "stack_pairs")


def kernel_call(
    body, name, arrays, out, scalars=(), scratch=(), mebibytes=16, waits=(), far_in=(), local=(), flops=1
):
    ns, na, nw, no, nl = len(scalars), len(arrays), len(waits), len(out), len(local)
    alone = name in kernels_alone
    far_in = [i for i in range(na) if alone and (far_in is hbm or i in far_in)]
    far_out = [i for i, o in enumerate(out) if alone and len(o) > 2 and o[2] is hbm]
    own_out = [i for i, o in enumerate(out) if len(o) > 2 and o[2] == "kernel"]
    buffers = [pltpu.VMEM(arrays[i].shape, arrays[i].dtype) for i in far_in]
    buffers += [pltpu.VMEM(out[i][0], out[i][1]) for i in far_out]
    count = len(buffers)

    def whole(*refs):
        here = list(refs[: ns + na])
        at = ns + na + nw
        kept, outs, rest = refs[at : at + nl], list(refs[at + nl : at + nl + no]), refs[at + nl + no :]
        rest, (*held_refs, sems) = (rest[: len(rest) - count - 1], rest[len(rest) - count - 1 :])
        copies = []
        for k, i in enumerate(far_in):
            copies.append(pltpu.make_async_copy(here[ns + i], held_refs[k], sems.at[k]))
            copies[-1].start()
            here[ns + i] = held_refs[k]
        for copy in copies:
            copy.wait()
        copies = []
        for k, i in enumerate(far_out, len(far_in)):
            copies.append(pltpu.make_async_copy(held_refs[k], outs[i], sems.at[k]))
            outs[i] = held_refs[k]
        body(*here, *kept, *outs, *rest)
        for copy in copies:
            copy.start()
        for copy in copies:
            copy.wait()

    return pl.pallas_call(
        whole,
        in_specs=[in_smem] * ns
        + [in_hbm if i in far_in else in_vmem for i in range(na)]
        + [anywhere] * nw
        + [in_hbm] * nl,
        out_specs=[in_hbm if i in far_out + own_out else in_vmem for i in range(no)],
        out_shape=[jax.ShapeDtypeStruct(o[0], o[1]) for o in out],
        scratch_shapes=list(scratch) + buffers + [pltpu.SemaphoreType.DMA((max(count, 1),))],
        compiler_params=params(60 if alone else mebibytes),
        cost_estimate=pl.CostEstimate(flops=flops, bytes_accessed=1, transcendentals=0),
        name=name,
    )(*scalars, *arrays, *waits, *local)


def nothing(*refs):
    pass


def gate(values, waits):
    values = [pltpu.with_memory_space_constraint(v, pltpu.HBM) for v in values]
    found = pl.pallas_call(
        nothing,
        in_specs=[anywhere] * (len(values) + len(waits)),
        out_specs=[anywhere] * len(values),
        out_shape=[jax.ShapeDtypeStruct(v.shape, v.dtype) for v in values],
        input_output_aliases={i: i for i in range(len(values))},
        compiler_params=params(1),
        name="gate",
    )(*values, *waits)
    return list(found)


def pad16(count):
    return -(-count // 16) * 16


def place(pos, proteins, groups, share, i, j):
    seq, heads = pos[proteins], pos[proteins + 1]
    return pl.multiple_of(((seq ^ i) * groups + (heads ^ j)) * share, share)


def masked(scores, length, first):
    key_at = first + lax.broadcasted_iota(jnp.int32, scores.shape, 0)
    return jnp.where(key_at < length, scores, masked_score)


def chunks(n, block):
    return [(0, n - block, False)] * (n > block) + [(n - block, n, True)]


def piece_list(refs, groups):
    found, count = [], 0
    for ref in refs:
        for n in range(ref.shape[0]):
            found.append((ref, count // groups, count % groups, n))
            count += 1
    return found


def start_keys(pos, p, proteins, groups, kv_refs, kv_all, sems, blocks, block, wait):
    share = kv_refs[0].shape[2]
    for k, (ref, i, j, n) in enumerate(piece_list(kv_refs, groups)):
        at = place(pos, proteins, groups, share, i, j)

        @pl.when(at < blocks * block)
        def _():
            copy = pltpu.make_async_copy(ref.at[n, p], kv_all.at[p, pl.ds(at, share), :], sems.at[p])
            if wait:
                copy.wait()
            else:
                copy.start()


def query_rows(refs, p):
    found = [ref[n, p] for ref in refs for n in range(ref.shape[0])]
    return jnp.concatenate(found) * jnp.asarray(score_scale, low)


def attend_kernel(counts, pos, *refs):
    stacks, arrays, groups = counts
    q_refs, kv_refs = refs[:stacks], refs[stacks : stacks + arrays]
    ctx_refs, (ctx_t_ref, lse_ref, kv_all, sems) = refs[stacks + arrays : -4], refs[-4:]
    _, proteins, share, width = q_refs[0].shape
    total = kv_all.shape[1]
    block = min(256, total)
    heads = range(width // HEAD_DIM)

    def keys_of(p, wait):
        blocks = (pos[p] + block - 1) // block
        start_keys(pos, p, proteins, groups, kv_refs, kv_all, sems, blocks, block, wait)
        return blocks

    for p in range(proteins):
        keys_of(p, False)

    def protein(p, carry):
        length = pos[p]
        blocks = keys_of(p, True)

        def body(count):
            n = count * block
            queries = query_rows(q_refs, p)
            cols = lambda h: slice(h * HEAD_DIM, (h + 1) * HEAD_DIM)
            value_cols = lambda h: slice(width + h * HEAD_DIM, width + (h + 1) * HEAD_DIM)
            cuts = chunks(n, block)
            scores = [
                [dot_nt(kv_all[p, a:b, cols(h)], queries[:, cols(h)]) for a, b, _ in cuts]
                for h in heads
            ]
            weights, denominators = [], []
            for h in heads:
                found = [
                    masked(value, length, a) if last else value
                    for value, (a, _, last) in zip(scores[h], cuts)
                ]
                high = functools.reduce(
                    jnp.maximum, [jnp.max(value, axis=0, keepdims=True) for value in found]
                )
                found = [jnp.exp(value - high) for value in found]
                denominator = sum(jnp.sum(value, axis=0, keepdims=True) for value in found)
                lse_ref[p, h : h + 1, :] = high + jnp.log(denominator)
                weights.append([value.astype(low) for value in found])
                denominators.append(denominator)
            context_t = jnp.concatenate(
                [
                    sum(
                        dot_tn(kv_all[p, a:b, value_cols(h)], value)
                        for (a, b, _), value in zip(cuts, weights[h])
                    )
                    / denominators[h]
                    for h in heads
                ]
            )
            ctx_t_ref[p] = context_t
            context = context_t.T.astype(low)
            for j, ref in enumerate(ctx_refs):
                ref[p] = context[j * share : (j + 1) * share]

        for count in range(1, total // block + 1):
            pl.when(blocks == count)(functools.partial(body, count))
        return carry

    lax.fori_loop(0, proteins, protein, 0)


def attend_back_kernel(counts, pos, *refs):
    stacks, arrays, groups = counts
    q_refs, dctx_refs, refs = refs[:stacks], refs[stacks : stacks + groups], refs[stacks + groups :]
    ctx_t_ref, lse_ref, kv_refs, refs = refs[0], refs[1], refs[2 : 2 + arrays], refs[2 + arrays :]
    dq_ref, dkv_refs, (kv_all, dkv_all, dq_all, sems, out_sems) = refs[0], refs[1:-5], refs[-5:]
    _, proteins, share, width = q_refs[0].shape
    rows = groups * share
    total = kv_all.shape[1]
    block = min(256, total)
    heads = range(width // HEAD_DIM)

    def keys_of(p, wait):
        blocks = jnp.where(pos[proteins] * rows < pos[p], (pos[p] + block - 1) // block, 0)
        start_keys(pos, p, proteins, groups, kv_refs, kv_all, sems, blocks, block, wait)
        return blocks

    for p in range(proteins):
        keys_of(p, False)

    def results_of(p, wait):
        for j in range(groups):
            copy = pltpu.make_async_copy(
                dq_all.at[p, pl.ds(j * share, share), :], dq_ref.at[j, p], out_sems.at[p]
            )
            copy.wait() if wait else copy.start()
            for i, ref in enumerate(dkv_refs):
                at = place(pos, proteins, groups, share, i, j)
                copy = pltpu.make_async_copy(
                    dkv_all.at[p, pl.ds(at, share), :], ref.at[j, p], out_sems.at[p]
                )
                copy.wait() if wait else copy.start()

    def protein(p, carry):
        length = pos[p]
        blocks = keys_of(p, True)

        @pl.when(blocks == 0)
        def _():
            dkv_all[p] = jnp.zeros(dkv_all.shape[1:], low)
            dq_all[p] = jnp.zeros(dq_all.shape[1:], low)

        def body(count):
            n = count * block
            queries = query_rows(q_refs, p)
            dctx = jnp.concatenate([ref[p] for ref in dctx_refs])
            product = dctx.astype(wide).T * ctx_t_ref[p]
            cols = lambda h: slice(h * HEAD_DIM, (h + 1) * HEAD_DIM)
            value_cols = lambda h: slice(width + h * HEAD_DIM, width + (h + 1) * HEAD_DIM)
            deltas = [jnp.sum(product[cols(h), :], axis=0, keepdims=True) for h in heads]
            dq = []
            for a, b, last in chunks(n, block):
                scores = [dot_nt(kv_all[p, a:b, cols(h)], queries[:, cols(h)]) for h in heads]
                dprobs = [dot_nt(kv_all[p, a:b, value_cols(h)], dctx[:, cols(h)]) for h in heads]
                probs, dscores = [], []
                for h in heads:
                    score = masked(scores[h], length, a) if last else scores[h]
                    prob = jnp.exp(score - lse_ref[p, h : h + 1, :])
                    probs.append(prob.astype(low))
                    dscores.append((prob * (dprobs[h] - deltas[h])).astype(low))
                dv = [dot(probs[h], dctx[:, cols(h)]) for h in heads]
                dk = [dot(dscores[h], queries[:, cols(h)]) for h in heads]
                dq.append(
                    jnp.concatenate([dot_tn(kv_all[p, a:b, cols(h)], dscores[h]) for h in heads])
                )
                dkv_all[p, a:b, :width] = jnp.concatenate(dk, axis=1).astype(low)
                dkv_all[p, a:b, width:] = jnp.concatenate(dv, axis=1).astype(low)
            if n < total:
                dkv_all[p, n:, :] = jnp.zeros((total - n, 2 * width), low)
            dq_all[p] = (sum(dq).T * score_scale).astype(low)

        for count in range(1, total // block + 1):
            pl.when(blocks == count)(functools.partial(body, count))
        results_of(p, False)
        return carry

    lax.fori_loop(0, proteins, protein, 0)
    for p in range(proteins):
        results_of(p, True)


def attend(pos, queries, kv_pieces, waits):
    groups = sum(q.shape[0] for q in queries)
    _, proteins, share, width = queries[0].shape
    rows = groups * share
    total = share * sum(piece.shape[0] for piece in kv_pieces)
    found = kernel_call(
        functools.partial(attend_kernel, (len(queries), len(kv_pieces), groups)),
        "attend",
        queries,
        [((proteins, share, width), low, hbm)] * groups
        + [((proteins, width, rows), wide, hbm), ((proteins, 8, rows), wide, hbm)],
        scalars=[pos],
        scratch=[
            pltpu.VMEM((proteins, total, 2 * width), low),
            pltpu.SemaphoreType.DMA((proteins,)),
        ],
        mebibytes=32,
        far_in=hbm,
        local=kv_pieces,
        waits=waits,
        flops=int(1e10),
    )
    return found[:groups], found[groups], found[groups + 1]


def attend_back(pos, queries, dctx, ctx_t, lse, kv_pieces, waits):
    groups = len(dctx)
    _, proteins, share, width = queries[0].shape
    total = share * sum(piece.shape[0] for piece in kv_pieces)
    pieces = total // (groups * share)
    arrays = [*queries, *dctx, ctx_t, lse]
    found = kernel_call(
        functools.partial(attend_back_kernel, (len(queries), len(kv_pieces), groups)),
        "attend_back",
        arrays,
        [((groups, proteins, share, width), low, "kernel")]
        + [((groups, proteins, share, 2 * width), low, "kernel")] * pieces,
        scalars=[pos],
        scratch=[
            pltpu.VMEM((proteins, total, 2 * width), low),
            pltpu.VMEM((proteins, total, 2 * width), low),
            pltpu.VMEM((proteins, groups * share, width), low),
            pltpu.SemaphoreType.DMA((proteins,)),
            pltpu.SemaphoreType.DMA((proteins,)),
        ],
        mebibytes=32,
        far_in=[i for i in range(len(arrays)) if not 0 <= i - len(queries) < groups],
        local=kv_pieces,
        waits=waits,
        flops=int(2e10),
    )
    return found[0], found[1:]


def project_kernel(count, *refs):
    tok_refs, (qmap_ref, kmap_ref, vmap_ref, qbias_ref, vbias_ref, q_ref, kv_ref) = refs[:count], refs[count:]
    width = q_ref.shape[-1]
    for j, tok_ref in enumerate(tok_refs):
        shape = q_ref.shape[1:]
        queries = dot(tok_ref[...], qmap_ref[...]) + qbias_ref[...].astype(wide)
        q_ref[j] = queries.astype(low).reshape(shape)
        kv_ref[j, :, :, :width] = dot(tok_ref[...], kmap_ref[...]).astype(low).reshape(shape)
        values = dot(tok_ref[...], vmap_ref[...]) + vbias_ref[...].astype(wide)
        kv_ref[j, :, :, width:] = values.astype(low).reshape(shape)


def project(tok, maps, proteins, waits=()):
    width = maps[0].shape[1]
    share = tok[0].shape[0] // proteins
    return kernel_call(
        functools.partial(project_kernel, len(tok)),
        "project",
        [*tok, *maps],
        [
            ((len(tok), proteins, share, width), low, hbm),
            ((len(tok), proteins, share, 2 * width), low, hbm),
        ],
        waits=waits,
        far_in=hbm,
    )


def unit_of(values):
    centered = values - jnp.mean(values, axis=-1, keepdims=True)
    variance = jnp.mean(centered * centered, axis=-1, keepdims=True)
    inverse = lax.rsqrt(variance + epsilon)
    return centered * inverse, inverse


def norm_back(grad_rows, unitized, inverse, scales):
    scaled = grad_rows * scales
    grad_mean = jnp.mean(scaled, axis=-1, keepdims=True)
    cross_mean = jnp.mean(scaled * unitized, axis=-1, keepdims=True)
    return inverse * (scaled - grad_mean - unitized * cross_mean)


def steps(rows):
    size = 64 if rows % 64 == 0 else rows
    return [slice(at, at + size) for at in range(0, rows, size)]


def merge_kernel(groups, heads, *refs):
    ctx_refs, refs = refs[:groups], refs[groups:]
    own_map, maps_all, tok_ref, small_ref = refs[:4]
    normed_ref, low_ref, unit_ref, inv_ref, maps_ref = refs[4:]
    others = groups - 1
    slots, _, size, _ = maps_all.shape
    for j in range(others):
        for k in range(slots):
            maps_ref[j, k * size : (k + 1) * size, :] = maps_all[k, heads[0] ^ (j + 1)]
    merged = small_ref[0:1, :] + dot(ctx_refs[0][...], own_map[...])
    for j in range(others):
        merged += dot(ctx_refs[j + 1][...], maps_ref[j])
    unit_ref[...] = tok_ref[...].astype(wide) + merged
    for rows in steps(tok_ref.shape[0]):
        unit, inverse = unit_of(unit_ref[rows, :])
        normed = unit * small_ref[1:2, :] + small_ref[2:3, :]
        normed_ref[rows, :] = normed
        low_ref[rows, :] = normed.astype(low)
        unit_ref[rows, :] = unit
        inv_ref[rows, :] = jnp.broadcast_to(inverse, (inverse.shape[0], 128))


def merge_norm(heads, ctx, own_map, maps_all, tok, small, waits):
    rows, model = tok.shape
    groups = len(ctx)
    return kernel_call(
        functools.partial(merge_kernel, groups),
        "merge_norm",
        [*ctx, own_map, maps_all, tok, small],
        [
            ((rows, model), wide, hbm),
            ((rows, model), low, hbm),
            ((rows, model), wide, hbm),
            ((rows, 128), wide, hbm),
            ((groups - 1, *own_map.shape), low, hbm),
        ],
        scalars=[heads],
        waits=waits,
        far_in=hbm,
    )


def final_kernel(*refs):
    normed_ref, near_ref, core_ref, far_ref, small_ref, cot_ref, live_ref = refs[:7]
    out_ref, dsum_ref, dbranch_ref, sums_ref = refs[7:]
    gain = small_ref[4:5, :]
    gain_sum = shift_sum = bias_sum = 0.0
    for rows in steps(normed_ref.shape[0]):
        branch = near_ref[rows, :].astype(wide) + core_ref[rows, :].astype(wide)
        branch = branch + far_ref[rows, :].astype(wide) + small_ref[3:4, :]
        unit, inverse = unit_of(normed_ref[rows, :] + branch)
        out_ref[rows, :] = (unit * gain + small_ref[5:6, :]).astype(low)
        grad = cot_ref[rows, :].astype(wide) * live_ref[rows, 0:1]
        dsum = norm_back(grad, unit, inverse, gain)
        dsum_ref[rows, :] = dsum
        dbranch = dsum.astype(low)
        dbranch_ref[rows, :] = dbranch
        gain_sum += jnp.sum(grad * unit, axis=0, keepdims=True)
        shift_sum += jnp.sum(grad, axis=0, keepdims=True)
        bias_sum += jnp.sum(dbranch.astype(wide), axis=0, keepdims=True)
    sums_ref[...] = jnp.zeros(sums_ref.shape, wide)
    sums_ref[0:1, :] = bias_sum
    sums_ref[1:2, :] = gain_sum
    sums_ref[2:3, :] = shift_sum


def final_norm(normed, near, core, across, small, cot, live, waits):
    rows, model = normed.shape
    return kernel_call(
        final_kernel,
        "final_norm",
        [normed, near, core, across, small, cot, live],
        [
            ((rows, model), low, hbm),
            ((rows, model), wide, hbm),
            ((rows, model), low),
            ((8, model), wide, hbm),
        ],
        far_in=[0, 4, 5, 6],
        waits=waits,
    )


def first_back_kernel(groups, *refs):
    dsum_ref, near_ref, core_ref, far_ref, unit_ref, inv_ref, small_ref, own_map, maps_ref = refs[:9]
    dfirst_ref, dmerged_ref, sums_ref = refs[9:12]
    dctx_refs = refs[12:]
    gain = small_ref[1:2, :]
    gain_sum = shift_sum = bias_sum = 0.0
    for rows in steps(dsum_ref.shape[0]):
        grad = near_ref[rows, :].astype(wide) + core_ref[rows, :].astype(wide)
        grad = dsum_ref[rows, :] + grad + far_ref[rows, :].astype(wide)
        unit = unit_ref[rows, :]
        dfirst = norm_back(grad, unit, inv_ref[rows, 0:1], gain)
        dfirst_ref[rows, :] = dfirst
        dmerged = dfirst.astype(low)
        dmerged_ref[rows, :] = dmerged
        gain_sum += jnp.sum(grad * unit, axis=0, keepdims=True)
        shift_sum += jnp.sum(grad, axis=0, keepdims=True)
        bias_sum += jnp.sum(dmerged.astype(wide), axis=0, keepdims=True)
    for j in range(groups):
        merge_map = maps_ref[j - 1] if j else own_map[...]
        dctx_refs[j][...] = dot_nt(dmerged_ref[...], merge_map).astype(low)
    sums_ref[...] = jnp.zeros(sums_ref.shape, wide)
    sums_ref[3:4, :] = bias_sum
    sums_ref[4:5, :] = gain_sum
    sums_ref[5:6, :] = shift_sum


def first_back(dsum, near, core, across, unit, inverse, small, own_map, maps, waits):
    rows, model = dsum.shape
    groups, width = maps.shape[0] + 1, own_map.shape[0]
    found = kernel_call(
        functools.partial(first_back_kernel, groups),
        "first_back",
        [dsum, near, core, across, unit, inverse, small, own_map, maps],
        [((rows, model), wide, hbm), ((rows, model), low), ((8, model), wide, hbm)]
        + [((rows, width), low)] * groups,
        waits=waits,
        far_in=[0, 4, 5, 6, 7, 8],
    )
    return found[0], found[1], found[2], found[3:]


def forward_kernel(a_ref, b_ref, inner_ref, outer_ref, bias_ref, act_ref, slope_ref, own_ref, other_ref):
    rows = a_ref.shape[0]
    for ref, out, at in ((a_ref, own_ref, 0), (b_ref, other_ref, rows)):
        pre = dot_nt(ref[...], inner_ref[...]) + bias_ref[...]
        upper = 0.5 + 0.5 * lax.erf(pre * 0.7071067811865476)
        active = (pre * upper).astype(low)
        slope = upper + pre * (0.3989422804014327 * jnp.exp(-0.5 * pre * pre))
        act_ref[at : at + rows, :] = active
        slope_ref[at : at + rows, :] = slope.astype(low)
        out[...] = dot(active, outer_ref[...]).astype(low)


def feed_forward(a, b, inner, outer, bias, waits=()):
    rows, model = a.shape
    hidden = inner.shape[0]
    return kernel_call(
        forward_kernel,
        "feed_forward",
        [a, b, inner, outer, bias],
        [((2 * rows, hidden), low, hbm)] * 2 + [((rows, model), low)] * 2,
        waits=waits,
        far_in=[0, 1],
    )


def backward_kernel(a_ref, b_ref, inner_ref, outer_ref, slope_ref, dinner_ref, own_ref, other_ref):
    rows = a_ref.shape[0]
    for ref, out, at in ((a_ref, own_ref, 0), (b_ref, other_ref, rows)):
        dactive = dot_nt(ref[...], outer_ref[...])
        dinner = (dactive * slope_ref[at : at + rows, :].astype(wide)).astype(low)
        dinner_ref[at : at + rows, :] = dinner
        out[...] = dot(dinner, inner_ref[...]).astype(low)


def feed_backward(a, b, inner, outer, slope, waits=()):
    rows, model = a.shape
    hidden = inner.shape[0]
    return kernel_call(
        backward_kernel,
        "feed_backward",
        [a, b, inner, outer, slope],
        [((2 * rows, hidden), low, hbm)] + [((rows, model), low)] * 2,
        waits=waits,
        far_in=[4],
    )


def grad_kernel(numbers, block, bias, split, *refs):
    hid, row_refs, refs = refs[:2], refs[2:6], refs[6:]
    got_ref, out_refs = (refs[0], refs[1:]) if split else (None, refs)
    model = out_refs[0].shape[-1]
    half = len(numbers) // len(out_refs)
    for k, number in enumerate(numbers):
        cols = slice(number * block, (number + 1) * block)
        total = sums = 0.0
        for i, ref in enumerate(hid):
            rows = ref.shape[0] // 2
            total += dot_tn(ref[:rows, cols], row_refs[2 * i][...])
            total += dot_tn(ref[rows:, cols], row_refs[2 * i + 1][...])
            if bias:
                sums += jnp.sum(ref[:, cols].astype(wide), axis=0, keepdims=True)
        out_ref, at = out_refs[k // half], k % half
        if split:
            total += got_ref[k, :block, :].astype(wide)
        out_ref[at, :block, :] = total.astype(low)
        if bias:
            sums = jnp.pad(sums, ((0, 15), (0, model - block)))
            if split:
                sums += got_ref[k, block:, :].astype(wide)
            out_ref[at, block:, :] = sums.astype(low)


def weight_grad(hid, row_list, block, numbers, bias, waits, got=None):
    model = row_list[0].shape[1]
    split = got is not None
    count = len(numbers) // (1 + split)
    found = kernel_call(
        functools.partial(grad_kernel, numbers, block, bias, split),
        "weight_grad",
        [*hid, *row_list] + [got] * split,
        [((count, block + 16 * bias, model), low)] * (1 + split),
        waits=waits,
    )
    return found if split else found[0]


def units_kernel(units, shares, slot, inner_ref, outer_ref, bias_ref, own_inner, own_outer, own_bias):
    for m in range(shares):
        at = pl.multiple_of((slot[0] ^ (m << 1)) * units, units)
        own_inner[m] = inner_ref[:, pl.ds(at, units)].T
        own_outer[m] = outer_ref[pl.ds(at, units), :]
        own_bias[m] = jnp.broadcast_to(bias_ref[:, pl.ds(at, units)], (16, units))


def own_units(slot, shares, innermap, outermap, innerbias, waits):
    model = innermap.shape[0]
    units = innermap.shape[1] // (2 * shares)
    if units % 128:
        found = []
        for m in range(shares):
            at = (slot[0] ^ (m << 1)) * units
            inner = lax.dynamic_slice_in_dim(innermap, at, units, 1).T
            outer = lax.dynamic_slice_in_dim(outermap, at, units, 0)
            bias = lax.dynamic_slice_in_dim(innerbias, at, units, 1)
            found.append((inner, outer, jnp.broadcast_to(bias, (16, units))))
        return [jnp.stack(pieces) for pieces in zip(*found)]
    return kernel_call(
        functools.partial(units_kernel, units, shares),
        "own_units",
        [innermap, outermap, innerbias],
        [((shares, units, model), low, hbm)] * 2 + [((shares, 16, units), innerbias.dtype, hbm)],
        scalars=[slot],
        waits=waits,
        far_in=[0, 1],
    )


def pack_inner_kernel(own_inner, own_bias, pack_ref):
    units = own_inner.shape[1]
    pack_ref[0, :units, :] = own_inner[0]
    pack_ref[0, units:, :] = jnp.zeros((16, pack_ref.shape[2]), low)
    pack_ref[0, units:, :units] = own_bias[0]


def pack_outer_kernel(own_outer, pack_ref):
    pack_ref[0] = own_outer[0]


def pack_inner(own):
    _, units, model = own[0].shape
    out = [((1, units + 16, model), low)]
    return kernel_call(pack_inner_kernel, "pack_inner", [own[0], own[2]], out)[0]


def pack_outer(own, waits):
    _, units, model = own[1].shape
    out = [((1, units, model), low)]
    return kernel_call(pack_outer_kernel, "pack_outer", [own[1]], out, waits=waits)[0]


def stack_kernel(*refs):
    count = len(refs) // 3
    for k in range(count):
        a_ref, b_ref, out_ref = refs[2 * k], refs[2 * k + 1], refs[2 * count + k]
        out_ref[: a_ref.shape[0]] = a_ref[...]
        out_ref[a_ref.shape[0] :] = b_ref[...]


def stack_pairs(pairs):
    return kernel_call(
        stack_kernel,
        "stack_pairs",
        [value for pair in pairs for value in pair],
        [((2 * a.shape[0], *a.shape[1:]), a.dtype) for a, _ in pairs],
    )


def join_kernel(units, masks, own_inner, own_outer, own_bias, *refs):
    parts, (inner_ref, outer_ref, bias_ref) = refs[:-3], refs[-3:]
    for m in range(own_inner.shape[0]):
        at, far = 2 * m * units, (2 * m + 1) * units
        inner_ref[at:far, :] = own_inner[m]
        outer_ref[at:far, :] = own_outer[m]
        bias_ref[:, at:far] = own_bias[m, 0:1, :].astype(wide)
    for which, (ref, order) in enumerate(zip(parts, masks)):
        for k, m in enumerate(order):
            far = (2 * m + 1) * units
            if which < 2:
                inner_ref[far : far + units, :] = ref[k, :units, :]
                bias_ref[:, far : far + units] = ref[k, units : units + 16, :units].astype(wide)[:1]
            else:
                outer_ref[far : far + units, :] = ref[k]


def join_units(own, parts, masks, waits):
    shares, units, model = own[0].shape
    hidden = 2 * shares * units
    return kernel_call(
        functools.partial(join_kernel, units, masks),
        "join_units",
        [*own, *parts],
        [((hidden, model), low)] * 2 + [((1, hidden), wide)],
        waits=waits,
        far_in=hbm,
    )


def slot_order(number, bits):
    return ((number & 1) << (bits - 1)) | (number >> 1)


def qkv_kernel(counts, slots, slot, *refs):
    out_ref, q_all, kv_all = refs[-3:]
    dq_ref, refs = refs[0], refs[1:-3]
    width, model = dq_ref.shape[-1], out_ref.shape[-1]
    q_all[...] = dq_ref[...].reshape(q_all.shape)
    q_sum = jnp.sum(q_all[...].astype(wide), axis=0, keepdims=True)
    q_grad = kv_grad = kv_sum = 0.0
    for i, count in enumerate(counts):
        dkv_ref, tok_refs, refs = refs[0], refs[1 : 1 + count], refs[1 + count :]
        kv_all[...] = dkv_ref[...].reshape(kv_all.shape)
        kv_sum += jnp.sum(kv_all[...].astype(wide), axis=0, keepdims=True)
        at = 0
        for tok_ref in tok_refs:
            there = slice(at, at + tok_ref.shape[0])
            at += tok_ref.shape[0]
            kv_grad += dot_tn(kv_all[there, :], tok_ref[...])
            if i == 0:
                q_grad += dot_tn(q_all[there, :], tok_ref[...])
    grad = jnp.concatenate([q_grad, kv_grad]).astype(low)
    sums = jnp.concatenate([q_sum, kv_sum], axis=1)
    bits = slots.bit_length() - 1
    block = 3 * width // slots
    for b in range(slots):
        at = slot_order(slot[0] ^ b, bits)
        out_ref[at, :block, :] = grad[b * block : (b + 1) * block]
        line = jnp.pad(sums[:, b * block : (b + 1) * block], ((0, 15), (0, model - block)))
        out_ref[at, pad16(block) :, :] = line.astype(low)


def qkv_grads(slot, slots, dq, pairs, waits):
    model = pairs[0][1][0].shape[-1]
    groups, width = dq.shape[0], dq.shape[-1]
    total = dq.size // width
    far_at, at = [], 1
    for dkv, tok in pairs:
        far_at += range(at + 1, at + 1 + len(tok))
        at += 1 + len(tok)
    return kernel_call(
        functools.partial(qkv_kernel, [len(tok) for _, tok in pairs], slots),
        "qkv_grads",
        [dq] + [a for dkv, tok in pairs for a in (dkv, *tok)],
        [((slots, pad16(3 * width // slots) + 16, model), low)],
        far_in=far_at,
        scalars=[slot],
        waits=waits,
        scratch=[pltpu.VMEM((total, width), low), pltpu.VMEM((total, 2 * width), low)],
        mebibytes=24,
    )[0]


def hold_kernel(value_ref, out_ref):
    out_ref[...] = value_ref[...]


def hold(value, waits):
    out = [(value.shape, value.dtype)]
    return kernel_call(hold_kernel, "hold", [value], out, waits=waits)[0]


def add_kernel(a_ref, b_ref, *out_refs):
    at = 0
    for ref in out_refs:
        there = slice(at, at + ref.shape[0])
        at += ref.shape[0]
        ref[...] = (a_ref[there].astype(wide) + b_ref[there].astype(wide)).astype(ref.dtype)


def add_split(a, b, counts, waits=(), kind=low):
    out = [((count, *a.shape[1:]), kind) for count in counts]
    return kernel_call(add_kernel, "add_split", [a, b], out, waits=waits)


def dtokens_kernel(dq_ref, own_ref, got_ref, q_ref, k_ref, v_ref, *out_refs):
    width = dq_ref.shape[-1]
    rows = dq_ref.shape[1] * dq_ref.shape[2]
    for j, ref in enumerate(out_refs):
        dkv = (own_ref[j].astype(wide) + got_ref[j].astype(wide)).astype(low)
        dkv = dkv.reshape(rows, 2 * width)
        total = dot_nt(dq_ref[j].reshape(rows, width), q_ref[...])
        total += dot_nt(dkv[:, :width], k_ref[...]) + dot_nt(dkv[:, width:], v_ref[...])
        ref[...] = total.astype(ref.dtype)


def dtokens(dq, own, got, maps, waits):
    rows, model = dq.shape[1] * dq.shape[2], maps[0].shape[0]
    return kernel_call(
        dtokens_kernel,
        "dtokens",
        [dq, own, got, *maps],
        [((rows, model), wide), ((rows, model), low)] * (dq.shape[0] // 2),
        waits=waits,
    )


def tokens_kernel(dfirst_ref, part_ref, near_ref, far_ref, out_ref):
    total = dfirst_ref[...] + part_ref[...] + near_ref[...].astype(wide)
    out_ref[...] = (total + far_ref[...].astype(wide)).astype(low)


def pack_sums_kernel(units, inner_ref, inner_got, outer_ref, outer_got, own_ref, send_ref):
    model = own_ref.shape[1]
    inner = inner_ref[0].astype(wide) + inner_got[0].astype(wide)
    outer = outer_ref[0].astype(wide) + outer_got[0].astype(wide)
    sums = inner[2 * units :, : 2 * units].astype(low)
    for k, ref in enumerate((own_ref, send_ref)):
        there = slice(k * units, (k + 1) * units)
        ref[:units, :] = inner[there].astype(low)
        ref[units : 2 * units, :] = outer[there].astype(low)
        ref[2 * units :, :] = jnp.zeros((16, model), low)
        ref[2 * units :, :units] = sums[:, there]


def pack_sums(units, inner, inner_got, outer, outer_got, waits):
    model = inner.shape[-1]
    return kernel_call(
        functools.partial(pack_sums_kernel, units),
        "pack_sums",
        [inner, inner_got, outer, outer_got],
        [((2 * units + 16, model), low)] * 2,
        waits=waits,
    )


def merge_grad_kernel(groups, core, *refs):
    ctx_refs, (dmerged_ref, a_ref, b_ref, keep_ref, send_ref, grad_all) = refs[:groups], refs[groups:]
    half = keep_ref.shape[1]
    for j, ref in enumerate(ctx_refs):
        grad_all[...] = dot_tn(ref[...], dmerged_ref[...]).astype(low)
        keep = pl.multiple_of(core[0] * half, half)
        send = pl.multiple_of((1 - core[0]) * half, half)
        keep_ref[j] = grad_all[pl.ds(keep, half), :]
        send_ref[j * half : (j + 1) * half, :] = grad_all[pl.ds(send, half), :]
    sums = a_ref[...] + b_ref[...]
    send_ref[groups * half :, :] = jnp.concatenate([sums, jnp.zeros_like(sums)]).astype(low)


def merge_grads(core, ctx, dmerged, a, b):
    rows, width = ctx[0].shape
    model = dmerged.shape[1]
    groups, half = len(ctx), width // 2
    return kernel_call(
        functools.partial(merge_grad_kernel, groups),
        "merge_grads",
        [*ctx, dmerged, a, b],
        [((groups, half, model), low), ((groups * half + 16, model), low)],
        far_in=[i for i in range(groups + 3) if i != groups],
        scalars=[core],
        scratch=[pltpu.VMEM((width, model), low)],
    )


def merge_heads_kernel(groups, a_ref, b_ref, keep_ref, got_ref, near_ref, send_ref, sums_ref):
    half = keep_ref.shape[1]
    total = lambda j: keep_ref[j].astype(wide) + got_ref[j * half : (j + 1) * half, :].astype(wide)
    for k in range(groups // 2):
        near_ref[k] = total(2 * k).astype(low)
        send_ref[k * half : (k + 1) * half, :] = total(2 * k + 1).astype(low)
    sums = a_ref[...] + b_ref[...] + got_ref[groups * half : groups * half + 16, :].astype(wide)[:8]
    sums_ref[...] = sums
    at = groups // 2 * half
    send_ref[at:, :] = jnp.concatenate([sums, jnp.zeros_like(sums)]).astype(low)


def merge_heads(a, b, keep, got):
    groups, half, model = keep.shape
    count = groups // 2
    return kernel_call(
        functools.partial(merge_heads_kernel, groups),
        "merge_heads",
        [a, b, keep, got],
        [((count, half, model), low), ((count * half + 16, model), low), ((8, model), wide)],
    )


def merge_far_kernel(keep_ref, got_ref, sums_ref, near_ref, send_ref, out_sums_ref):
    half = keep_ref.shape[1]
    near_ref[...] = (keep_ref[0].astype(wide) + got_ref[:half, :].astype(wide)).astype(low)
    far = keep_ref[1].astype(wide) + got_ref[half : 2 * half, :].astype(wide)
    send_ref[:half, :] = far.astype(low)
    sums = sums_ref[...] + got_ref[2 * half :, :].astype(wide)[:8]
    out_sums_ref[...] = sums
    send_ref[half:, :] = jnp.concatenate([sums, jnp.zeros_like(sums)]).astype(low)


def merge_far(keep, got, sums, waits):
    _, half, model = keep.shape
    return kernel_call(
        merge_far_kernel,
        "merge_far",
        [keep, got, sums],
        [((half, model), low), ((half + 16, model), low), ((8, model), wide)],
        waits=waits,
    )


def slots_kernel(block, size, slot, grad_ref, core_ref, near_ref, far_ref, sums_ref, *refs):
    own_ref, send_refs, (out_sums_ref, rows_all) = refs[0], refs[1:-2], refs[-2:]
    shares = len(send_refs) + 1
    half = near_ref.shape[0]
    merged = (near_ref[...].astype(wide) + far_ref[:half, :].astype(wide)).astype(low)
    for k in range(shares):
        rows_all[k] = merged[k * size : (k + 1) * size]
    sums = sums_ref[...] + far_ref[half:, :].astype(wide)[:8]
    out_sums_ref[...] = sums
    start = pad16(block) + 16
    for m, ref in enumerate((own_ref, *send_refs)):
        ref[:start, :] = (grad_ref[m].astype(wide) + core_ref[m].astype(wide)).astype(low)
        ref[start : start + size, :] = rows_all[(slot[0] >> 1) ^ m]
        if m:
            both = jnp.concatenate([sums, jnp.zeros_like(sums)]).astype(low)
            ref[start + pad16(size) :, :] = both


def slot_parts(slot, block, size, grads, core, near, far, sums, waits):
    shares, _, model = core.shape
    rows = pad16(block) + 16 + pad16(size)
    return kernel_call(
        functools.partial(slots_kernel, block, size),
        "slot_parts",
        [grads, core, near, far, sums],
        [((rows, model), low)]
        + [((rows + 16, model), low)] * (shares - 1)
        + [((8, model), wide)],
        scalars=[slot],
        scratch=[pltpu.VMEM((shares, size, model), low)],
        waits=waits,
    )


def slot_sum_kernel(own_ref, sums_ref, *refs):
    got_refs, (out_ref, out_sums_ref) = refs[:-2], refs[-2:]
    rows = own_ref.shape[0]
    total, sums = own_ref[...].astype(wide), sums_ref[...]
    for ref in got_refs:
        total += ref[:rows, :].astype(wide)
        sums += ref[rows:, :].astype(wide)[:8]
    out_ref[...] = total.astype(low)
    out_sums_ref[...] = sums


def slot_sum(own, sums, got, waits):
    return kernel_call(
        slot_sum_kernel,
        "slot_sum",
        [own, sums, *got],
        [(own.shape, low), (sums.shape, wide)],
        waits=waits,
    )


def feed_out_kernel(units, grads_ref, inner_ref, outer_ref, bias_ref, here, inner, outer, bias, sems):
    slots, rows, model = grads_ref.shape
    copies = [pltpu.make_async_copy(grads_ref.at[k], here.at[k], sems.at[0, k]) for k in range(slots)]
    for copy in copies:
        copy.start()
    done = []
    for k, copy in enumerate(copies):
        copy.wait()
        cols = slice(k * units, (k + 1) * units)
        inner[:, cols] = here[k, :units, :].astype(wide).T
        outer[cols, :] = here[k, units : 2 * units, :].astype(wide)
        bias[k : k + 1, :] = here[k, 2 * units : 2 * units + 16, :units].astype(wide)[:1]
        done.append(pltpu.make_async_copy(inner.at[:, cols], inner_ref.at[:, cols], sems.at[1, k]))
        done.append(pltpu.make_async_copy(outer.at[cols, :], outer_ref.at[cols, :], sems.at[2, k]))
        done[-2].start()
        done[-1].start()
    done.append(pltpu.make_async_copy(bias, bias_ref, sems.at[0, 0]))
    done[-1].start()
    for copy in done:
        copy.wait()


def feed_out(grads, units):
    slots, rows, model = grads.shape
    hidden = slots * units
    if units % 128:
        inner = grads[:, :units].reshape(hidden, model).astype(wide).T
        outer = grads[:, units : 2 * units].reshape(hidden, model).astype(wide)
        return inner, outer, grads[:, 2 * units, :units].astype(wide)
    shapes = [(model, hidden), (hidden, model), (slots, units)]
    return pl.pallas_call(
        functools.partial(feed_out_kernel, units),
        in_specs=[in_hbm],
        out_specs=[in_hbm] * 3,
        out_shape=[jax.ShapeDtypeStruct(shape, wide) for shape in shapes],
        scratch_shapes=[pltpu.VMEM(grads.shape, low)]
        + [pltpu.VMEM(shape, wide) for shape in shapes]
        + [pltpu.SemaphoreType.DMA((3, slots))],
        compiler_params=params(60),
        name="feed_out",
    )(grads)


def qkv_out_kernel(block, order, slot, *refs):
    parts, refs = refs[: len(order)], refs[len(order) :]
    q_ref, k_ref, v_ref, merge_ref, bias_ref, rows_all, merge_all = refs
    start, size = pad16(block), merge_all.shape[1]
    width = q_ref.shape[1]
    slots = merge_all.shape[0]
    for mask, part in zip(order, parts):
        at = slot[0] ^ mask
        rows_all[at] = part[:block, :]
        bias_ref[pl.ds(at, 1), :] = part[start : start + 16, :].astype(wide)[:1]
        at = (at & 1) * (slots // 2) + (at >> 1)
        merge_all[at] = part[start + 16 : start + 16 + size, :]
    grad = rows_all[...].reshape(3 * width, -1)
    for i, ref in enumerate((q_ref, k_ref, v_ref)):
        ref[...] = grad[i * width : (i + 1) * width].astype(wide).T
    merge_ref[...] = merge_all[...].reshape(merge_ref.shape).astype(wide)


def qkv_out(slot, parts, order, block, width):
    model = parts[0].shape[-1]
    slots = 3 * width // block
    size = width // slots
    return kernel_call(
        functools.partial(qkv_out_kernel, block, order),
        "qkv_out",
        parts,
        [((model, width), wide)] * 3 + [((width, model), wide), ((slots, model), wide)],
        scalars=[slot],
        scratch=[pltpu.VMEM((slots, block, model), low), pltpu.VMEM((slots, size, model), low)],
    )


def shards(
    tokens,
    querymap,
    querybias,
    keymap,
    valuemap,
    valuebias,
    mergemap,
    mergebias,
    normgain,
    normshift,
    innermap,
    innerbias,
    outermap,
    outerbias,
    finalgain,
    finalshift,
    lengths,
    cotangent,
):
    proteins, share, model = tokens.shape
    groups = lax.axis_size("heads")
    rows = proteins * share
    width = querymap.shape[1]
    seq, heads = lax.axis_index("seq"), lax.axis_index("heads")
    seq_size, dp_size = lax.axis_size("seq"), lax.axis_size("dp")
    pos = jnp.concatenate([lengths, jnp.stack([seq, heads]).astype(jnp.int32)])
    core_bit, row_bit, far_bit = ("seq", 1), ("heads", 1), ("heads", 2)
    seq_bits = [("seq", 1 << k) for k in range(1, seq_size.bit_length() - 1)]
    share_bits = seq_bits + [("dp", 1 << k) for k in range(dp_size.bit_length() - 1)]
    slot_bits = [core_bit] + share_bits
    slots = 1 << len(slot_bits)
    shares = slots // 2
    slot = lax.axis_index("dp") * seq_size + seq
    units = innermap.shape[1] // slots
    merge_units = width // slots
    row = lambda vector: vector.reshape(1, -1)

    slot_scalar = slot.reshape(1).astype(jnp.int32)

    own_rows = tokens.reshape(rows, model)
    small = jnp.stack([mergebias, normgain, normshift, outerbias, finalgain, finalshift])
    small = jnp.pad(small.astype(wide), ((0, 2), (0, 0)))
    second = swap(own_rows, *far_bit)
    first = swap(own_rows, *row_bit)
    maps = [querymap, keymap, valuemap]
    biases = [row(querybias), row(valuebias)]
    merge_own = lax.dynamic_slice_in_dim(mergemap, slot * merge_units, merge_units, 0)
    merge_all = lax.all_gather(merge_own, ("dp", "seq", "heads"))
    merge_all = merge_all.reshape(slots, groups, merge_units, model)
    own = own_units(slot_scalar, shares, innermap, outermap, row(innerbias), [small])

    def exchange_keys(piece):
        found = {0: piece}
        for axis, stride in seq_bits + [core_bit]:
            for i in list(found):
                found[i | stride] = swap(found[i], axis, stride)
        return found

    maps_biases = [*maps, *biases]
    seq_tokens = {i: [] for i in range(0, seq_size, 2)}

    def exchange_tokens(piece):
        found = {0: piece}
        for axis, stride in seq_bits:
            for i in list(found):
                found[i | stride] = swap(found[i], axis, stride)
        for i in found:
            seq_tokens[i].append(found[i])
        return [found[i] for i in found if i]

    far_tokens = [exchange_tokens(own_rows)]
    far_inner = swap(pack_inner(own), *far_bit)
    second_held = hold(second, [first, own[0]])
    third = swap(second_held, *row_bit)
    q_three, kv_three = project([own_rows, first, second_held], maps_biases, proteins)
    kv_three = exchange_keys(kv_three)
    q_last, kv_last = project([third], maps_biases, proteins, [q_three])
    kv_last = exchange_keys(kv_last)
    queries = [q_three, q_last]
    kv_pieces = [stack[i] for i in range(seq_size) for stack in (kv_three, kv_last)]
    token_pieces = [own_rows, first, second, third]
    far_outer = swap(pack_outer(own, [third]), *far_bit)
    pairs = [far_inner, far_outer]
    order = list(range(len(share_bits)))
    masks = [[0], [0]]
    for k, bits in enumerate(zip(order, order[::-1])):
        if k:
            pairs = stack_pairs(pairs)
        pairs = [(p, swap(p, *share_bits[bit])) for p, bit in zip(pairs, bits)]
        masks = [(have, [m | (1 << bit) for m in have]) for have, bit in zip(masks, bits)]
        if k < len(order) - 1:
            masks = [a + b for a, b in masks]
    far_tokens += [exchange_tokens(piece) for piece in token_pieces[1:]]

    stacked = [p for pair in pairs for p in pair[:1]]
    context, context_t, logsum = attend(pos, queries, kv_pieces, stacked)
    context = [c.reshape(rows, width) for c in context]
    context = [context[0]] + [swap(context[j], "heads", j) for j in range(1, groups)]
    normed, normed_low, first_unit, first_inverse, other_maps = merge_norm(
        heads.reshape(1).astype(jnp.int32),
        context,
        mergemap,
        merge_all,
        own_rows,
        small,
        [],
    )
    inner_t, outer_w, inner_b = join_units(
        own, [p for pair in pairs for p in pair], [m for pair in masks for m in pair], [normed_low]
    )

    normed_near, normed_across = swap(normed_low, *core_bit), swap(normed_low, *row_bit)
    near_act, near_slope, near_own, near_other = feed_forward(
        normed_low, normed_near, inner_t, outer_w, inner_b
    )
    normed_across = hold(normed_across, [near_act, *far_tokens[1]])
    normed_both = swap(normed_across, *core_bit)
    normed_rows = [normed_low, normed_near, normed_across, normed_both]
    far_act, far_slope, far_own, far_other = feed_forward(
        normed_across, normed_both, inner_t, outer_w, inner_b, [near_act]
    )
    (far_part,) = add_split(far_own, swap(far_other, *core_bit), [rows])
    far_sum = swap(far_part, *row_bit)
    own_at = (seq * groups + heads) * share + jnp.arange(share, dtype=jnp.int32)
    live = (own_at[None, :] < lengths[:, None]).astype(wide).reshape(rows, 1)
    layer_output, dsum_final, dbranch, final_sums = final_norm(
        normed,
        near_own,
        swap(near_other, *core_bit),
        far_sum,
        small,
        cotangent.reshape(rows, model),
        jnp.broadcast_to(live, (rows, 128)),
        far_tokens[2],
    )
    dbranch_near, dbranch_across = swap(dbranch, *core_bit), swap(dbranch, *row_bit)
    near_dinner, near_own, near_other = feed_backward(
        dbranch, dbranch_near, inner_t, outer_w, near_slope
    )
    dbranch_across = hold(dbranch_across, [near_dinner, *far_tokens[3]])
    dbranch_both = swap(dbranch_across, *core_bit)
    dbranch_rows = [dbranch, dbranch_near, dbranch_across, dbranch_both]
    hid_block = 2 * units
    last = len(share_bits) - 1
    numbers = lambda k, side: [m for m in range(shares) if (m >> k) & 1 == side]
    acts = [near_act, far_act]
    outer_send = weight_grad(acts, dbranch_rows, hid_block, numbers(last, 1), 0, [near_dinner])
    outer_got = swap(outer_send, *share_bits[last])
    far_dinner, far_own, far_other = feed_backward(
        dbranch_across,
        dbranch_both,
        inner_t,
        outer_w,
        far_slope,
        [outer_send, near_dinner],
    )
    (far_part,) = add_split(far_own, swap(far_other, *core_bit), [rows])
    far_sum = swap(far_part, *row_bit)

    dinners = [near_dinner, far_dinner]
    inner_send = weight_grad(dinners, normed_rows, hid_block, numbers(0, 1), 1, [far_part])
    inner_got = swap(inner_send, *share_bits[0])
    dfirst, dmerged, first_sums, dcontext = first_back(
        dsum_final,
        near_own,
        swap(near_other, *core_bit),
        far_sum,
        first_unit,
        first_inverse,
        small,
        mergemap,
        other_maps,
        [inner_send, *far_tokens[0]],
    )
    dcontext = [dcontext[0]] + [swap(dcontext[j], "heads", j) for j in range(1, groups)]
    dcontext = [d.reshape(proteins, share, width) for d in dcontext]
    core = bit_of(core_bit).reshape(1).astype(jnp.int32)
    merge_keep, merge_send = merge_grads(core, context, dmerged, final_sums, first_sums)
    merge_keep, merge_send, sums = merge_heads(
        final_sums, first_sums, merge_keep, swap(merge_send, *core_bit)
    )
    merge_got = swap(merge_send, *row_bit)
    merge_near, merge_send, sums = merge_far(merge_keep, merge_got, sums, [])
    merge_got = swap(merge_send, *far_bit)

    def shared_sum(hid, row_list, got, k, bias, waits):
        bits = [b for i, b in enumerate(share_bits) if i != k]
        if not bits:
            (keep,) = weight_grad(hid, row_list, hid_block, numbers(k, 0), bias, waits)
            return keep, got
        keep, send = weight_grad(hid, row_list, hid_block, numbers(k, 0), bias, waits, got)
        got = swap(send, *bits[-1])
        for bit in reversed(bits[:-1]):
            half = keep.shape[0] // 2
            keep, send = add_split(keep, got, [half, half])
            got = swap(send, *bit)
        return keep, got

    outer_sums = shared_sum(acts, dbranch_rows, outer_got, last, 0, [merge_send])
    inner_sums = shared_sum(dinners, normed_rows, inner_got, 0, 1, [merge_send])

    dqueries, dkv_by_seq = attend_back(
        pos, queries, dcontext, context_t, logsum, kv_pieces, [outer_sums[0], inner_sums[0], merge_send]
    )
    half = groups // 2
    dkv_by_seq = list(dkv_by_seq)
    dkv_by_seq[1::2] = gate(dkv_by_seq[1::2], [inner_sums[1], outer_sums[1], merge_got])
    own_pack, send_pack = pack_sums(units, *inner_sums, *outer_sums, [dqueries])
    far_pack = swap(send_pack, *far_bit)
    dkv_parts = [
        add_split(dkv_by_seq[i], swap(dkv_by_seq[i + 1], *core_bit), [groups])[0]
        for i in range(0, seq_size, 2)
    ]
    pairs = list(zip(dkv_parts, [seq_tokens[i] for i in range(0, seq_size, 2)]))
    slot_grads = qkv_grads(slot_scalar, slots, dqueries, pairs, [send_pack])
    block = 3 * width // slots
    slot_send = slot_parts(
        slot_scalar,
        block,
        merge_units,
        slot_grads,
        swap(slot_grads[shares:], *core_bit),
        merge_near,
        merge_got,
        sums,
        [],
    )
    slot_got = [swap_slots(slot_send[m], m << 1) for m in range(1, shares)]
    parts = dkv_parts
    for k in reversed(range(len(seq_bits))):
        count = 1 << k
        got = [swap(parts[count + i], *seq_bits[k]) for i in range(count)]
        if k:
            parts = [add_split(parts[i], got[i], [groups])[0] for i in range(count)]

    got[:1] = gate(got[:1], slot_got)

    part_none, part_one, part_two, part_three = dtokens(
        dqueries, parts[0], got[0], maps, [slot_send[0]]
    )
    rest = swap(part_three, *row_bit)
    near = swap(part_one, *row_bit)
    out_pack, extra = slot_sum(slot_send[0], slot_send[-1], slot_got, [part_three])
    (far_send,) = add_split(part_two, rest, [rows], [out_pack])
    far = swap(far_send, *far_bit)

    (pack,) = add_split(own_pack, far_pack, [own_pack.shape[0]], [part_three])
    grads = lax.all_gather(pack, ("dp", "seq"))

    parts = [out_pack] + [swap_slots(out_pack, m << 1) for m in range(1, shares)]
    order = [m << 1 for m in range(shares)]
    q_grad, k_grad, v_grad, mergemap_grad, bias_rows = qkv_out(
        slot_scalar,
        parts + [swap(part, *core_bit) for part in parts],
        order + [m | 1 for m in order],
        block,
        width,
    )
    tokens_grad = kernel_call(
        tokens_kernel, "tokens_grad", [dfirst, part_none, near, far], [((rows, model), low)]
    )[0]
    innermap_grad, outermap_grad, innerbias_grad = feed_out(grads, units)
    innerbias_grad = innerbias_grad.reshape(-1)
    bias_grads = bias_rows[:, :block].reshape(-1)
    shape = tokens.shape
    return (
        layer_output.reshape(shape),
        tokens_grad.reshape(shape),
        q_grad,
        bias_grads[:width],
        k_grad,
        v_grad,
        bias_grads[2 * width :],
        mergemap_grad,
        extra[3],
        extra[4],
        extra[5],
        innermap_grad,
        innerbias_grad,
        outermap_grad,
        extra[0],
        extra[1],
        extra[2],
    )


def solution(mesh):
    return jax.shard_map(
        shards,
        mesh=mesh,
        in_specs=(
            P("dp", ("seq", "heads"), None),
            P(None, "heads"),
            P("heads"),
            P(None, "heads"),
            P(None, "heads"),
            P("heads"),
            P("heads", None),
            P(),
            P(),
            P(),
            P(None, "heads"),
            P("heads"),
            P("heads", None),
            P(),
            P(),
            P(),
            P("dp"),
            P("dp", ("seq", "heads"), None),
        ),
        out_specs=(
            P("dp", ("seq", "heads"), None),
            P("dp", ("seq", "heads"), None),
            P(None, "heads"),
            P("heads"),
            P(None, "heads"),
            P(None, "heads"),
            P("heads"),
            P("heads", None),
            P(),
            P(),
            P(),
            P(None, "heads"),
            P("heads"),
            P("heads", None),
            P(),
            P(),
            P(),
        ),
        check_vma=False,
    )
```

```python
import functools

import jax
import jax.numpy as jnp
from jax import lax
from jax.experimental import pallas as pl
from jax.experimental.pallas import tpu as pltpu
from jax.sharding import PartitionSpec as P

HEAD_DIM = 64


epsilon = 1e-06
score_scale = 0.125
masked_score = -1000000000.0
low = jnp.bfloat16
wide = jnp.float32
vmem_bytes = 48 * 1024 * 1024


def dot(a, b):
    return jnp.dot(a, b, preferred_element_type=wide)


def dot_nt(a, b):
    return lax.dot_general(a, b, (((1,), (1,)), ((), ())), preferred_element_type=wide)


def dot_tn(a, b):
    return lax.dot_general(a, b, (((0,), (0,)), ((), ())), preferred_element_type=wide)


def swap(value, axis, stride):
    size = lax.axis_size(axis)
    return lax.ppermute(value, axis, [(i, i ^ stride) for i in range(size)])


def swap_slots(value, mask):
    size = lax.axis_size("dp") * lax.axis_size("seq")
    return lax.ppermute(value, ("dp", "seq"), [(i, i ^ mask) for i in range(size)])


def bit_of(bit):
    axis, stride = bit
    return (lax.axis_index(axis) // stride) % 2


def add_low(a, b):
    return (a.astype(wide) + b.astype(wide)).astype(low)


def params(mebibytes):
    return pltpu.CompilerParams(vmem_limit_bytes=mebibytes * 1024 * 1024)


in_vmem = pl.BlockSpec(memory_space=pltpu.VMEM)
in_smem = pl.BlockSpec(memory_space=pltpu.SMEM)
anywhere = pl.BlockSpec(memory_space=pl.ANY)
in_hbm = pl.BlockSpec(memory_space=pltpu.HBM)
hbm = True
kernels_alone = ("attend", "attend_back", "merge_norm", "project", "join_units", "stack_pairs")


def kernel_call(
    body, name, arrays, out, scalars=(), scratch=(), mebibytes=16, waits=(), far_in=(), local=(), flops=1
):
    ns, na, nw, no, nl = len(scalars), len(arrays), len(waits), len(out), len(local)
    alone = name in kernels_alone
    far_in = [i for i in range(na) if alone and (far_in is hbm or i in far_in)]
    far_out = [i for i, o in enumerate(out) if alone and len(o) > 2 and o[2] is hbm]
    own_out = [i for i, o in enumerate(out) if len(o) > 2 and o[2] == "kernel"]
    buffers = [pltpu.VMEM(arrays[i].shape, arrays[i].dtype) for i in far_in]
    buffers += [pltpu.VMEM(out[i][0], out[i][1]) for i in far_out]
    count = len(buffers)

    def whole(*refs):
        here = list(refs[: ns + na])
        at = ns + na + nw
        kept, outs, rest = refs[at : at + nl], list(refs[at + nl : at + nl + no]), refs[at + nl + no :]
        rest, (*held_refs, sems) = (rest[: len(rest) - count - 1], rest[len(rest) - count - 1 :])
        copies = []
        for k, i in enumerate(far_in):
            copies.append(pltpu.make_async_copy(here[ns + i], held_refs[k], sems.at[k]))
            copies[-1].start()
            here[ns + i] = held_refs[k]
        for copy in copies:
            copy.wait()
        copies = []
        for k, i in enumerate(far_out, len(far_in)):
            copies.append(pltpu.make_async_copy(held_refs[k], outs[i], sems.at[k]))
            outs[i] = held_refs[k]
        body(*here, *kept, *outs, *rest)
        for copy in copies:
            copy.start()
        for copy in copies:
            copy.wait()

    return pl.pallas_call(
        whole,
        in_specs=[in_smem] * ns
        + [in_hbm if i in far_in else in_vmem for i in range(na)]
        + [anywhere] * nw
        + [in_hbm] * nl,
        out_specs=[in_hbm if i in far_out + own_out else in_vmem for i in range(no)],
        out_shape=[jax.ShapeDtypeStruct(o[0], o[1]) for o in out],
        scratch_shapes=list(scratch) + buffers + [pltpu.SemaphoreType.DMA((max(count, 1),))],
        compiler_params=params(60 if alone else mebibytes),
        cost_estimate=pl.CostEstimate(flops=flops, bytes_accessed=1, transcendentals=0),
        name=name,
    )(*scalars, *arrays, *waits, *local)


def nothing(*refs):
    pass


def gate(values, waits):
    values = [pltpu.with_memory_space_constraint(v, pltpu.HBM) for v in values]
    found = pl.pallas_call(
        nothing,
        in_specs=[anywhere] * (len(values) + len(waits)),
        out_specs=[anywhere] * len(values),
        out_shape=[jax.ShapeDtypeStruct(v.shape, v.dtype) for v in values],
        input_output_aliases={i: i for i in range(len(values))},
        compiler_params=params(1),
        name="gate",
    )(*values, *waits)
    return list(found)


def pad16(count):
    return -(-count // 16) * 16


def place(pos, proteins, groups, share, i, j):
    seq, heads = pos[proteins], pos[proteins + 1]
    return pl.multiple_of(((seq ^ i) * groups + (heads ^ j)) * share, share)


def masked(scores, length, first):
    key_at = first + lax.broadcasted_iota(jnp.int32, scores.shape, 0)
    return jnp.where(key_at < length, scores, masked_score)


def chunks(n, block):
    return [(0, n - block, False)] * (n > block) + [(n - block, n, True)]


def piece_list(refs, groups):
    found, count = [], 0
    for ref in refs:
        for n in range(ref.shape[0]):
            found.append((ref, count // groups, count % groups, n))
            count += 1
    return found


def start_keys(pos, p, proteins, groups, kv_refs, kv_all, sems, blocks, block, wait):
    share = kv_refs[0].shape[2]
    for k, (ref, i, j, n) in enumerate(piece_list(kv_refs, groups)):
        at = place(pos, proteins, groups, share, i, j)

        @pl.when(at < blocks * block)
        def _():
            copy = pltpu.make_async_copy(ref.at[n, p], kv_all.at[p, pl.ds(at, share), :], sems.at[p])
            if wait:
                copy.wait()
            else:
                copy.start()


def query_rows(refs, p):
    found = [ref[n, p] for ref in refs for n in range(ref.shape[0])]
    return jnp.concatenate(found) * jnp.asarray(score_scale, low)


def attend_kernel(counts, pos, *refs):
    stacks, arrays, groups = counts
    q_refs, kv_refs = refs[:stacks], refs[stacks : stacks + arrays]
    ctx_refs, (ctx_t_ref, lse_ref, kv_all, sems) = refs[stacks + arrays : -4], refs[-4:]
    _, proteins, share, width = q_refs[0].shape
    total = kv_all.shape[1]
    block = min(256, total)
    heads = range(width // HEAD_DIM)

    def keys_of(p, wait):
        blocks = (pos[p] + block - 1) // block
        start_keys(pos, p, proteins, groups, kv_refs, kv_all, sems, blocks, block, wait)
        return blocks

    for p in range(proteins):
        keys_of(p, False)

    def protein(p, carry):
        length = pos[p]
        blocks = keys_of(p, True)

        def body(count):
            n = count * block
            queries = query_rows(q_refs, p)
            cols = lambda h: slice(h * HEAD_DIM, (h + 1) * HEAD_DIM)
            value_cols = lambda h: slice(width + h * HEAD_DIM, width + (h + 1) * HEAD_DIM)
            cuts = chunks(n, block)
            scores = [
                [dot_nt(kv_all[p, a:b, cols(h)], queries[:, cols(h)]) for a, b, _ in cuts]
                for h in heads
            ]
            weights, denominators = [], []
            for h in heads:
                found = [
                    masked(value, length, a) if last else value
                    for value, (a, _, last) in zip(scores[h], cuts)
                ]
                high = functools.reduce(
                    jnp.maximum, [jnp.max(value, axis=0, keepdims=True) for value in found]
                )
                found = [jnp.exp(value - high) for value in found]
                denominator = sum(jnp.sum(value, axis=0, keepdims=True) for value in found)
                lse_ref[p, h : h + 1, :] = high + jnp.log(denominator)
                weights.append([value.astype(low) for value in found])
                denominators.append(denominator)
            context_t = jnp.concatenate(
                [
                    sum(
                        dot_tn(kv_all[p, a:b, value_cols(h)], value)
                        for (a, b, _), value in zip(cuts, weights[h])
                    )
                    / denominators[h]
                    for h in heads
                ]
            )
            ctx_t_ref[p] = context_t
            context = context_t.T.astype(low)
            for j, ref in enumerate(ctx_refs):
                ref[p] = context[j * share : (j + 1) * share]

        for count in range(1, total // block + 1):
            pl.when(blocks == count)(functools.partial(body, count))
        return carry

    lax.fori_loop(0, proteins, protein, 0)


def attend_back_kernel(counts, pos, *refs):
    stacks, arrays, groups = counts
    q_refs, dctx_refs, refs = refs[:stacks], refs[stacks : stacks + groups], refs[stacks + groups :]
    ctx_t_ref, lse_ref, kv_refs, refs = refs[0], refs[1], refs[2 : 2 + arrays], refs[2 + arrays :]
    dq_ref, dkv_refs, (kv_all, dkv_all, dq_all, sems, out_sems) = refs[0], refs[1:-5], refs[-5:]
    _, proteins, share, width = q_refs[0].shape
    rows = groups * share
    total = kv_all.shape[1]
    block = min(256, total)
    heads = range(width // HEAD_DIM)

    def keys_of(p, wait):
        blocks = jnp.where(pos[proteins] * rows < pos[p], (pos[p] + block - 1) // block, 0)
        start_keys(pos, p, proteins, groups, kv_refs, kv_all, sems, blocks, block, wait)
        return blocks

    for p in range(proteins):
        keys_of(p, False)

    def results_of(p, wait):
        for j in range(groups):
            copy = pltpu.make_async_copy(
                dq_all.at[p, pl.ds(j * share, share), :], dq_ref.at[j, p], out_sems.at[p]
            )
            copy.wait() if wait else copy.start()
            for i, ref in enumerate(dkv_refs):
                at = place(pos, proteins, groups, share, i, j)
                copy = pltpu.make_async_copy(
                    dkv_all.at[p, pl.ds(at, share), :], ref.at[j, p], out_sems.at[p]
                )
                copy.wait() if wait else copy.start()

    def protein(p, carry):
        length = pos[p]
        blocks = keys_of(p, True)

        @pl.when(blocks == 0)
        def _():
            dkv_all[p] = jnp.zeros(dkv_all.shape[1:], low)
            dq_all[p] = jnp.zeros(dq_all.shape[1:], low)

        def body(count):
            n = count * block
            queries = query_rows(q_refs, p)
            dctx = jnp.concatenate([ref[p] for ref in dctx_refs])
            product = dctx.astype(wide).T * ctx_t_ref[p]
            cols = lambda h: slice(h * HEAD_DIM, (h + 1) * HEAD_DIM)
            value_cols = lambda h: slice(width + h * HEAD_DIM, width + (h + 1) * HEAD_DIM)
            deltas = [jnp.sum(product[cols(h), :], axis=0, keepdims=True) for h in heads]
            dq = []
            for a, b, last in chunks(n, block):
                scores = [dot_nt(kv_all[p, a:b, cols(h)], queries[:, cols(h)]) for h in heads]
                dprobs = [dot_nt(kv_all[p, a:b, value_cols(h)], dctx[:, cols(h)]) for h in heads]
                probs, dscores = [], []
                for h in heads:
                    score = masked(scores[h], length, a) if last else scores[h]
                    prob = jnp.exp(score - lse_ref[p, h : h + 1, :])
                    probs.append(prob.astype(low))
                    dscores.append((prob * (dprobs[h] - deltas[h])).astype(low))
                dv = [dot(probs[h], dctx[:, cols(h)]) for h in heads]
                dk = [dot(dscores[h], queries[:, cols(h)]) for h in heads]
                dq.append(
                    jnp.concatenate([dot_tn(kv_all[p, a:b, cols(h)], dscores[h]) for h in heads])
                )
                dkv_all[p, a:b, :width] = jnp.concatenate(dk, axis=1).astype(low)
                dkv_all[p, a:b, width:] = jnp.concatenate(dv, axis=1).astype(low)
            if n < total:
                dkv_all[p, n:, :] = jnp.zeros((total - n, 2 * width), low)
            dq_all[p] = (sum(dq).T * score_scale).astype(low)

        for count in range(1, total // block + 1):
            pl.when(blocks == count)(functools.partial(body, count))
        results_of(p, False)
        return carry

    lax.fori_loop(0, proteins, protein, 0)
    for p in range(proteins):
        results_of(p, True)


def attend(pos, queries, kv_pieces, waits):
    groups = sum(q.shape[0] for q in queries)
    _, proteins, share, width = queries[0].shape
    rows = groups * share
    total = share * sum(piece.shape[0] for piece in kv_pieces)
    found = kernel_call(
        functools.partial(attend_kernel, (len(queries), len(kv_pieces), groups)),
        "attend",
        queries,
        [((proteins, share, width), low, hbm)] * groups
        + [((proteins, width, rows), wide, hbm), ((proteins, 8, rows), wide, hbm)],
        scalars=[pos],
        scratch=[
            pltpu.VMEM((proteins, total, 2 * width), low),
            pltpu.SemaphoreType.DMA((proteins,)),
        ],
        mebibytes=32,
        far_in=hbm,
        local=kv_pieces,
        waits=waits,
        flops=int(1e10),
    )
    return found[:groups], found[groups], found[groups + 1]


def attend_back(pos, queries, dctx, ctx_t, lse, kv_pieces, waits):
    groups = len(dctx)
    _, proteins, share, width = queries[0].shape
    total = share * sum(piece.shape[0] for piece in kv_pieces)
    pieces = total // (groups * share)
    arrays = [*queries, *dctx, ctx_t, lse]
    found = kernel_call(
        functools.partial(attend_back_kernel, (len(queries), len(kv_pieces), groups)),
        "attend_back",
        arrays,
        [((groups, proteins, share, width), low, "kernel")]
        + [((groups, proteins, share, 2 * width), low, "kernel")] * pieces,
        scalars=[pos],
        scratch=[
            pltpu.VMEM((proteins, total, 2 * width), low),
            pltpu.VMEM((proteins, total, 2 * width), low),
            pltpu.VMEM((proteins, groups * share, width), low),
            pltpu.SemaphoreType.DMA((proteins,)),
            pltpu.SemaphoreType.DMA((proteins,)),
        ],
        mebibytes=32,
        far_in=[i for i in range(len(arrays)) if not 0 <= i - len(queries) < groups],
        local=kv_pieces,
        waits=waits,
        flops=int(2e10),
    )
    return found[0], found[1:]


def project_kernel(count, *refs):
    tok_refs, (qmap_ref, kmap_ref, vmap_ref, qbias_ref, vbias_ref, q_ref, kv_ref) = refs[:count], refs[count:]
    width = q_ref.shape[-1]
    for j, tok_ref in enumerate(tok_refs):
        shape = q_ref.shape[1:]
        queries = dot(tok_ref[...], qmap_ref[...]) + qbias_ref[...].astype(wide)
        q_ref[j] = queries.astype(low).reshape(shape)
        kv_ref[j, :, :, :width] = dot(tok_ref[...], kmap_ref[...]).astype(low).reshape(shape)
        values = dot(tok_ref[...], vmap_ref[...]) + vbias_ref[...].astype(wide)
        kv_ref[j, :, :, width:] = values.astype(low).reshape(shape)


def project(tok, maps, proteins, waits=()):
    width = maps[0].shape[1]
    share = tok[0].shape[0] // proteins
    return kernel_call(
        functools.partial(project_kernel, len(tok)),
        "project",
        [*tok, *maps],
        [
            ((len(tok), proteins, share, width), low, hbm),
            ((len(tok), proteins, share, 2 * width), low, hbm),
        ],
        waits=waits,
        far_in=hbm,
    )


def unit_of(values):
    centered = values - jnp.mean(values, axis=-1, keepdims=True)
    variance = jnp.mean(centered * centered, axis=-1, keepdims=True)
    inverse = lax.rsqrt(variance + epsilon)
    return centered * inverse, inverse


def norm_back(grad_rows, unitized, inverse, scales):
    scaled = grad_rows * scales
    grad_mean = jnp.mean(scaled, axis=-1, keepdims=True)
    cross_mean = jnp.mean(scaled * unitized, axis=-1, keepdims=True)
    return inverse * (scaled - grad_mean - unitized * cross_mean)


def steps(rows):
    size = 64 if rows % 64 == 0 else rows
    return [slice(at, at + size) for at in range(0, rows, size)]


def merge_kernel(groups, heads, *refs):
    ctx_refs, refs = refs[:groups], refs[groups:]
    own_map, maps_all, tok_ref, small_ref = refs[:4]
    normed_ref, low_ref, unit_ref, inv_ref, maps_ref = refs[4:]
    others = groups - 1
    slots, _, size, _ = maps_all.shape
    for j in range(others):
        for k in range(slots):
            maps_ref[j, k * size : (k + 1) * size, :] = maps_all[k, heads[0] ^ (j + 1)]
    merged = small_ref[0:1, :] + dot(ctx_refs[0][...], own_map[...])
    for j in range(others):
        merged += dot(ctx_refs[j + 1][...], maps_ref[j])
    unit_ref[...] = tok_ref[...].astype(wide) + merged
    for rows in steps(tok_ref.shape[0]):
        unit, inverse = unit_of(unit_ref[rows, :])
        normed = unit * small_ref[1:2, :] + small_ref[2:3, :]
        normed_ref[rows, :] = normed
        low_ref[rows, :] = normed.astype(low)
        unit_ref[rows, :] = unit
        inv_ref[rows, :] = jnp.broadcast_to(inverse, (inverse.shape[0], 128))


def merge_norm(heads, ctx, own_map, maps_all, tok, small, waits):
    rows, model = tok.shape
    groups = len(ctx)
    return kernel_call(
        functools.partial(merge_kernel, groups),
        "merge_norm",
        [*ctx, own_map, maps_all, tok, small],
        [
            ((rows, model), wide, hbm),
            ((rows, model), low, hbm),
            ((rows, model), wide, hbm),
            ((rows, 128), wide, hbm),
            ((groups - 1, *own_map.shape), low, hbm),
        ],
        scalars=[heads],
        waits=waits,
        far_in=hbm,
    )


def final_kernel(*refs):
    normed_ref, near_ref, core_ref, far_ref, small_ref, cot_ref, live_ref = refs[:7]
    out_ref, dsum_ref, dbranch_ref, sums_ref = refs[7:]
    gain = small_ref[4:5, :]
    gain_sum = shift_sum = bias_sum = 0.0
    for rows in steps(normed_ref.shape[0]):
        branch = near_ref[rows, :].astype(wide) + core_ref[rows, :].astype(wide)
        branch = branch + far_ref[rows, :].astype(wide) + small_ref[3:4, :]
        unit, inverse = unit_of(normed_ref[rows, :] + branch)
        out_ref[rows, :] = (unit * gain + small_ref[5:6, :]).astype(low)
        grad = cot_ref[rows, :].astype(wide) * live_ref[rows, 0:1]
        dsum = norm_back(grad, unit, inverse, gain)
        dsum_ref[rows, :] = dsum
        dbranch = dsum.astype(low)
        dbranch_ref[rows, :] = dbranch
        gain_sum += jnp.sum(grad * unit, axis=0, keepdims=True)
        shift_sum += jnp.sum(grad, axis=0, keepdims=True)
        bias_sum += jnp.sum(dbranch.astype(wide), axis=0, keepdims=True)
    sums_ref[...] = jnp.zeros(sums_ref.shape, wide)
    sums_ref[0:1, :] = bias_sum
    sums_ref[1:2, :] = gain_sum
    sums_ref[2:3, :] = shift_sum


def final_norm(normed, near, core, across, small, cot, live, waits):
    rows, model = normed.shape
    return kernel_call(
        final_kernel,
        "final_norm",
        [normed, near, core, across, small, cot, live],
        [
            ((rows, model), low, hbm),
            ((rows, model), wide, hbm),
            ((rows, model), low),
            ((8, model), wide, hbm),
        ],
        far_in=[0, 4, 5, 6],
        waits=waits,
    )


def first_back_kernel(groups, *refs):
    dsum_ref, near_ref, core_ref, far_ref, unit_ref, inv_ref, small_ref, own_map, maps_ref = refs[:9]
    dfirst_ref, dmerged_ref, sums_ref = refs[9:12]
    dctx_refs = refs[12:]
    gain = small_ref[1:2, :]
    gain_sum = shift_sum = bias_sum = 0.0
    for rows in steps(dsum_ref.shape[0]):
        grad = near_ref[rows, :].astype(wide) + core_ref[rows, :].astype(wide)
        grad = dsum_ref[rows, :] + grad + far_ref[rows, :].astype(wide)
        unit = unit_ref[rows, :]
        dfirst = norm_back(grad, unit, inv_ref[rows, 0:1], gain)
        dfirst_ref[rows, :] = dfirst
        dmerged = dfirst.astype(low)
        dmerged_ref[rows, :] = dmerged
        gain_sum += jnp.sum(grad * unit, axis=0, keepdims=True)
        shift_sum += jnp.sum(grad, axis=0, keepdims=True)
        bias_sum += jnp.sum(dmerged.astype(wide), axis=0, keepdims=True)
    for j in range(groups):
        merge_map = maps_ref[j - 1] if j else own_map[...]
        dctx_refs[j][...] = dot_nt(dmerged_ref[...], merge_map).astype(low)
    sums_ref[...] = jnp.zeros(sums_ref.shape, wide)
    sums_ref[3:4, :] = bias_sum
    sums_ref[4:5, :] = gain_sum
    sums_ref[5:6, :] = shift_sum


def first_back(dsum, near, core, across, unit, inverse, small, own_map, maps, waits):
    rows, model = dsum.shape
    groups, width = maps.shape[0] + 1, own_map.shape[0]
    found = kernel_call(
        functools.partial(first_back_kernel, groups),
        "first_back",
        [dsum, near, core, across, unit, inverse, small, own_map, maps],
        [((rows, model), wide, hbm), ((rows, model), low), ((8, model), wide, hbm)]
        + [((rows, width), low)] * groups,
        waits=waits,
        far_in=[0, 4, 5, 6, 7, 8],
    )
    return found[0], found[1], found[2], found[3:]


def forward_kernel(a_ref, b_ref, inner_ref, outer_ref, bias_ref, act_ref, slope_ref, own_ref, other_ref):
    rows = a_ref.shape[0]
    for ref, out, at in ((a_ref, own_ref, 0), (b_ref, other_ref, rows)):
        pre = dot_nt(ref[...], inner_ref[...]) + bias_ref[...]
        upper = 0.5 + 0.5 * lax.erf(pre * 0.7071067811865476)
        active = (pre * upper).astype(low)
        slope = upper + pre * (0.3989422804014327 * jnp.exp(-0.5 * pre * pre))
        act_ref[at : at + rows, :] = active
        slope_ref[at : at + rows, :] = slope.astype(low)
        out[...] = dot(active, outer_ref[...]).astype(low)


def feed_forward(a, b, inner, outer, bias, waits=()):
    rows, model = a.shape
    hidden = inner.shape[0]
    return kernel_call(
        forward_kernel,
        "feed_forward",
        [a, b, inner, outer, bias],
        [((2 * rows, hidden), low, hbm)] * 2 + [((rows, model), low)] * 2,
        waits=waits,
        far_in=[0, 1],
    )


def backward_kernel(a_ref, b_ref, inner_ref, outer_ref, slope_ref, dinner_ref, own_ref, other_ref):
    rows = a_ref.shape[0]
    for ref, out, at in ((a_ref, own_ref, 0), (b_ref, other_ref, rows)):
        dactive = dot_nt(ref[...], outer_ref[...])
        dinner = (dactive * slope_ref[at : at + rows, :].astype(wide)).astype(low)
        dinner_ref[at : at + rows, :] = dinner
        out[...] = dot(dinner, inner_ref[...]).astype(low)


def feed_backward(a, b, inner, outer, slope, waits=()):
    rows, model = a.shape
    hidden = inner.shape[0]
    return kernel_call(
        backward_kernel,
        "feed_backward",
        [a, b, inner, outer, slope],
        [((2 * rows, hidden), low, hbm)] + [((rows, model), low)] * 2,
        waits=waits,
        far_in=[4],
    )


def grad_kernel(numbers, block, bias, split, *refs):
    hid, row_refs, refs = refs[:2], refs[2:6], refs[6:]
    got_ref, out_refs = (refs[0], refs[1:]) if split else (None, refs)
    model = out_refs[0].shape[-1]
    half = len(numbers) // len(out_refs)
    for k, number in enumerate(numbers):
        cols = slice(number * block, (number + 1) * block)
        total = sums = 0.0
        for i, ref in enumerate(hid):
            rows = ref.shape[0] // 2
            total += dot_tn(ref[:rows, cols], row_refs[2 * i][...])
            total += dot_tn(ref[rows:, cols], row_refs[2 * i + 1][...])
            if bias:
                sums += jnp.sum(ref[:, cols].astype(wide), axis=0, keepdims=True)
        out_ref, at = out_refs[k // half], k % half
        if split:
            total += got_ref[k, :block, :].astype(wide)
        out_ref[at, :block, :] = total.astype(low)
        if bias:
            sums = jnp.pad(sums, ((0, 15), (0, model - block)))
            if split:
                sums += got_ref[k, block:, :].astype(wide)
            out_ref[at, block:, :] = sums.astype(low)


def weight_grad(hid, row_list, block, numbers, bias, waits, got=None):
    model = row_list[0].shape[1]
    split = got is not None
    count = len(numbers) // (1 + split)
    found = kernel_call(
        functools.partial(grad_kernel, numbers, block, bias, split),
        "weight_grad",
        [*hid, *row_list] + [got] * split,
        [((count, block + 16 * bias, model), low)] * (1 + split),
        waits=waits,
    )
    return found if split else found[0]


def units_kernel(units, shares, slot, inner_ref, outer_ref, bias_ref, own_inner, own_outer, own_bias):
    for m in range(shares):
        at = pl.multiple_of((slot[0] ^ (m << 1)) * units, units)
        own_inner[m] = inner_ref[:, pl.ds(at, units)].T
        own_outer[m] = outer_ref[pl.ds(at, units), :]
        own_bias[m] = jnp.broadcast_to(bias_ref[:, pl.ds(at, units)], (16, units))


def own_units(slot, shares, innermap, outermap, innerbias, waits):
    model = innermap.shape[0]
    units = innermap.shape[1] // (2 * shares)
    if units % 128:
        found = []
        for m in range(shares):
            at = (slot[0] ^ (m << 1)) * units
            inner = lax.dynamic_slice_in_dim(innermap, at, units, 1).T
            outer = lax.dynamic_slice_in_dim(outermap, at, units, 0)
            bias = lax.dynamic_slice_in_dim(innerbias, at, units, 1)
            found.append((inner, outer, jnp.broadcast_to(bias, (16, units))))
        return [jnp.stack(pieces) for pieces in zip(*found)]
    return kernel_call(
        functools.partial(units_kernel, units, shares),
        "own_units",
        [innermap, outermap, innerbias],
        [((shares, units, model), low, hbm)] * 2 + [((shares, 16, units), innerbias.dtype, hbm)],
        scalars=[slot],
        waits=waits,
        far_in=[0, 1],
    )


def pack_inner_kernel(own_inner, own_bias, pack_ref):
    units = own_inner.shape[1]
    pack_ref[0, :units, :] = own_inner[0]
    pack_ref[0, units:, :] = jnp.zeros((16, pack_ref.shape[2]), low)
    pack_ref[0, units:, :units] = own_bias[0]


def pack_outer_kernel(own_outer, pack_ref):
    pack_ref[0] = own_outer[0]


def pack_inner(own):
    _, units, model = own[0].shape
    out = [((1, units + 16, model), low)]
    return kernel_call(pack_inner_kernel, "pack_inner", [own[0], own[2]], out)[0]


def pack_outer(own, waits):
    _, units, model = own[1].shape
    out = [((1, units, model), low)]
    return kernel_call(pack_outer_kernel, "pack_outer", [own[1]], out, waits=waits)[0]


def stack_kernel(*refs):
    count = len(refs) // 3
    for k in range(count):
        a_ref, b_ref, out_ref = refs[2 * k], refs[2 * k + 1], refs[2 * count + k]
        out_ref[: a_ref.shape[0]] = a_ref[...]
        out_ref[a_ref.shape[0] :] = b_ref[...]


def stack_pairs(pairs):
    return kernel_call(
        stack_kernel,
        "stack_pairs",
        [value for pair in pairs for value in pair],
        [((2 * a.shape[0], *a.shape[1:]), a.dtype) for a, _ in pairs],
    )


def join_kernel(units, masks, own_inner, own_outer, own_bias, *refs):
    parts, (inner_ref, outer_ref, bias_ref) = refs[:-3], refs[-3:]
    for m in range(own_inner.shape[0]):
        at, far = 2 * m * units, (2 * m + 1) * units
        inner_ref[at:far, :] = own_inner[m]
        outer_ref[at:far, :] = own_outer[m]
        bias_ref[:, at:far] = own_bias[m, 0:1, :].astype(wide)
    for which, (ref, order) in enumerate(zip(parts, masks)):
        for k, m in enumerate(order):
            far = (2 * m + 1) * units
            if which < 2:
                inner_ref[far : far + units, :] = ref[k, :units, :]
                bias_ref[:, far : far + units] = ref[k, units : units + 16, :units].astype(wide)[:1]
            else:
                outer_ref[far : far + units, :] = ref[k]


def join_units(own, parts, masks, waits):
    shares, units, model = own[0].shape
    hidden = 2 * shares * units
    return kernel_call(
        functools.partial(join_kernel, units, masks),
        "join_units",
        [*own, *parts],
        [((hidden, model), low)] * 2 + [((1, hidden), wide)],
        waits=waits,
        far_in=hbm,
    )


def slot_order(number, bits):
    return ((number & 1) << (bits - 1)) | (number >> 1)


def qkv_kernel(counts, slots, slot, *refs):
    out_ref, q_all, kv_all = refs[-3:]
    dq_ref, refs = refs[0], refs[1:-3]
    width, model = dq_ref.shape[-1], out_ref.shape[-1]
    q_all[...] = dq_ref[...].reshape(q_all.shape)
    q_sum = jnp.sum(q_all[...].astype(wide), axis=0, keepdims=True)
    q_grad = kv_grad = kv_sum = 0.0
    for i, count in enumerate(counts):
        dkv_ref, tok_refs, refs = refs[0], refs[1 : 1 + count], refs[1 + count :]
        kv_all[...] = dkv_ref[...].reshape(kv_all.shape)
        kv_sum += jnp.sum(kv_all[...].astype(wide), axis=0, keepdims=True)
        at = 0
        for tok_ref in tok_refs:
            there = slice(at, at + tok_ref.shape[0])
            at += tok_ref.shape[0]
            kv_grad += dot_tn(kv_all[there, :], tok_ref[...])
            if i == 0:
                q_grad += dot_tn(q_all[there, :], tok_ref[...])
    grad = jnp.concatenate([q_grad, kv_grad]).astype(low)
    sums = jnp.concatenate([q_sum, kv_sum], axis=1)
    bits = slots.bit_length() - 1
    block = 3 * width // slots
    for b in range(slots):
        at = slot_order(slot[0] ^ b, bits)
        out_ref[at, :block, :] = grad[b * block : (b + 1) * block]
        line = jnp.pad(sums[:, b * block : (b + 1) * block], ((0, 15), (0, model - block)))
        out_ref[at, pad16(block) :, :] = line.astype(low)


def qkv_grads(slot, slots, dq, pairs, waits):
    model = pairs[0][1][0].shape[-1]
    groups, width = dq.shape[0], dq.shape[-1]
    total = dq.size // width
    far_at, at = [], 1
    for dkv, tok in pairs:
        far_at += range(at + 1, at + 1 + len(tok))
        at += 1 + len(tok)
    return kernel_call(
        functools.partial(qkv_kernel, [len(tok) for _, tok in pairs], slots),
        "qkv_grads",
        [dq] + [a for dkv, tok in pairs for a in (dkv, *tok)],
        [((slots, pad16(3 * width // slots) + 16, model), low)],
        far_in=far_at,
        scalars=[slot],
        waits=waits,
        scratch=[pltpu.VMEM((total, width), low), pltpu.VMEM((total, 2 * width), low)],
        mebibytes=24,
    )[0]


def hold_kernel(value_ref, out_ref):
    out_ref[...] = value_ref[...]


def hold(value, waits):
    out = [(value.shape, value.dtype)]
    return kernel_call(hold_kernel, "hold", [value], out, waits=waits)[0]


def add_kernel(a_ref, b_ref, *out_refs):
    at = 0
    for ref in out_refs:
        there = slice(at, at + ref.shape[0])
        at += ref.shape[0]
        ref[...] = (a_ref[there].astype(wide) + b_ref[there].astype(wide)).astype(ref.dtype)


def add_split(a, b, counts, waits=(), kind=low):
    out = [((count, *a.shape[1:]), kind) for count in counts]
    return kernel_call(add_kernel, "add_split", [a, b], out, waits=waits)


def dtokens_kernel(dq_ref, own_ref, got_ref, q_ref, k_ref, v_ref, *out_refs):
    width = dq_ref.shape[-1]
    rows = dq_ref.shape[1] * dq_ref.shape[2]
    for j, ref in enumerate(out_refs):
        dkv = (own_ref[j].astype(wide) + got_ref[j].astype(wide)).astype(low)
        dkv = dkv.reshape(rows, 2 * width)
        total = dot_nt(dq_ref[j].reshape(rows, width), q_ref[...])
        total += dot_nt(dkv[:, :width], k_ref[...]) + dot_nt(dkv[:, width:], v_ref[...])
        ref[...] = total.astype(ref.dtype)


def dtokens(dq, own, got, maps, waits):
    rows, model = dq.shape[1] * dq.shape[2], maps[0].shape[0]
    return kernel_call(
        dtokens_kernel,
        "dtokens",
        [dq, own, got, *maps],
        [((rows, model), wide), ((rows, model), low)] * (dq.shape[0] // 2),
        waits=waits,
    )


def tokens_kernel(dfirst_ref, part_ref, near_ref, far_ref, out_ref):
    total = dfirst_ref[...] + part_ref[...] + near_ref[...].astype(wide)
    out_ref[...] = (total + far_ref[...].astype(wide)).astype(low)


def pack_sums_kernel(units, inner_ref, inner_got, outer_ref, outer_got, own_ref, send_ref):
    model = own_ref.shape[1]
    inner = inner_ref[0].astype(wide) + inner_got[0].astype(wide)
    outer = outer_ref[0].astype(wide) + outer_got[0].astype(wide)
    sums = inner[2 * units :, : 2 * units].astype(low)
    for k, ref in enumerate((own_ref, send_ref)):
        there = slice(k * units, (k + 1) * units)
        ref[:units, :] = inner[there].astype(low)
        ref[units : 2 * units, :] = outer[there].astype(low)
        ref[2 * units :, :] = jnp.zeros((16, model), low)
        ref[2 * units :, :units] = sums[:, there]


def pack_sums(units, inner, inner_got, outer, outer_got, waits):
    model = inner.shape[-1]
    return kernel_call(
        functools.partial(pack_sums_kernel, units),
        "pack_sums",
        [inner, inner_got, outer, outer_got],
        [((2 * units + 16, model), low)] * 2,
        waits=waits,
    )


def merge_grad_kernel(groups, core, *refs):
    ctx_refs, (dmerged_ref, a_ref, b_ref, keep_ref, send_ref, grad_all) = refs[:groups], refs[groups:]
    half = keep_ref.shape[1]
    for j, ref in enumerate(ctx_refs):
        grad_all[...] = dot_tn(ref[...], dmerged_ref[...]).astype(low)
        keep = pl.multiple_of(core[0] * half, half)
        send = pl.multiple_of((1 - core[0]) * half, half)
        keep_ref[j] = grad_all[pl.ds(keep, half), :]
        send_ref[j * half : (j + 1) * half, :] = grad_all[pl.ds(send, half), :]
    sums = a_ref[...] + b_ref[...]
    send_ref[groups * half :, :] = jnp.concatenate([sums, jnp.zeros_like(sums)]).astype(low)


def merge_grads(core, ctx, dmerged, a, b):
    rows, width = ctx[0].shape
    model = dmerged.shape[1]
    groups, half = len(ctx), width // 2
    return kernel_call(
        functools.partial(merge_grad_kernel, groups),
        "merge_grads",
        [*ctx, dmerged, a, b],
        [((groups, half, model), low), ((groups * half + 16, model), low)],
        far_in=[i for i in range(groups + 3) if i != groups],
        scalars=[core],
        scratch=[pltpu.VMEM((width, model), low)],
    )


def merge_heads_kernel(groups, a_ref, b_ref, keep_ref, got_ref, near_ref, send_ref, sums_ref):
    half = keep_ref.shape[1]
    total = lambda j: keep_ref[j].astype(wide) + got_ref[j * half : (j + 1) * half, :].astype(wide)
    for k in range(groups // 2):
        near_ref[k] = total(2 * k).astype(low)
        send_ref[k * half : (k + 1) * half, :] = total(2 * k + 1).astype(low)
    sums = a_ref[...] + b_ref[...] + got_ref[groups * half : groups * half + 16, :].astype(wide)[:8]
    sums_ref[...] = sums
    at = groups // 2 * half
    send_ref[at:, :] = jnp.concatenate([sums, jnp.zeros_like(sums)]).astype(low)


def merge_heads(a, b, keep, got):
    groups, half, model = keep.shape
    count = groups // 2
    return kernel_call(
        functools.partial(merge_heads_kernel, groups),
        "merge_heads",
        [a, b, keep, got],
        [((count, half, model), low), ((count * half + 16, model), low), ((8, model), wide)],
    )


def merge_far_kernel(keep_ref, got_ref, sums_ref, near_ref, send_ref, out_sums_ref):
    half = keep_ref.shape[1]
    near_ref[...] = (keep_ref[0].astype(wide) + got_ref[:half, :].astype(wide)).astype(low)
    far = keep_ref[1].astype(wide) + got_ref[half : 2 * half, :].astype(wide)
    send_ref[:half, :] = far.astype(low)
    sums = sums_ref[...] + got_ref[2 * half :, :].astype(wide)[:8]
    out_sums_ref[...] = sums
    send_ref[half:, :] = jnp.concatenate([sums, jnp.zeros_like(sums)]).astype(low)


def merge_far(keep, got, sums, waits):
    _, half, model = keep.shape
    return kernel_call(
        merge_far_kernel,
        "merge_far",
        [keep, got, sums],
        [((half, model), low), ((half + 16, model), low), ((8, model), wide)],
        waits=waits,
    )


def slots_kernel(block, size, slot, grad_ref, core_ref, near_ref, far_ref, sums_ref, *refs):
    own_ref, send_refs, (out_sums_ref, rows_all) = refs[0], refs[1:-2], refs[-2:]
    shares = len(send_refs) + 1
    half = near_ref.shape[0]
    merged = (near_ref[...].astype(wide) + far_ref[:half, :].astype(wide)).astype(low)
    for k in range(shares):
        rows_all[k] = merged[k * size : (k + 1) * size]
    sums = sums_ref[...] + far_ref[half:, :].astype(wide)[:8]
    out_sums_ref[...] = sums
    start = pad16(block) + 16
    for m, ref in enumerate((own_ref, *send_refs)):
        ref[:start, :] = (grad_ref[m].astype(wide) + core_ref[m].astype(wide)).astype(low)
        ref[start : start + size, :] = rows_all[(slot[0] >> 1) ^ m]
        if m:
            both = jnp.concatenate([sums, jnp.zeros_like(sums)]).astype(low)
            ref[start + pad16(size) :, :] = both


def slot_parts(slot, block, size, grads, core, near, far, sums, waits):
    shares, _, model = core.shape
    rows = pad16(block) + 16 + pad16(size)
    return kernel_call(
        functools.partial(slots_kernel, block, size),
        "slot_parts",
        [grads, core, near, far, sums],
        [((rows, model), low)]
        + [((rows + 16, model), low)] * (shares - 1)
        + [((8, model), wide)],
        scalars=[slot],
        scratch=[pltpu.VMEM((shares, size, model), low)],
        waits=waits,
    )


def slot_sum_kernel(own_ref, sums_ref, *refs):
    got_refs, (out_ref, out_sums_ref) = refs[:-2], refs[-2:]
    rows = own_ref.shape[0]
    total, sums = own_ref[...].astype(wide), sums_ref[...]
    for ref in got_refs:
        total += ref[:rows, :].astype(wide)
        sums += ref[rows:, :].astype(wide)[:8]
    out_ref[...] = total.astype(low)
    out_sums_ref[...] = sums


def slot_sum(own, sums, got, waits):
    return kernel_call(
        slot_sum_kernel,
        "slot_sum",
        [own, sums, *got],
        [(own.shape, low), (sums.shape, wide)],
        waits=waits,
    )


def feed_out_kernel(units, grads_ref, inner_ref, outer_ref, bias_ref, here, inner, outer, bias, sems):
    slots, rows, model = grads_ref.shape
    copies = [pltpu.make_async_copy(grads_ref.at[k], here.at[k], sems.at[0, k]) for k in range(slots)]
    for copy in copies:
        copy.start()
    done = []
    for k, copy in enumerate(copies):
        copy.wait()
        cols = slice(k * units, (k + 1) * units)
        inner[:, cols] = here[k, :units, :].astype(wide).T
        outer[cols, :] = here[k, units : 2 * units, :].astype(wide)
        bias[k : k + 1, :] = here[k, 2 * units : 2 * units + 16, :units].astype(wide)[:1]
        done.append(pltpu.make_async_copy(inner.at[:, cols], inner_ref.at[:, cols], sems.at[1, k]))
        done.append(pltpu.make_async_copy(outer.at[cols, :], outer_ref.at[cols, :], sems.at[2, k]))
        done[-2].start()
        done[-1].start()
    done.append(pltpu.make_async_copy(bias, bias_ref, sems.at[0, 0]))
    done[-1].start()
    for copy in done:
        copy.wait()


def feed_out(grads, units):
    slots, rows, model = grads.shape
    hidden = slots * units
    if units % 128:
        inner = grads[:, :units].reshape(hidden, model).astype(wide).T
        outer = grads[:, units : 2 * units].reshape(hidden, model).astype(wide)
        return inner, outer, grads[:, 2 * units, :units].astype(wide)
    shapes = [(model, hidden), (hidden, model), (slots, units)]
    return pl.pallas_call(
        functools.partial(feed_out_kernel, units),
        in_specs=[in_hbm],
        out_specs=[in_hbm] * 3,
        out_shape=[jax.ShapeDtypeStruct(shape, wide) for shape in shapes],
        scratch_shapes=[pltpu.VMEM(grads.shape, low)]
        + [pltpu.VMEM(shape, wide) for shape in shapes]
        + [pltpu.SemaphoreType.DMA((3, slots))],
        compiler_params=params(60),
        name="feed_out",
    )(grads)


def qkv_out_kernel(block, order, slot, *refs):
    parts, refs = refs[: len(order)], refs[len(order) :]
    q_ref, k_ref, v_ref, merge_ref, bias_ref, rows_all, merge_all = refs
    start, size = pad16(block), merge_all.shape[1]
    width = q_ref.shape[1]
    slots = merge_all.shape[0]
    for mask, part in zip(order, parts):
        at = slot[0] ^ mask
        rows_all[at] = part[:block, :]
        bias_ref[pl.ds(at, 1), :] = part[start : start + 16, :].astype(wide)[:1]
        at = (at & 1) * (slots // 2) + (at >> 1)
        merge_all[at] = part[start + 16 : start + 16 + size, :]
    grad = rows_all[...].reshape(3 * width, -1)
    for i, ref in enumerate((q_ref, k_ref, v_ref)):
        ref[...] = grad[i * width : (i + 1) * width].astype(wide).T
    merge_ref[...] = merge_all[...].reshape(merge_ref.shape).astype(wide)


def qkv_out(slot, parts, order, block, width):
    model = parts[0].shape[-1]
    slots = 3 * width // block
    size = width // slots
    return kernel_call(
        functools.partial(qkv_out_kernel, block, order),
        "qkv_out",
        parts,
        [((model, width), wide)] * 3 + [((width, model), wide), ((slots, model), wide)],
        scalars=[slot],
        scratch=[pltpu.VMEM((slots, block, model), low), pltpu.VMEM((slots, size, model), low)],
    )


def shards(
    tokens,
    querymap,
    querybias,
    keymap,
    valuemap,
    valuebias,
    mergemap,
    mergebias,
    normgain,
    normshift,
    innermap,
    innerbias,
    outermap,
    outerbias,
    finalgain,
    finalshift,
    lengths,
    cotangent,
):
    proteins, share, model = tokens.shape
    groups = lax.axis_size("heads")
    rows = proteins * share
    width = querymap.shape[1]
    seq, heads = lax.axis_index("seq"), lax.axis_index("heads")
    seq_size, dp_size = lax.axis_size("seq"), lax.axis_size("dp")
    pos = jnp.concatenate([lengths, jnp.stack([seq, heads]).astype(jnp.int32)])
    core_bit, row_bit, far_bit = ("seq", 1), ("heads", 1), ("heads", 2)
    seq_bits = [("seq", 1 << k) for k in range(1, seq_size.bit_length() - 1)]
    share_bits = seq_bits + [("dp", 1 << k) for k in range(dp_size.bit_length() - 1)]
    slot_bits = [core_bit] + share_bits
    slots = 1 << len(slot_bits)
    shares = slots // 2
    slot = lax.axis_index("dp") * seq_size + seq
    units = innermap.shape[1] // slots
    merge_units = width // slots
    row = lambda vector: vector.reshape(1, -1)

    slot_scalar = slot.reshape(1).astype(jnp.int32)

    own_rows = tokens.reshape(rows, model)
    small = jnp.stack([mergebias, normgain, normshift, outerbias, finalgain, finalshift])
    small = jnp.pad(small.astype(wide), ((0, 2), (0, 0)))
    second = swap(own_rows, *far_bit)
    first = swap(own_rows, *row_bit)
    maps = [querymap, keymap, valuemap]
    biases = [row(querybias), row(valuebias)]
    merge_own = lax.dynamic_slice_in_dim(mergemap, slot * merge_units, merge_units, 0)
    merge_all = lax.all_gather(merge_own, ("dp", "seq", "heads"))
    merge_all = merge_all.reshape(slots, groups, merge_units, model)
    own = own_units(slot_scalar, shares, innermap, outermap, row(innerbias), [small])

    def exchange_keys(piece):
        found = {0: piece}
        for axis, stride in seq_bits + [core_bit]:
            for i in list(found):
                found[i | stride] = swap(found[i], axis, stride)
        return found

    maps_biases = [*maps, *biases]
    seq_tokens = {i: [] for i in range(0, seq_size, 2)}

    def exchange_tokens(piece):
        found = {0: piece}
        for axis, stride in seq_bits:
            for i in list(found):
                found[i | stride] = swap(found[i], axis, stride)
        for i in found:
            seq_tokens[i].append(found[i])
        return [found[i] for i in found if i]

    far_tokens = [exchange_tokens(own_rows)]
    far_inner = swap(pack_inner(own), *far_bit)
    second_held = hold(second, [first, own[0]])
    third = swap(second_held, *row_bit)
    q_three, kv_three = project([own_rows, first, second_held], maps_biases, proteins)
    kv_three = exchange_keys(kv_three)
    q_last, kv_last = project([third], maps_biases, proteins, [q_three])
    kv_last = exchange_keys(kv_last)
    queries = [q_three, q_last]
    kv_pieces = [stack[i] for i in range(seq_size) for stack in (kv_three, kv_last)]
    token_pieces = [own_rows, first, second, third]
    far_outer = swap(pack_outer(own, [third]), *far_bit)
    pairs = [far_inner, far_outer]
    order = list(range(len(share_bits)))
    masks = [[0], [0]]
    for k, bits in enumerate(zip(order, order[::-1])):
        if k:
            pairs = stack_pairs(pairs)
        pairs = [(p, swap(p, *share_bits[bit])) for p, bit in zip(pairs, bits)]
        masks = [(have, [m | (1 << bit) for m in have]) for have, bit in zip(masks, bits)]
        if k < len(order) - 1:
            masks = [a + b for a, b in masks]
    far_tokens += [exchange_tokens(piece) for piece in token_pieces[1:]]

    stacked = [p for pair in pairs for p in pair[:1]]
    context, context_t, logsum = attend(pos, queries, kv_pieces, stacked)
    context = [c.reshape(rows, width) for c in context]
    context = [context[0]] + [swap(context[j], "heads", j) for j in range(1, groups)]
    normed, normed_low, first_unit, first_inverse, other_maps = merge_norm(
        heads.reshape(1).astype(jnp.int32),
        context,
        mergemap,
        merge_all,
        own_rows,
        small,
        [],
    )
    inner_t, outer_w, inner_b = join_units(
        own, [p for pair in pairs for p in pair], [m for pair in masks for m in pair], [normed_low]
    )

    normed_near, normed_across = swap(normed_low, *core_bit), swap(normed_low, *row_bit)
    near_act, near_slope, near_own, near_other = feed_forward(
        normed_low, normed_near, inner_t, outer_w, inner_b
    )
    normed_across = hold(normed_across, [near_act, *far_tokens[1]])
    normed_both = swap(normed_across, *core_bit)
    normed_rows = [normed_low, normed_near, normed_across, normed_both]
    far_act, far_slope, far_own, far_other = feed_forward(
        normed_across, normed_both, inner_t, outer_w, inner_b, [near_act]
    )
    (far_part,) = add_split(far_own, swap(far_other, *core_bit), [rows])
    far_sum = swap(far_part, *row_bit)
    own_at = (seq * groups + heads) * share + jnp.arange(share, dtype=jnp.int32)
    live = (own_at[None, :] < lengths[:, None]).astype(wide).reshape(rows, 1)
    layer_output, dsum_final, dbranch, final_sums = final_norm(
        normed,
        near_own,
        swap(near_other, *core_bit),
        far_sum,
        small,
        cotangent.reshape(rows, model),
        jnp.broadcast_to(live, (rows, 128)),
        far_tokens[2],
    )
    dbranch_near, dbranch_across = swap(dbranch, *core_bit), swap(dbranch, *row_bit)
    near_dinner, near_own, near_other = feed_backward(
        dbranch, dbranch_near, inner_t, outer_w, near_slope
    )
    dbranch_across = hold(dbranch_across, [near_dinner, *far_tokens[3]])
    dbranch_both = swap(dbranch_across, *core_bit)
    dbranch_rows = [dbranch, dbranch_near, dbranch_across, dbranch_both]
    hid_block = 2 * units
    last = len(share_bits) - 1
    numbers = lambda k, side: [m for m in range(shares) if (m >> k) & 1 == side]
    acts = [near_act, far_act]
    far_dinner, far_own, far_other = feed_backward(
        dbranch_across,
        dbranch_both,
        inner_t,
        outer_w,
        far_slope,
        [near_dinner],
    )
    (far_part,) = add_split(far_own, swap(far_other, *core_bit), [rows])
    far_sum = swap(far_part, *row_bit)

    dinners = [near_dinner, far_dinner]
    outer_send = weight_grad(acts, dbranch_rows, hid_block, numbers(last, 1), 0, [far_part])
    outer_got = swap(outer_send, *share_bits[last])
    inner_send = weight_grad(dinners, normed_rows, hid_block, numbers(0, 1), 1, [far_part])
    inner_got = swap(inner_send, *share_bits[0])
    dfirst, dmerged, first_sums, dcontext = first_back(
        dsum_final,
        near_own,
        swap(near_other, *core_bit),
        far_sum,
        first_unit,
        first_inverse,
        small,
        mergemap,
        other_maps,
        [inner_send, *far_tokens[0]],
    )
    dcontext = [dcontext[0]] + [swap(dcontext[j], "heads", j) for j in range(1, groups)]
    dcontext = [d.reshape(proteins, share, width) for d in dcontext]
    core = bit_of(core_bit).reshape(1).astype(jnp.int32)
    merge_keep, merge_send = merge_grads(core, context, dmerged, final_sums, first_sums)
    merge_keep, merge_send, sums = merge_heads(
        final_sums, first_sums, merge_keep, swap(merge_send, *core_bit)
    )
    merge_got = swap(merge_send, *row_bit)
    outer_keep = weight_grad(acts, dbranch_rows, hid_block, numbers(last, 0), 0, [dmerged])
    inner_keep = weight_grad(dinners, normed_rows, hid_block, numbers(0, 0), 1, [outer_keep])
    merge_near, merge_send, sums = merge_far(
        merge_keep, merge_got, sums, [outer_keep, inner_keep]
    )
    merge_got = swap(merge_send, *far_bit)

    def shared_sum(hid, row_list, got, k, bias, waits):
        bits = [b for i, b in enumerate(share_bits) if i != k]
        if not bits:
            (keep,) = weight_grad(hid, row_list, hid_block, numbers(k, 0), bias, waits)
            return keep, got
        half = hid.shape[0] // 2
        keep, send = add_split(hid, got, [half, half], waits)
        got = swap(send, *bits[-1])
        for bit in reversed(bits[:-1]):
            half = keep.shape[0] // 2
            keep, send = add_split(keep, got, [half, half])
            got = swap(send, *bit)
        return keep, got

    outer_sums = shared_sum(outer_keep, dbranch_rows, outer_got, last, 0, [merge_send])
    inner_sums = shared_sum(inner_keep, normed_rows, inner_got, 0, 1, [merge_send])

    dqueries, dkv_by_seq = attend_back(
        pos, queries, dcontext, context_t, logsum, kv_pieces, [outer_sums[0], inner_sums[0], merge_send]
    )
    half = groups // 2
    dkv_by_seq = list(dkv_by_seq)
    dkv_by_seq[1::2] = gate(dkv_by_seq[1::2], [inner_sums[1], outer_sums[1], merge_got])
    own_pack, send_pack = pack_sums(units, *inner_sums, *outer_sums, [dqueries])
    far_pack = swap(send_pack, *far_bit)
    dkv_parts = [
        add_split(dkv_by_seq[i], swap(dkv_by_seq[i + 1], *core_bit), [groups])[0]
        for i in range(0, seq_size, 2)
    ]
    pairs = list(zip(dkv_parts, [seq_tokens[i] for i in range(0, seq_size, 2)]))
    slot_grads = qkv_grads(slot_scalar, slots, dqueries, pairs, [send_pack])
    block = 3 * width // slots
    slot_send = slot_parts(
        slot_scalar,
        block,
        merge_units,
        slot_grads,
        swap(slot_grads[shares:], *core_bit),
        merge_near,
        merge_got,
        sums,
        [],
    )
    slot_got = [swap_slots(slot_send[m], m << 1) for m in range(1, shares)]
    parts = dkv_parts
    for k in reversed(range(len(seq_bits))):
        count = 1 << k
        got = [swap(parts[count + i], *seq_bits[k]) for i in range(count)]
        if k:
            parts = [add_split(parts[i], got[i], [groups])[0] for i in range(count)]

    got[:1] = gate(got[:1], slot_got)

    part_none, part_one, part_two, part_three = dtokens(
        dqueries, parts[0], got[0], maps, [slot_send[0]]
    )
    rest = swap(part_three, *row_bit)
    near = swap(part_one, *row_bit)
    out_pack, extra = slot_sum(slot_send[0], slot_send[-1], slot_got, [part_three])
    (far_send,) = add_split(part_two, rest, [rows], [out_pack])
    far = swap(far_send, *far_bit)

    (pack,) = add_split(own_pack, far_pack, [own_pack.shape[0]], [part_three])
    grads = lax.all_gather(pack, ("dp", "seq"))

    parts = [out_pack] + [swap_slots(out_pack, m << 1) for m in range(1, shares)]
    order = [m << 1 for m in range(shares)]
    q_grad, k_grad, v_grad, mergemap_grad, bias_rows = qkv_out(
        slot_scalar,
        parts + [swap(part, *core_bit) for part in parts],
        order + [m | 1 for m in order],
        block,
        width,
    )
    tokens_grad = kernel_call(
        tokens_kernel, "tokens_grad", [dfirst, part_none, near, far], [((rows, model), low)]
    )[0]
    innermap_grad, outermap_grad, innerbias_grad = feed_out(grads, units)
    innerbias_grad = innerbias_grad.reshape(-1)
    bias_grads = bias_rows[:, :block].reshape(-1)
    shape = tokens.shape
    return (
        layer_output.reshape(shape),
        tokens_grad.reshape(shape),
        q_grad,
        bias_grads[:width],
        k_grad,
        v_grad,
        bias_grads[2 * width :],
        mergemap_grad,
        extra[3],
        extra[4],
        extra[5],
        innermap_grad,
        innerbias_grad,
        outermap_grad,
        extra[0],
        extra[1],
        extra[2],
    )


def solution(mesh):
    return jax.shard_map(
        shards,
        mesh=mesh,
        in_specs=(
            P("dp", ("seq", "heads"), None),
            P(None, "heads"),
            P("heads"),
            P(None, "heads"),
            P(None, "heads"),
            P("heads"),
            P("heads", None),
            P(),
            P(),
            P(),
            P(None, "heads"),
            P("heads"),
            P("heads", None),
            P(),
            P(),
            P(),
            P("dp"),
            P("dp", ("seq", "heads"), None),
        ),
        out_specs=(
            P("dp", ("seq", "heads"), None),
            P("dp", ("seq", "heads"), None),
            P(None, "heads"),
            P("heads"),
            P(None, "heads"),
            P(None, "heads"),
            P("heads"),
            P("heads", None),
            P(),
            P(),
            P(),
            P(None, "heads"),
            P("heads"),
            P("heads", None),
            P(),
            P(),
            P(),
        ),
        check_vma=False,
    )
```

```python
import functools

import jax
import jax.numpy as jnp
from jax import lax
from jax.experimental import pallas as pl
from jax.experimental.pallas import tpu as pltpu
from jax.sharding import PartitionSpec as P

HEAD_DIM = 64


epsilon = 1e-06
score_scale = 0.125
masked_score = -1000000000.0
low = jnp.bfloat16
wide = jnp.float32
vmem_bytes = 48 * 1024 * 1024


def dot(a, b):
    return jnp.dot(a, b, preferred_element_type=wide)


def dot_nt(a, b):
    return lax.dot_general(a, b, (((1,), (1,)), ((), ())), preferred_element_type=wide)


def dot_tn(a, b):
    return lax.dot_general(a, b, (((0,), (0,)), ((), ())), preferred_element_type=wide)


def swap(value, axis, stride):
    size = lax.axis_size(axis)
    return lax.ppermute(value, axis, [(i, i ^ stride) for i in range(size)])


def swap_slots(value, mask):
    size = lax.axis_size("dp") * lax.axis_size("seq")
    return lax.ppermute(value, ("dp", "seq"), [(i, i ^ mask) for i in range(size)])


def bit_of(bit):
    axis, stride = bit
    return (lax.axis_index(axis) // stride) % 2


def add_low(a, b):
    return (a.astype(wide) + b.astype(wide)).astype(low)


def params(mebibytes):
    return pltpu.CompilerParams(vmem_limit_bytes=mebibytes * 1024 * 1024)


in_vmem = pl.BlockSpec(memory_space=pltpu.VMEM)
in_smem = pl.BlockSpec(memory_space=pltpu.SMEM)
anywhere = pl.BlockSpec(memory_space=pl.ANY)
in_hbm = pl.BlockSpec(memory_space=pltpu.HBM)
hbm = True
kernels_alone = ("attend", "attend_back", "merge_norm", "project", "join_units", "stack_pairs")


def kernel_call(
    body, name, arrays, out, scalars=(), scratch=(), mebibytes=16, waits=(), far_in=(), local=(), flops=1, early=None
):
    ns, na, nw, no, nl = len(scalars), len(arrays), len(waits), len(out), len(local)
    alone = name in kernels_alone
    far_in = [i for i in range(na) if alone and (far_in is hbm or i in far_in)]
    far_out = [i for i, o in enumerate(out) if alone and len(o) > 2 and o[2] is hbm]
    own_out = [i for i, o in enumerate(out) if len(o) > 2 and o[2] == "kernel"]
    buffers = [pltpu.VMEM(arrays[i].shape, arrays[i].dtype) for i in far_in]
    buffers += [pltpu.VMEM(out[i][0], out[i][1]) for i in far_out]
    count = len(buffers)

    def whole(*refs):
        here = list(refs[: ns + na])
        at = ns + na + nw
        kept, outs, rest = refs[at : at + nl], list(refs[at + nl : at + nl + no]), refs[at + nl + no :]
        rest, (*held_refs, sems) = (rest[: len(rest) - count - 1], rest[len(rest) - count - 1 :])
        copies = []
        for k, i in enumerate(far_in):
            copies.append(pltpu.make_async_copy(here[ns + i], held_refs[k], sems.at[k]))
            copies[-1].start()
            here[ns + i] = held_refs[k]
        if early is not None:
            early(*here, *kept, *outs, *rest)
        for copy in copies:
            copy.wait()
        copies = []
        for k, i in enumerate(far_out, len(far_in)):
            copies.append(pltpu.make_async_copy(held_refs[k], outs[i], sems.at[k]))
            outs[i] = held_refs[k]
        body(*here, *kept, *outs, *rest)
        for copy in copies:
            copy.start()
        for copy in copies:
            copy.wait()

    return pl.pallas_call(
        whole,
        in_specs=[in_smem] * ns
        + [in_hbm if i in far_in else in_vmem for i in range(na)]
        + [anywhere] * nw
        + [in_hbm] * nl,
        out_specs=[in_hbm if i in far_out + own_out else in_vmem for i in range(no)],
        out_shape=[jax.ShapeDtypeStruct(o[0], o[1]) for o in out],
        scratch_shapes=list(scratch) + buffers + [pltpu.SemaphoreType.DMA((max(count, 1),))],
        compiler_params=params(60 if alone else mebibytes),
        cost_estimate=pl.CostEstimate(flops=flops, bytes_accessed=1, transcendentals=0),
        name=name,
    )(*scalars, *arrays, *waits, *local)


def nothing(*refs):
    pass


def gate(values, waits):
    values = [pltpu.with_memory_space_constraint(v, pltpu.HBM) for v in values]
    found = pl.pallas_call(
        nothing,
        in_specs=[anywhere] * (len(values) + len(waits)),
        out_specs=[anywhere] * len(values),
        out_shape=[jax.ShapeDtypeStruct(v.shape, v.dtype) for v in values],
        input_output_aliases={i: i for i in range(len(values))},
        compiler_params=params(1),
        name="gate",
    )(*values, *waits)
    return list(found)


def pad16(count):
    return -(-count // 16) * 16


def place(pos, proteins, groups, share, i, j):
    seq, heads = pos[proteins], pos[proteins + 1]
    return pl.multiple_of(((seq ^ i) * groups + (heads ^ j)) * share, share)


def masked(scores, length, first):
    key_at = first + lax.broadcasted_iota(jnp.int32, scores.shape, 0)
    return jnp.where(key_at < length, scores, masked_score)


def chunks(n, block):
    return [(0, n - block, False)] * (n > block) + [(n - block, n, True)]


def piece_list(refs, groups):
    found, count = [], 0
    for ref in refs:
        for n in range(ref.shape[0]):
            found.append((ref, count // groups, count % groups, n))
            count += 1
    return found


def start_keys(pos, p, proteins, groups, kv_refs, kv_all, sems, blocks, block, wait):
    share = kv_refs[0].shape[2]
    for k, (ref, i, j, n) in enumerate(piece_list(kv_refs, groups)):
        at = place(pos, proteins, groups, share, i, j)

        @pl.when(at < blocks * block)
        def _():
            copy = pltpu.make_async_copy(ref.at[n, p], kv_all.at[p, pl.ds(at, share), :], sems.at[p])
            if wait:
                copy.wait()
            else:
                copy.start()


def query_rows(refs, p):
    found = [ref[n, p] for ref in refs for n in range(ref.shape[0])]
    return jnp.concatenate(found) * jnp.asarray(score_scale, low)


def attend_kernel(counts, start, pos, *refs):
    stacks, arrays, groups = counts
    q_refs, kv_refs = refs[:stacks], refs[stacks : stacks + arrays]
    ctx_refs, (ctx_t_ref, lse_ref, kv_all, sems) = refs[stacks + arrays : -4], refs[-4:]
    _, proteins, share, width = q_refs[0].shape
    total = kv_all.shape[1]
    block = min(256, total)
    heads = range(width // HEAD_DIM)

    def keys_of(p, wait):
        blocks = (pos[p] + block - 1) // block
        start_keys(pos, p, proteins, groups, kv_refs, kv_all, sems, blocks, block, wait)
        return blocks

    if start:
        for p in range(proteins):
            keys_of(p, False)
        return

    def protein(p, carry):
        length = pos[p]
        blocks = keys_of(p, True)

        def body(count):
            n = count * block
            queries = query_rows(q_refs, p)
            cols = lambda h: slice(h * HEAD_DIM, (h + 1) * HEAD_DIM)
            value_cols = lambda h: slice(width + h * HEAD_DIM, width + (h + 1) * HEAD_DIM)
            cuts = chunks(n, block)
            scores = [
                [dot_nt(kv_all[p, a:b, cols(h)], queries[:, cols(h)]) for a, b, _ in cuts]
                for h in heads
            ]
            weights, denominators = [], []
            for h in heads:
                found = [
                    masked(value, length, a) if last else value
                    for value, (a, _, last) in zip(scores[h], cuts)
                ]
                high = functools.reduce(
                    jnp.maximum, [jnp.max(value, axis=0, keepdims=True) for value in found]
                )
                found = [jnp.exp(value - high) for value in found]
                denominator = sum(jnp.sum(value, axis=0, keepdims=True) for value in found)
                lse_ref[p, h : h + 1, :] = high + jnp.log(denominator)
                weights.append([value.astype(low) for value in found])
                denominators.append(denominator)
            context_t = jnp.concatenate(
                [
                    sum(
                        dot_tn(kv_all[p, a:b, value_cols(h)], value)
                        for (a, b, _), value in zip(cuts, weights[h])
                    )
                    / denominators[h]
                    for h in heads
                ]
            )
            ctx_t_ref[p] = context_t
            context = context_t.T.astype(low)
            for j, ref in enumerate(ctx_refs):
                ref[p] = context[j * share : (j + 1) * share]

        for count in range(1, total // block + 1):
            pl.when(blocks == count)(functools.partial(body, count))
        return carry

    lax.fori_loop(0, proteins, protein, 0)


def attend_back_kernel(counts, start, pos, *refs):
    stacks, arrays, groups = counts
    q_refs, dctx_refs, refs = refs[:stacks], refs[stacks : stacks + groups], refs[stacks + groups :]
    ctx_t_ref, lse_ref, kv_refs, refs = refs[0], refs[1], refs[2 : 2 + arrays], refs[2 + arrays :]
    dq_ref, dkv_refs, (kv_all, dkv_all, dq_all, sems, out_sems) = refs[0], refs[1:-5], refs[-5:]
    _, proteins, share, width = q_refs[0].shape
    rows = groups * share
    total = kv_all.shape[1]
    block = min(256, total)
    heads = range(width // HEAD_DIM)

    def keys_of(p, wait):
        blocks = jnp.where(pos[proteins] * rows < pos[p], (pos[p] + block - 1) // block, 0)
        start_keys(pos, p, proteins, groups, kv_refs, kv_all, sems, blocks, block, wait)
        return blocks

    if start:
        for p in range(proteins):
            keys_of(p, False)
        return

    def results_of(p, wait):
        for j in range(groups):
            copy = pltpu.make_async_copy(
                dq_all.at[p, pl.ds(j * share, share), :], dq_ref.at[j, p], out_sems.at[p]
            )
            copy.wait() if wait else copy.start()
            for i, ref in enumerate(dkv_refs):
                at = place(pos, proteins, groups, share, i, j)
                copy = pltpu.make_async_copy(
                    dkv_all.at[p, pl.ds(at, share), :], ref.at[j, p], out_sems.at[p]
                )
                copy.wait() if wait else copy.start()

    def protein(p, carry):
        length = pos[p]
        blocks = keys_of(p, True)

        @pl.when(blocks == 0)
        def _():
            dkv_all[p] = jnp.zeros(dkv_all.shape[1:], low)
            dq_all[p] = jnp.zeros(dq_all.shape[1:], low)

        def body(count):
            n = count * block
            queries = query_rows(q_refs, p)
            dctx = jnp.concatenate([ref[p] for ref in dctx_refs])
            product = dctx.astype(wide).T * ctx_t_ref[p]
            cols = lambda h: slice(h * HEAD_DIM, (h + 1) * HEAD_DIM)
            value_cols = lambda h: slice(width + h * HEAD_DIM, width + (h + 1) * HEAD_DIM)
            deltas = [jnp.sum(product[cols(h), :], axis=0, keepdims=True) for h in heads]
            dq = []
            for a, b, last in chunks(n, block):
                scores = [dot_nt(kv_all[p, a:b, cols(h)], queries[:, cols(h)]) for h in heads]
                dprobs = [dot_nt(kv_all[p, a:b, value_cols(h)], dctx[:, cols(h)]) for h in heads]
                probs, dscores = [], []
                for h in heads:
                    score = masked(scores[h], length, a) if last else scores[h]
                    prob = jnp.exp(score - lse_ref[p, h : h + 1, :])
                    probs.append(prob.astype(low))
                    dscores.append((prob * (dprobs[h] - deltas[h])).astype(low))
                dv = [dot(probs[h], dctx[:, cols(h)]) for h in heads]
                dk = [dot(dscores[h], queries[:, cols(h)]) for h in heads]
                dq.append(
                    jnp.concatenate([dot_tn(kv_all[p, a:b, cols(h)], dscores[h]) for h in heads])
                )
                dkv_all[p, a:b, :width] = jnp.concatenate(dk, axis=1).astype(low)
                dkv_all[p, a:b, width:] = jnp.concatenate(dv, axis=1).astype(low)
            if n < total:
                dkv_all[p, n:, :] = jnp.zeros((total - n, 2 * width), low)
            dq_all[p] = (sum(dq).T * score_scale).astype(low)

        for count in range(1, total // block + 1):
            pl.when(blocks == count)(functools.partial(body, count))
        results_of(p, False)
        return carry

    lax.fori_loop(0, proteins, protein, 0)
    for p in range(proteins):
        results_of(p, True)


def attend(pos, queries, kv_pieces, waits):
    groups = sum(q.shape[0] for q in queries)
    _, proteins, share, width = queries[0].shape
    rows = groups * share
    total = share * sum(piece.shape[0] for piece in kv_pieces)
    found = kernel_call(
        functools.partial(attend_kernel, (len(queries), len(kv_pieces), groups), False),
        "attend",
        queries,
        [((proteins, share, width), low, hbm)] * groups
        + [((proteins, width, rows), wide, hbm), ((proteins, 8, rows), wide, hbm)],
        scalars=[pos],
        scratch=[
            pltpu.VMEM((proteins, total, 2 * width), low),
            pltpu.SemaphoreType.DMA((proteins,)),
        ],
        mebibytes=32,
        far_in=hbm,
        local=kv_pieces,
        waits=waits,
        flops=int(1e10),
        early=functools.partial(attend_kernel, (len(queries), len(kv_pieces), groups), True),
    )
    return found[:groups], found[groups], found[groups + 1]


def attend_back(pos, queries, dctx, ctx_t, lse, kv_pieces, waits):
    groups = len(dctx)
    _, proteins, share, width = queries[0].shape
    total = share * sum(piece.shape[0] for piece in kv_pieces)
    pieces = total // (groups * share)
    arrays = [*queries, *dctx, ctx_t, lse]
    found = kernel_call(
        functools.partial(attend_back_kernel, (len(queries), len(kv_pieces), groups), False),
        "attend_back",
        arrays,
        [((groups, proteins, share, width), low, "kernel")]
        + [((groups, proteins, share, 2 * width), low, "kernel")] * pieces,
        scalars=[pos],
        scratch=[
            pltpu.VMEM((proteins, total, 2 * width), low),
            pltpu.VMEM((proteins, total, 2 * width), low),
            pltpu.VMEM((proteins, groups * share, width), low),
            pltpu.SemaphoreType.DMA((proteins,)),
            pltpu.SemaphoreType.DMA((proteins,)),
        ],
        mebibytes=32,
        far_in=[i for i in range(len(arrays)) if not 0 <= i - len(queries) < groups],
        local=kv_pieces,
        waits=waits,
        flops=int(2e10),
        early=functools.partial(attend_back_kernel, (len(queries), len(kv_pieces), groups), True),
    )
    return found[0], found[1:]


def project_kernel(count, *refs):
    tok_refs, (qmap_ref, kmap_ref, vmap_ref, qbias_ref, vbias_ref, q_ref, kv_ref) = refs[:count], refs[count:]
    width = q_ref.shape[-1]
    for j, tok_ref in enumerate(tok_refs):
        shape = q_ref.shape[1:]
        queries = dot(tok_ref[...], qmap_ref[...]) + qbias_ref[...].astype(wide)
        q_ref[j] = queries.astype(low).reshape(shape)
        kv_ref[j, :, :, :width] = dot(tok_ref[...], kmap_ref[...]).astype(low).reshape(shape)
        values = dot(tok_ref[...], vmap_ref[...]) + vbias_ref[...].astype(wide)
        kv_ref[j, :, :, width:] = values.astype(low).reshape(shape)


def project(tok, maps, proteins, waits=()):
    width = maps[0].shape[1]
    share = tok[0].shape[0] // proteins
    return kernel_call(
        functools.partial(project_kernel, len(tok)),
        "project",
        [*tok, *maps],
        [
            ((len(tok), proteins, share, width), low, hbm),
            ((len(tok), proteins, share, 2 * width), low, hbm),
        ],
        waits=waits,
        far_in=hbm,
    )


def unit_of(values):
    centered = values - jnp.mean(values, axis=-1, keepdims=True)
    variance = jnp.mean(centered * centered, axis=-1, keepdims=True)
    inverse = lax.rsqrt(variance + epsilon)
    return centered * inverse, inverse


def norm_back(grad_rows, unitized, inverse, scales):
    scaled = grad_rows * scales
    grad_mean = jnp.mean(scaled, axis=-1, keepdims=True)
    cross_mean = jnp.mean(scaled * unitized, axis=-1, keepdims=True)
    return inverse * (scaled - grad_mean - unitized * cross_mean)


def steps(rows):
    size = 64 if rows % 64 == 0 else rows
    return [slice(at, at + size) for at in range(0, rows, size)]


def merge_kernel(groups, heads, *refs):
    ctx_refs, refs = refs[:groups], refs[groups:]
    own_map, maps_all, tok_ref, small_ref = refs[:4]
    normed_ref, low_ref, unit_ref, inv_ref, maps_ref = refs[4:]
    others = groups - 1
    slots, _, size, _ = maps_all.shape
    for j in range(others):
        for k in range(slots):
            maps_ref[j, k * size : (k + 1) * size, :] = maps_all[k, heads[0] ^ (j + 1)]
    merged = small_ref[0:1, :] + dot(ctx_refs[0][...], own_map[...])
    for j in range(others):
        merged += dot(ctx_refs[j + 1][...], maps_ref[j])
    unit_ref[...] = tok_ref[...].astype(wide) + merged
    for rows in steps(tok_ref.shape[0]):
        unit, inverse = unit_of(unit_ref[rows, :])
        normed = unit * small_ref[1:2, :] + small_ref[2:3, :]
        normed_ref[rows, :] = normed
        low_ref[rows, :] = normed.astype(low)
        unit_ref[rows, :] = unit
        inv_ref[rows, :] = jnp.broadcast_to(inverse, (inverse.shape[0], 128))


def merge_norm(heads, ctx, own_map, maps_all, tok, small, waits):
    rows, model = tok.shape
    groups = len(ctx)
    return kernel_call(
        functools.partial(merge_kernel, groups),
        "merge_norm",
        [*ctx, own_map, maps_all, tok, small],
        [
            ((rows, model), wide, hbm),
            ((rows, model), low, hbm),
            ((rows, model), wide, hbm),
            ((rows, 128), wide, hbm),
            ((groups - 1, *own_map.shape), low, hbm),
        ],
        scalars=[heads],
        waits=waits,
        far_in=hbm,
    )


def final_kernel(*refs):
    normed_ref, near_ref, core_ref, far_ref, small_ref, cot_ref, live_ref = refs[:7]
    out_ref, dsum_ref, dbranch_ref, sums_ref = refs[7:]
    gain = small_ref[4:5, :]
    gain_sum = shift_sum = bias_sum = 0.0
    for rows in steps(normed_ref.shape[0]):
        branch = near_ref[rows, :].astype(wide) + core_ref[rows, :].astype(wide)
        branch = branch + far_ref[rows, :].astype(wide) + small_ref[3:4, :]
        unit, inverse = unit_of(normed_ref[rows, :] + branch)
        out_ref[rows, :] = (unit * gain + small_ref[5:6, :]).astype(low)
        grad = cot_ref[rows, :].astype(wide) * live_ref[rows, 0:1]
        dsum = norm_back(grad, unit, inverse, gain)
        dsum_ref[rows, :] = dsum
        dbranch = dsum.astype(low)
        dbranch_ref[rows, :] = dbranch
        gain_sum += jnp.sum(grad * unit, axis=0, keepdims=True)
        shift_sum += jnp.sum(grad, axis=0, keepdims=True)
        bias_sum += jnp.sum(dbranch.astype(wide), axis=0, keepdims=True)
    sums_ref[...] = jnp.zeros(sums_ref.shape, wide)
    sums_ref[0:1, :] = bias_sum
    sums_ref[1:2, :] = gain_sum
    sums_ref[2:3, :] = shift_sum


def final_norm(normed, near, core, across, small, cot, live, waits):
    rows, model = normed.shape
    return kernel_call(
        final_kernel,
        "final_norm",
        [normed, near, core, across, small, cot, live],
        [
            ((rows, model), low, hbm),
            ((rows, model), wide, hbm),
            ((rows, model), low),
            ((8, model), wide, hbm),
        ],
        far_in=[0, 4, 5, 6],
        waits=waits,
    )


def first_back_kernel(groups, *refs):
    dsum_ref, near_ref, core_ref, far_ref, unit_ref, inv_ref, small_ref, own_map, maps_ref = refs[:9]
    dfirst_ref, dmerged_ref, sums_ref = refs[9:12]
    dctx_refs = refs[12:]
    gain = small_ref[1:2, :]
    gain_sum = shift_sum = bias_sum = 0.0
    for rows in steps(dsum_ref.shape[0]):
        grad = near_ref[rows, :].astype(wide) + core_ref[rows, :].astype(wide)
        grad = dsum_ref[rows, :] + grad + far_ref[rows, :].astype(wide)
        unit = unit_ref[rows, :]
        dfirst = norm_back(grad, unit, inv_ref[rows, 0:1], gain)
        dfirst_ref[rows, :] = dfirst
        dmerged = dfirst.astype(low)
        dmerged_ref[rows, :] = dmerged
        gain_sum += jnp.sum(grad * unit, axis=0, keepdims=True)
        shift_sum += jnp.sum(grad, axis=0, keepdims=True)
        bias_sum += jnp.sum(dmerged.astype(wide), axis=0, keepdims=True)
    for j in range(groups):
        merge_map = maps_ref[j - 1] if j else own_map[...]
        dctx_refs[j][...] = dot_nt(dmerged_ref[...], merge_map).astype(low)
    sums_ref[...] = jnp.zeros(sums_ref.shape, wide)
    sums_ref[3:4, :] = bias_sum
    sums_ref[4:5, :] = gain_sum
    sums_ref[5:6, :] = shift_sum


def first_back(dsum, near, core, across, unit, inverse, small, own_map, maps, waits):
    rows, model = dsum.shape
    groups, width = maps.shape[0] + 1, own_map.shape[0]
    found = kernel_call(
        functools.partial(first_back_kernel, groups),
        "first_back",
        [dsum, near, core, across, unit, inverse, small, own_map, maps],
        [((rows, model), wide, hbm), ((rows, model), low), ((8, model), wide, hbm)]
        + [((rows, width), low)] * groups,
        waits=waits,
        far_in=[0, 4, 5, 6, 7, 8],
    )
    return found[0], found[1], found[2], found[3:]


def forward_kernel(a_ref, b_ref, inner_ref, outer_ref, bias_ref, act_ref, slope_ref, own_ref, other_ref):
    rows = a_ref.shape[0]
    for ref, out, at in ((a_ref, own_ref, 0), (b_ref, other_ref, rows)):
        pre = dot_nt(ref[...], inner_ref[...]) + bias_ref[...]
        upper = 0.5 + 0.5 * lax.erf(pre * 0.7071067811865476)
        active = (pre * upper).astype(low)
        slope = upper + pre * (0.3989422804014327 * jnp.exp(-0.5 * pre * pre))
        act_ref[at : at + rows, :] = active
        slope_ref[at : at + rows, :] = slope.astype(low)
        out[...] = dot(active, outer_ref[...]).astype(low)


def feed_forward(a, b, inner, outer, bias, waits=()):
    rows, model = a.shape
    hidden = inner.shape[0]
    return kernel_call(
        forward_kernel,
        "feed_forward",
        [a, b, inner, outer, bias],
        [((2 * rows, hidden), low, hbm)] * 2 + [((rows, model), low)] * 2,
        waits=waits,
        far_in=[0, 1],
    )


def backward_kernel(a_ref, b_ref, inner_ref, outer_ref, slope_ref, dinner_ref, own_ref, other_ref):
    rows = a_ref.shape[0]
    for ref, out, at in ((a_ref, own_ref, 0), (b_ref, other_ref, rows)):
        dactive = dot_nt(ref[...], outer_ref[...])
        dinner = (dactive * slope_ref[at : at + rows, :].astype(wide)).astype(low)
        dinner_ref[at : at + rows, :] = dinner
        out[...] = dot(dinner, inner_ref[...]).astype(low)


def feed_backward(a, b, inner, outer, slope, waits=()):
    rows, model = a.shape
    hidden = inner.shape[0]
    return kernel_call(
        backward_kernel,
        "feed_backward",
        [a, b, inner, outer, slope],
        [((2 * rows, hidden), low, hbm)] + [((rows, model), low)] * 2,
        waits=waits,
        far_in=[4],
    )


def grad_kernel(numbers, block, bias, split, *refs):
    hid, row_refs, refs = refs[:2], refs[2:6], refs[6:]
    got_ref, out_refs = (refs[0], refs[1:]) if split else (None, refs)
    model = out_refs[0].shape[-1]
    half = len(numbers) // len(out_refs)
    for k, number in enumerate(numbers):
        cols = slice(number * block, (number + 1) * block)
        total = sums = 0.0
        for i, ref in enumerate(hid):
            rows = ref.shape[0] // 2
            total += dot_tn(ref[:rows, cols], row_refs[2 * i][...])
            total += dot_tn(ref[rows:, cols], row_refs[2 * i + 1][...])
            if bias:
                sums += jnp.sum(ref[:, cols].astype(wide), axis=0, keepdims=True)
        out_ref, at = out_refs[k // half], k % half
        if split:
            total += got_ref[k, :block, :].astype(wide)
        out_ref[at, :block, :] = total.astype(low)
        if bias:
            sums = jnp.pad(sums, ((0, 15), (0, model - block)))
            if split:
                sums += got_ref[k, block:, :].astype(wide)
            out_ref[at, block:, :] = sums.astype(low)


def weight_grad(hid, row_list, block, numbers, bias, waits, got=None):
    model = row_list[0].shape[1]
    split = got is not None
    count = len(numbers) // (1 + split)
    found = kernel_call(
        functools.partial(grad_kernel, numbers, block, bias, split),
        "weight_grad",
        [*hid, *row_list] + [got] * split,
        [((count, block + 16 * bias, model), low)] * (1 + split),
        waits=waits,
    )
    return found if split else found[0]


def units_kernel(units, shares, slot, inner_ref, outer_ref, bias_ref, own_inner, own_outer, own_bias):
    for m in range(shares):
        at = pl.multiple_of((slot[0] ^ (m << 1)) * units, units)
        own_inner[m] = inner_ref[:, pl.ds(at, units)].T
        own_outer[m] = outer_ref[pl.ds(at, units), :]
        own_bias[m] = jnp.broadcast_to(bias_ref[:, pl.ds(at, units)], (16, units))


def own_units(slot, shares, innermap, outermap, innerbias, waits):
    model = innermap.shape[0]
    units = innermap.shape[1] // (2 * shares)
    if units % 128:
        found = []
        for m in range(shares):
            at = (slot[0] ^ (m << 1)) * units
            inner = lax.dynamic_slice_in_dim(innermap, at, units, 1).T
            outer = lax.dynamic_slice_in_dim(outermap, at, units, 0)
            bias = lax.dynamic_slice_in_dim(innerbias, at, units, 1)
            found.append((inner, outer, jnp.broadcast_to(bias, (16, units))))
        return [jnp.stack(pieces) for pieces in zip(*found)]
    return kernel_call(
        functools.partial(units_kernel, units, shares),
        "own_units",
        [innermap, outermap, innerbias],
        [((shares, units, model), low, hbm)] * 2 + [((shares, 16, units), innerbias.dtype, hbm)],
        scalars=[slot],
        waits=waits,
        far_in=[0, 1],
    )


def pack_inner_kernel(own_inner, own_bias, pack_ref):
    units = own_inner.shape[1]
    pack_ref[0, :units, :] = own_inner[0]
    pack_ref[0, units:, :] = jnp.zeros((16, pack_ref.shape[2]), low)
    pack_ref[0, units:, :units] = own_bias[0]


def pack_outer_kernel(own_outer, pack_ref):
    pack_ref[0] = own_outer[0]


def pack_inner(own):
    _, units, model = own[0].shape
    out = [((1, units + 16, model), low)]
    return kernel_call(pack_inner_kernel, "pack_inner", [own[0], own[2]], out)[0]


def pack_outer(own, waits):
    _, units, model = own[1].shape
    out = [((1, units, model), low)]
    return kernel_call(pack_outer_kernel, "pack_outer", [own[1]], out, waits=waits)[0]


def stack_kernel(*refs):
    count = len(refs) // 3
    for k in range(count):
        a_ref, b_ref, out_ref = refs[2 * k], refs[2 * k + 1], refs[2 * count + k]
        out_ref[: a_ref.shape[0]] = a_ref[...]
        out_ref[a_ref.shape[0] :] = b_ref[...]


def stack_pairs(pairs):
    return kernel_call(
        stack_kernel,
        "stack_pairs",
        [value for pair in pairs for value in pair],
        [((2 * a.shape[0], *a.shape[1:]), a.dtype) for a, _ in pairs],
    )


def join_kernel(units, masks, own_inner, own_outer, own_bias, *refs):
    parts, (inner_ref, outer_ref, bias_ref) = refs[:-3], refs[-3:]
    for m in range(own_inner.shape[0]):
        at, far = 2 * m * units, (2 * m + 1) * units
        inner_ref[at:far, :] = own_inner[m]
        outer_ref[at:far, :] = own_outer[m]
        bias_ref[:, at:far] = own_bias[m, 0:1, :].astype(wide)
    for which, (ref, order) in enumerate(zip(parts, masks)):
        for k, m in enumerate(order):
            far = (2 * m + 1) * units
            if which < 2:
                inner_ref[far : far + units, :] = ref[k, :units, :]
                bias_ref[:, far : far + units] = ref[k, units : units + 16, :units].astype(wide)[:1]
            else:
                outer_ref[far : far + units, :] = ref[k]


def join_units(own, parts, masks, waits):
    shares, units, model = own[0].shape
    hidden = 2 * shares * units
    return kernel_call(
        functools.partial(join_kernel, units, masks),
        "join_units",
        [*own, *parts],
        [((hidden, model), low)] * 2 + [((1, hidden), wide)],
        waits=waits,
        far_in=hbm,
    )


def slot_order(number, bits):
    return ((number & 1) << (bits - 1)) | (number >> 1)


def qkv_kernel(counts, slots, slot, *refs):
    out_ref, q_all, kv_all = refs[-3:]
    dq_ref, refs = refs[0], refs[1:-3]
    width, model = dq_ref.shape[-1], out_ref.shape[-1]
    q_all[...] = dq_ref[...].reshape(q_all.shape)
    q_sum = jnp.sum(q_all[...].astype(wide), axis=0, keepdims=True)
    q_grad = kv_grad = kv_sum = 0.0
    for i, count in enumerate(counts):
        dkv_ref, tok_refs, refs = refs[0], refs[1 : 1 + count], refs[1 + count :]
        kv_all[...] = dkv_ref[...].reshape(kv_all.shape)
        kv_sum += jnp.sum(kv_all[...].astype(wide), axis=0, keepdims=True)
        at = 0
        for tok_ref in tok_refs:
            there = slice(at, at + tok_ref.shape[0])
            at += tok_ref.shape[0]
            kv_grad += dot_tn(kv_all[there, :], tok_ref[...])
            if i == 0:
                q_grad += dot_tn(q_all[there, :], tok_ref[...])
    grad = jnp.concatenate([q_grad, kv_grad]).astype(low)
    sums = jnp.concatenate([q_sum, kv_sum], axis=1)
    bits = slots.bit_length() - 1
    block = 3 * width // slots
    for b in range(slots):
        at = slot_order(slot[0] ^ b, bits)
        out_ref[at, :block, :] = grad[b * block : (b + 1) * block]
        line = jnp.pad(sums[:, b * block : (b + 1) * block], ((0, 15), (0, model - block)))
        out_ref[at, pad16(block) :, :] = line.astype(low)


def qkv_grads(slot, slots, dq, pairs, waits):
    model = pairs[0][1][0].shape[-1]
    groups, width = dq.shape[0], dq.shape[-1]
    total = dq.size // width
    far_at, at = [], 1
    for dkv, tok in pairs:
        far_at += range(at + 1, at + 1 + len(tok))
        at += 1 + len(tok)
    return kernel_call(
        functools.partial(qkv_kernel, [len(tok) for _, tok in pairs], slots),
        "qkv_grads",
        [dq] + [a for dkv, tok in pairs for a in (dkv, *tok)],
        [((slots, pad16(3 * width // slots) + 16, model), low)],
        far_in=far_at,
        scalars=[slot],
        waits=waits,
        scratch=[pltpu.VMEM((total, width), low), pltpu.VMEM((total, 2 * width), low)],
        mebibytes=24,
    )[0]


def hold_kernel(value_ref, out_ref):
    out_ref[...] = value_ref[...]


def hold(value, waits):
    out = [(value.shape, value.dtype)]
    return kernel_call(hold_kernel, "hold", [value], out, waits=waits)[0]


def add_kernel(a_ref, b_ref, *out_refs):
    at = 0
    for ref in out_refs:
        there = slice(at, at + ref.shape[0])
        at += ref.shape[0]
        ref[...] = (a_ref[there].astype(wide) + b_ref[there].astype(wide)).astype(ref.dtype)


def add_split(a, b, counts, waits=(), kind=low):
    out = [((count, *a.shape[1:]), kind) for count in counts]
    return kernel_call(add_kernel, "add_split", [a, b], out, waits=waits)


def dtokens_kernel(dq_ref, own_ref, got_ref, q_ref, k_ref, v_ref, *out_refs):
    width = dq_ref.shape[-1]
    rows = dq_ref.shape[1] * dq_ref.shape[2]
    for j, ref in enumerate(out_refs):
        dkv = (own_ref[j].astype(wide) + got_ref[j].astype(wide)).astype(low)
        dkv = dkv.reshape(rows, 2 * width)
        total = dot_nt(dq_ref[j].reshape(rows, width), q_ref[...])
        total += dot_nt(dkv[:, :width], k_ref[...]) + dot_nt(dkv[:, width:], v_ref[...])
        ref[...] = total.astype(ref.dtype)


def dtokens(dq, own, got, maps, waits):
    rows, model = dq.shape[1] * dq.shape[2], maps[0].shape[0]
    return kernel_call(
        dtokens_kernel,
        "dtokens",
        [dq, own, got, *maps],
        [((rows, model), wide), ((rows, model), low)] * (dq.shape[0] // 2),
        waits=waits,
    )


def tokens_kernel(dfirst_ref, part_ref, near_ref, far_ref, out_ref):
    total = dfirst_ref[...] + part_ref[...] + near_ref[...].astype(wide)
    out_ref[...] = (total + far_ref[...].astype(wide)).astype(low)


def pack_sums_kernel(units, inner_ref, inner_got, outer_ref, outer_got, own_ref, send_ref):
    model = own_ref.shape[1]
    inner = inner_ref[0].astype(wide) + inner_got[0].astype(wide)
    outer = outer_ref[0].astype(wide) + outer_got[0].astype(wide)
    sums = inner[2 * units :, : 2 * units].astype(low)
    for k, ref in enumerate((own_ref, send_ref)):
        there = slice(k * units, (k + 1) * units)
        ref[:units, :] = inner[there].astype(low)
        ref[units : 2 * units, :] = outer[there].astype(low)
        ref[2 * units :, :] = jnp.zeros((16, model), low)
        ref[2 * units :, :units] = sums[:, there]


def pack_sums(units, inner, inner_got, outer, outer_got, waits):
    model = inner.shape[-1]
    return kernel_call(
        functools.partial(pack_sums_kernel, units),
        "pack_sums",
        [inner, inner_got, outer, outer_got],
        [((2 * units + 16, model), low)] * 2,
        waits=waits,
    )


def merge_grad_kernel(groups, core, *refs):
    ctx_refs, (dmerged_ref, a_ref, b_ref, keep_ref, send_ref, grad_all) = refs[:groups], refs[groups:]
    half = keep_ref.shape[1]
    for j, ref in enumerate(ctx_refs):
        grad_all[...] = dot_tn(ref[...], dmerged_ref[...]).astype(low)
        keep = pl.multiple_of(core[0] * half, half)
        send = pl.multiple_of((1 - core[0]) * half, half)
        keep_ref[j] = grad_all[pl.ds(keep, half), :]
        send_ref[j * half : (j + 1) * half, :] = grad_all[pl.ds(send, half), :]
    sums = a_ref[...] + b_ref[...]
    send_ref[groups * half :, :] = jnp.concatenate([sums, jnp.zeros_like(sums)]).astype(low)


def merge_grads(core, ctx, dmerged, a, b):
    rows, width = ctx[0].shape
    model = dmerged.shape[1]
    groups, half = len(ctx), width // 2
    return kernel_call(
        functools.partial(merge_grad_kernel, groups),
        "merge_grads",
        [*ctx, dmerged, a, b],
        [((groups, half, model), low), ((groups * half + 16, model), low)],
        far_in=[i for i in range(groups + 3) if i != groups],
        scalars=[core],
        scratch=[pltpu.VMEM((width, model), low)],
    )


def merge_heads_kernel(groups, a_ref, b_ref, keep_ref, got_ref, near_ref, send_ref, sums_ref):
    half = keep_ref.shape[1]
    total = lambda j: keep_ref[j].astype(wide) + got_ref[j * half : (j + 1) * half, :].astype(wide)
    for k in range(groups // 2):
        near_ref[k] = total(2 * k).astype(low)
        send_ref[k * half : (k + 1) * half, :] = total(2 * k + 1).astype(low)
    sums = a_ref[...] + b_ref[...] + got_ref[groups * half : groups * half + 16, :].astype(wide)[:8]
    sums_ref[...] = sums
    at = groups // 2 * half
    send_ref[at:, :] = jnp.concatenate([sums, jnp.zeros_like(sums)]).astype(low)


def merge_heads(a, b, keep, got):
    groups, half, model = keep.shape
    count = groups // 2
    return kernel_call(
        functools.partial(merge_heads_kernel, groups),
        "merge_heads",
        [a, b, keep, got],
        [((count, half, model), low), ((count * half + 16, model), low), ((8, model), wide)],
    )


def merge_far_kernel(keep_ref, got_ref, sums_ref, near_ref, send_ref, out_sums_ref):
    half = keep_ref.shape[1]
    near_ref[...] = (keep_ref[0].astype(wide) + got_ref[:half, :].astype(wide)).astype(low)
    far = keep_ref[1].astype(wide) + got_ref[half : 2 * half, :].astype(wide)
    send_ref[:half, :] = far.astype(low)
    sums = sums_ref[...] + got_ref[2 * half :, :].astype(wide)[:8]
    out_sums_ref[...] = sums
    send_ref[half:, :] = jnp.concatenate([sums, jnp.zeros_like(sums)]).astype(low)


def merge_far(keep, got, sums, waits):
    _, half, model = keep.shape
    return kernel_call(
        merge_far_kernel,
        "merge_far",
        [keep, got, sums],
        [((half, model), low), ((half + 16, model), low), ((8, model), wide)],
        waits=waits,
    )


def slots_kernel(block, size, slot, grad_ref, core_ref, near_ref, far_ref, sums_ref, *refs):
    own_ref, send_refs, (out_sums_ref, rows_all) = refs[0], refs[1:-2], refs[-2:]
    shares = len(send_refs) + 1
    half = near_ref.shape[0]
    merged = (near_ref[...].astype(wide) + far_ref[:half, :].astype(wide)).astype(low)
    for k in range(shares):
        rows_all[k] = merged[k * size : (k + 1) * size]
    sums = sums_ref[...] + far_ref[half:, :].astype(wide)[:8]
    out_sums_ref[...] = sums
    start = pad16(block) + 16
    for m, ref in enumerate((own_ref, *send_refs)):
        ref[:start, :] = (grad_ref[m].astype(wide) + core_ref[m].astype(wide)).astype(low)
        ref[start : start + size, :] = rows_all[(slot[0] >> 1) ^ m]
        if m:
            both = jnp.concatenate([sums, jnp.zeros_like(sums)]).astype(low)
            ref[start + pad16(size) :, :] = both


def slot_parts(slot, block, size, grads, core, near, far, sums, waits):
    shares, _, model = core.shape
    rows = pad16(block) + 16 + pad16(size)
    return kernel_call(
        functools.partial(slots_kernel, block, size),
        "slot_parts",
        [grads, core, near, far, sums],
        [((rows, model), low)]
        + [((rows + 16, model), low)] * (shares - 1)
        + [((8, model), wide)],
        scalars=[slot],
        scratch=[pltpu.VMEM((shares, size, model), low)],
        waits=waits,
    )


def slot_sum_kernel(own_ref, sums_ref, *refs):
    got_refs, (out_ref, out_sums_ref) = refs[:-2], refs[-2:]
    rows = own_ref.shape[0]
    total, sums = own_ref[...].astype(wide), sums_ref[...]
    for ref in got_refs:
        total += ref[:rows, :].astype(wide)
        sums += ref[rows:, :].astype(wide)[:8]
    out_ref[...] = total.astype(low)
    out_sums_ref[...] = sums


def slot_sum(own, sums, got, waits):
    return kernel_call(
        slot_sum_kernel,
        "slot_sum",
        [own, sums, *got],
        [(own.shape, low), (sums.shape, wide)],
        waits=waits,
    )


def feed_out_kernel(units, grads_ref, inner_ref, outer_ref, bias_ref, here, inner, outer, bias, sems):
    slots, rows, model = grads_ref.shape
    copies = [pltpu.make_async_copy(grads_ref.at[k], here.at[k], sems.at[0, k]) for k in range(slots)]
    for copy in copies:
        copy.start()
    done = []
    for k, copy in enumerate(copies):
        copy.wait()
        cols = slice(k * units, (k + 1) * units)
        inner[:, cols] = here[k, :units, :].astype(wide).T
        outer[cols, :] = here[k, units : 2 * units, :].astype(wide)
        bias[k : k + 1, :] = here[k, 2 * units : 2 * units + 16, :units].astype(wide)[:1]
        done.append(pltpu.make_async_copy(inner.at[:, cols], inner_ref.at[:, cols], sems.at[1, k]))
        done.append(pltpu.make_async_copy(outer.at[cols, :], outer_ref.at[cols, :], sems.at[2, k]))
        done[-2].start()
        done[-1].start()
    done.append(pltpu.make_async_copy(bias, bias_ref, sems.at[0, 0]))
    done[-1].start()
    for copy in done:
        copy.wait()


def feed_out(grads, units):
    slots, rows, model = grads.shape
    hidden = slots * units
    if units % 128:
        inner = grads[:, :units].reshape(hidden, model).astype(wide).T
        outer = grads[:, units : 2 * units].reshape(hidden, model).astype(wide)
        return inner, outer, grads[:, 2 * units, :units].astype(wide)
    shapes = [(model, hidden), (hidden, model), (slots, units)]
    return pl.pallas_call(
        functools.partial(feed_out_kernel, units),
        in_specs=[in_hbm],
        out_specs=[in_hbm] * 3,
        out_shape=[jax.ShapeDtypeStruct(shape, wide) for shape in shapes],
        scratch_shapes=[pltpu.VMEM(grads.shape, low)]
        + [pltpu.VMEM(shape, wide) for shape in shapes]
        + [pltpu.SemaphoreType.DMA((3, slots))],
        compiler_params=params(60),
        name="feed_out",
    )(grads)


def qkv_out_kernel(block, order, slot, *refs):
    parts, refs = refs[: len(order)], refs[len(order) :]
    q_ref, k_ref, v_ref, merge_ref, bias_ref, rows_all, merge_all = refs
    start, size = pad16(block), merge_all.shape[1]
    width = q_ref.shape[1]
    slots = merge_all.shape[0]
    for mask, part in zip(order, parts):
        at = slot[0] ^ mask
        rows_all[at] = part[:block, :]
        bias_ref[pl.ds(at, 1), :] = part[start : start + 16, :].astype(wide)[:1]
        at = (at & 1) * (slots // 2) + (at >> 1)
        merge_all[at] = part[start + 16 : start + 16 + size, :]
    grad = rows_all[...].reshape(3 * width, -1)
    for i, ref in enumerate((q_ref, k_ref, v_ref)):
        ref[...] = grad[i * width : (i + 1) * width].astype(wide).T
    merge_ref[...] = merge_all[...].reshape(merge_ref.shape).astype(wide)


def qkv_out(slot, parts, order, block, width):
    model = parts[0].shape[-1]
    slots = 3 * width // block
    size = width // slots
    return kernel_call(
        functools.partial(qkv_out_kernel, block, order),
        "qkv_out",
        parts,
        [((model, width), wide)] * 3 + [((width, model), wide), ((slots, model), wide)],
        scalars=[slot],
        scratch=[pltpu.VMEM((slots, block, model), low), pltpu.VMEM((slots, size, model), low)],
    )


def shards(
    tokens,
    querymap,
    querybias,
    keymap,
    valuemap,
    valuebias,
    mergemap,
    mergebias,
    normgain,
    normshift,
    innermap,
    innerbias,
    outermap,
    outerbias,
    finalgain,
    finalshift,
    lengths,
    cotangent,
):
    proteins, share, model = tokens.shape
    groups = lax.axis_size("heads")
    rows = proteins * share
    width = querymap.shape[1]
    seq, heads = lax.axis_index("seq"), lax.axis_index("heads")
    seq_size, dp_size = lax.axis_size("seq"), lax.axis_size("dp")
    pos = jnp.concatenate([lengths, jnp.stack([seq, heads]).astype(jnp.int32)])
    core_bit, row_bit, far_bit = ("seq", 1), ("heads", 1), ("heads", 2)
    seq_bits = [("seq", 1 << k) for k in range(1, seq_size.bit_length() - 1)]
    share_bits = seq_bits + [("dp", 1 << k) for k in range(dp_size.bit_length() - 1)]
    slot_bits = [core_bit] + share_bits
    slots = 1 << len(slot_bits)
    shares = slots // 2
    slot = lax.axis_index("dp") * seq_size + seq
    units = innermap.shape[1] // slots
    merge_units = width // slots
    row = lambda vector: vector.reshape(1, -1)

    slot_scalar = slot.reshape(1).astype(jnp.int32)

    own_rows = tokens.reshape(rows, model)
    small = jnp.stack([mergebias, normgain, normshift, outerbias, finalgain, finalshift])
    small = jnp.pad(small.astype(wide), ((0, 2), (0, 0)))
    second = swap(own_rows, *far_bit)
    first = swap(own_rows, *row_bit)
    maps = [querymap, keymap, valuemap]
    biases = [row(querybias), row(valuebias)]
    merge_own = lax.dynamic_slice_in_dim(mergemap, slot * merge_units, merge_units, 0)
    merge_all = lax.all_gather(merge_own, ("dp", "seq", "heads"))
    merge_all = merge_all.reshape(slots, groups, merge_units, model)
    own = own_units(slot_scalar, shares, innermap, outermap, row(innerbias), [small])

    def exchange_keys(piece):
        found = {0: piece}
        for axis, stride in seq_bits + [core_bit]:
            for i in list(found):
                found[i | stride] = swap(found[i], axis, stride)
        return found

    maps_biases = [*maps, *biases]
    seq_tokens = {i: [] for i in range(0, seq_size, 2)}

    def exchange_tokens(piece):
        found = {0: piece}
        for axis, stride in seq_bits:
            for i in list(found):
                found[i | stride] = swap(found[i], axis, stride)
        for i in found:
            seq_tokens[i].append(found[i])
        return [found[i] for i in found if i]

    far_tokens = [exchange_tokens(own_rows)]
    far_inner = swap(pack_inner(own), *far_bit)
    second_held = hold(second, [first, own[0]])
    third = swap(second_held, *row_bit)
    q_three, kv_three = project([own_rows, first, second_held], maps_biases, proteins)
    kv_three = exchange_keys(kv_three)
    q_last, kv_last = project([third], maps_biases, proteins, [q_three])
    kv_last = exchange_keys(kv_last)
    queries = [q_three, q_last]
    kv_pieces = [stack[i] for i in range(seq_size) for stack in (kv_three, kv_last)]
    token_pieces = [own_rows, first, second, third]
    far_outer = swap(pack_outer(own, [third]), *far_bit)
    pairs = [far_inner, far_outer]
    order = list(range(len(share_bits)))
    masks = [[0], [0]]
    for k, bits in enumerate(zip(order, order[::-1])):
        if k:
            pairs = stack_pairs(pairs)
        pairs = [(p, swap(p, *share_bits[bit])) for p, bit in zip(pairs, bits)]
        masks = [(have, [m | (1 << bit) for m in have]) for have, bit in zip(masks, bits)]
        if k < len(order) - 1:
            masks = [a + b for a, b in masks]
    far_tokens += [exchange_tokens(piece) for piece in token_pieces[1:]]

    stacked = [p for pair in pairs for p in pair[:1]]
    context, context_t, logsum = attend(pos, queries, kv_pieces, stacked)
    context = [c.reshape(rows, width) for c in context]
    context = [context[0]] + [swap(context[j], "heads", j) for j in range(1, groups)]
    normed, normed_low, first_unit, first_inverse, other_maps = merge_norm(
        heads.reshape(1).astype(jnp.int32),
        context,
        mergemap,
        merge_all,
        own_rows,
        small,
        [],
    )
    inner_t, outer_w, inner_b = join_units(
        own, [p for pair in pairs for p in pair], [m for pair in masks for m in pair], [normed_low]
    )

    normed_near, normed_across = swap(normed_low, *core_bit), swap(normed_low, *row_bit)
    near_act, near_slope, near_own, near_other = feed_forward(
        normed_low, normed_near, inner_t, outer_w, inner_b
    )
    normed_across = hold(normed_across, [near_act, *far_tokens[1]])
    normed_both = swap(normed_across, *core_bit)
    normed_rows = [normed_low, normed_near, normed_across, normed_both]
    far_act, far_slope, far_own, far_other = feed_forward(
        normed_across, normed_both, inner_t, outer_w, inner_b, [near_act]
    )
    (far_part,) = add_split(far_own, swap(far_other, *core_bit), [rows])
    far_sum = swap(far_part, *row_bit)
    own_at = (seq * groups + heads) * share + jnp.arange(share, dtype=jnp.int32)
    live = (own_at[None, :] < lengths[:, None]).astype(wide).reshape(rows, 1)
    layer_output, dsum_final, dbranch, final_sums = final_norm(
        normed,
        near_own,
        swap(near_other, *core_bit),
        far_sum,
        small,
        cotangent.reshape(rows, model),
        jnp.broadcast_to(live, (rows, 128)),
        far_tokens[2],
    )
    dbranch_near, dbranch_across = swap(dbranch, *core_bit), swap(dbranch, *row_bit)
    near_dinner, near_own, near_other = feed_backward(
        dbranch, dbranch_near, inner_t, outer_w, near_slope
    )
    dbranch_across = hold(dbranch_across, [near_dinner, *far_tokens[3]])
    dbranch_both = swap(dbranch_across, *core_bit)
    dbranch_rows = [dbranch, dbranch_near, dbranch_across, dbranch_both]
    hid_block = 2 * units
    last = len(share_bits) - 1
    numbers = lambda k, side: [m for m in range(shares) if (m >> k) & 1 == side]
    acts = [near_act, far_act]
    far_dinner, far_own, far_other = feed_backward(
        dbranch_across,
        dbranch_both,
        inner_t,
        outer_w,
        far_slope,
        [near_dinner],
    )
    (far_part,) = add_split(far_own, swap(far_other, *core_bit), [rows])
    far_sum = swap(far_part, *row_bit)

    dinners = [near_dinner, far_dinner]
    outer_send = weight_grad(acts, dbranch_rows, hid_block, numbers(last, 1), 0, [far_part])
    outer_got = swap(outer_send, *share_bits[last])
    inner_send = weight_grad(dinners, normed_rows, hid_block, numbers(0, 1), 1, [far_part])
    inner_got = swap(inner_send, *share_bits[0])
    dfirst, dmerged, first_sums, dcontext = first_back(
        dsum_final,
        near_own,
        swap(near_other, *core_bit),
        far_sum,
        first_unit,
        first_inverse,
        small,
        mergemap,
        other_maps,
        [inner_send, *far_tokens[0]],
    )
    dcontext = [dcontext[0]] + [swap(dcontext[j], "heads", j) for j in range(1, groups)]
    dcontext = [d.reshape(proteins, share, width) for d in dcontext]
    core = bit_of(core_bit).reshape(1).astype(jnp.int32)
    merge_keep, merge_send = merge_grads(core, context, dmerged, final_sums, first_sums)
    merge_keep, merge_send, sums = merge_heads(
        final_sums, first_sums, merge_keep, swap(merge_send, *core_bit)
    )
    merge_got = swap(merge_send, *row_bit)
    outer_keep = weight_grad(acts, dbranch_rows, hid_block, numbers(last, 0), 0, [dmerged])
    inner_keep = weight_grad(dinners, normed_rows, hid_block, numbers(0, 0), 1, [outer_keep])
    merge_near, merge_send, sums = merge_far(
        merge_keep, merge_got, sums, [outer_keep, inner_keep]
    )
    merge_got = swap(merge_send, *far_bit)

    def shared_sum(hid, row_list, got, k, bias, waits):
        bits = [b for i, b in enumerate(share_bits) if i != k]
        if not bits:
            (keep,) = weight_grad(hid, row_list, hid_block, numbers(k, 0), bias, waits)
            return keep, got
        half = hid.shape[0] // 2
        keep, send = add_split(hid, got, [half, half], waits)
        got = swap(send, *bits[-1])
        for bit in reversed(bits[:-1]):
            half = keep.shape[0] // 2
            keep, send = add_split(keep, got, [half, half])
            got = swap(send, *bit)
        return keep, got

    outer_sums = shared_sum(outer_keep, dbranch_rows, outer_got, last, 0, [merge_send])
    inner_sums = shared_sum(inner_keep, normed_rows, inner_got, 0, 1, [merge_send])

    dqueries, dkv_by_seq = attend_back(
        pos, queries, dcontext, context_t, logsum, kv_pieces, [outer_sums[0], inner_sums[0], merge_send]
    )
    half = groups // 2
    dkv_by_seq = list(dkv_by_seq)
    dkv_by_seq[1::2] = gate(dkv_by_seq[1::2], [inner_sums[1], outer_sums[1], merge_got])
    own_pack, send_pack = pack_sums(units, *inner_sums, *outer_sums, [dqueries])
    far_pack = swap(send_pack, *far_bit)
    dkv_parts = [
        add_split(dkv_by_seq[i], swap(dkv_by_seq[i + 1], *core_bit), [groups])[0]
        for i in range(0, seq_size, 2)
    ]
    pairs = list(zip(dkv_parts, [seq_tokens[i] for i in range(0, seq_size, 2)]))
    slot_grads = qkv_grads(slot_scalar, slots, dqueries, pairs, [send_pack])
    block = 3 * width // slots
    slot_send = slot_parts(
        slot_scalar,
        block,
        merge_units,
        slot_grads,
        swap(slot_grads[shares:], *core_bit),
        merge_near,
        merge_got,
        sums,
        [],
    )
    slot_got = [swap_slots(slot_send[m], m << 1) for m in range(1, shares)]
    parts = dkv_parts
    for k in reversed(range(len(seq_bits))):
        count = 1 << k
        got = [swap(parts[count + i], *seq_bits[k]) for i in range(count)]
        if k:
            parts = [add_split(parts[i], got[i], [groups])[0] for i in range(count)]

    got[:1] = gate(got[:1], slot_got)

    part_none, part_one, part_two, part_three = dtokens(
        dqueries, parts[0], got[0], maps, [slot_send[0]]
    )
    rest = swap(part_three, *row_bit)
    near = swap(part_one, *row_bit)
    out_pack, extra = slot_sum(slot_send[0], slot_send[-1], slot_got, [part_three])
    (far_send,) = add_split(part_two, rest, [rows], [out_pack])
    far = swap(far_send, *far_bit)

    (pack,) = add_split(own_pack, far_pack, [own_pack.shape[0]], [part_three])
    grads = lax.all_gather(pack, ("dp", "seq"))

    parts = [out_pack] + [swap_slots(out_pack, m << 1) for m in range(1, shares)]
    order = [m << 1 for m in range(shares)]
    q_grad, k_grad, v_grad, mergemap_grad, bias_rows = qkv_out(
        slot_scalar,
        parts + [swap(part, *core_bit) for part in parts],
        order + [m | 1 for m in order],
        block,
        width,
    )
    tokens_grad = kernel_call(
        tokens_kernel, "tokens_grad", [dfirst, part_none, near, far], [((rows, model), low)]
    )[0]
    innermap_grad, outermap_grad, innerbias_grad = feed_out(grads, units)
    innerbias_grad = innerbias_grad.reshape(-1)
    bias_grads = bias_rows[:, :block].reshape(-1)
    shape = tokens.shape
    return (
        layer_output.reshape(shape),
        tokens_grad.reshape(shape),
        q_grad,
        bias_grads[:width],
        k_grad,
        v_grad,
        bias_grads[2 * width :],
        mergemap_grad,
        extra[3],
        extra[4],
        extra[5],
        innermap_grad,
        innerbias_grad,
        outermap_grad,
        extra[0],
        extra[1],
        extra[2],
    )


def solution(mesh):
    return jax.shard_map(
        shards,
        mesh=mesh,
        in_specs=(
            P("dp", ("seq", "heads"), None),
            P(None, "heads"),
            P("heads"),
            P(None, "heads"),
            P(None, "heads"),
            P("heads"),
            P("heads", None),
            P(),
            P(),
            P(),
            P(None, "heads"),
            P("heads"),
            P("heads", None),
            P(),
            P(),
            P(),
            P("dp"),
            P("dp", ("seq", "heads"), None),
        ),
        out_specs=(
            P("dp", ("seq", "heads"), None),
            P("dp", ("seq", "heads"), None),
            P(None, "heads"),
            P("heads"),
            P(None, "heads"),
            P(None, "heads"),
            P("heads"),
            P("heads", None),
            P(),
            P(),
            P(),
            P(None, "heads"),
            P("heads"),
            P("heads", None),
            P(),
            P(),
            P(),
        ),
        check_vma=False,
    )
```
